256 devices in a mesh: row: 8 (over x, z_lo), col: 32 (over y, z_hi, core).
Axes of the slice: x: 4, y: 4, z: 8 (z_hi: 4, z_lo: 2; z = z_hi * 2 + z_lo), core: 2. Of those that a mesh axis runs over, the one named last changes fastest.
Arguments:
- left_factor: bfloat16 [8192, 2048], P('row', 'col'), may hold values from -160 to 160
- right_factor: bfloat16 [2048, 8192], P('row', 'col'), may hold values from -12 to 12
- weights: float32 [2048], P('col'), may hold values from 0.02 to 1
- plan: int32 [4, 256], replicated, may hold values from 0 to 255, as said below
Outputs:
- rotated: float32 [8192, 8192], P('row', 'col')
The draws below stay inside these ranges and needn't reach their ends.
Inputs may be any that keep to these rules, and one draw needn't show every extreme that they name: `plan`: each row is a permutation of the 256 blocks. In row 0 slot s holds a block b with b // 8 == s // 8. Each later row follows from the one before: slot 2p takes the block of slot 2p - 2 (slot 0 that of slot 1), slot 2p + 1 takes the block of slot 2p + 3 (slot 255 that of slot 254).
All inputs are finite; a program needn't handle non-finite values.
Results may differ from the reference program's by a relative error of at most 0.0031.
Values may be sent and summed in bfloat16 or wider, within the bound.
A program may use at most 64 MiB of HBM per device.

```python
import math
import jax
import jax.numpy as jnp
from jax import lax

M = 8192
K = 2048
BS = 32
ROUNDS = 4
NB = 256
SLOTS_DEV = 8


def draw_plan(key, part):
    key = jax.random.fold_in(key, 7)
    groups = NB // SLOTS_DEV
    scores = jax.random.randint(key, (groups, SLOTS_DEV), 0, 1 << 20) * SLOTS_DEV
    scores = scores + jnp.arange(SLOTS_DEV, dtype=jnp.int32)[None, :]
    ranking = jnp.argsort(scores, axis=1, stable=True).astype(jnp.int32)
    current = (ranking + (jnp.arange(groups, dtype=jnp.int32) * SLOTS_DEV)[:, None]).reshape(NB)
    slot_ids = jnp.arange(NB, dtype=jnp.int32)
    proc_ids = slot_ids // 2
    source = jnp.where(slot_ids % 2 == 0, jnp.where(proc_ids > 0, slot_ids - 2, 1), jnp.where(proc_ids < NB // 2 - 1, slot_ids + 2, NB - 2)).astype(jnp.int32)
    history = [current]
    for round_index in range(1, ROUNDS):
        current = current[source]
        history.append(current)
    return jnp.stack(history).astype(jnp.int32)


def row_scaled(key, rise):
    entry_key, scale_key = jax.random.split(key, 2)
    entries = jnp.clip(jax.random.normal(entry_key, (M, K), jnp.float32), -4.0, 4.0)
    position = jnp.arange(M, dtype=jnp.float32) / M
    rough = jnp.exp(jnp.log(2.0) * jax.random.uniform(scale_key, (M,), jnp.float32))
    scale = jnp.exp(jnp.log(rise) * position) * rough
    return entries * scale[:, None]


def draw_left_factor(key, part):
    key = jax.random.fold_in(key, 11)
    return row_scaled(key, 8.0).astype(jnp.bfloat16)


def draw_right_factor(key, part):
    key = jax.random.fold_in(key, 13)
    entry_key, scale_key = jax.random.split(key)
    entries = jnp.clip(jax.random.normal(entry_key, (K, M), jnp.float32), -4.0, 4.0)
    column_scale = jnp.exp(jax.random.uniform(scale_key, (M,), jnp.float32, jnp.log(0.3), jnp.log(3.0)))
    return (entries * column_scale[None, :] / K ** 0.5).astype(jnp.bfloat16)


def levels(rng, shape, cuts, low, top_value):
    def one(axis_at, blocks):
        heights = jax.random.uniform(jax.random.fold_in(jax.random.fold_in(rng, 6), axis_at), (blocks,), jnp.float32, low / len(cuts), top_value / len(cuts))
        return jnp.repeat(jnp.exp(heights), shape[axis_at] // blocks).reshape((-1,) + (1,) * (len(shape) - axis_at - 1))

    factor_of = one(*cuts[0])
    for cut in cuts[1:]:
        factor_of = factor_of * one(*cut)
    return factor_of


def setup_inputs(seed: int = 0) -> dict:
    splits = jax.random.split(jax.random.key(seed), 5)
    return {
        "left_factor": draw_left_factor(jax.random.fold_in(splits[4], 71), 0),
        "right_factor": draw_right_factor(jax.random.fold_in(splits[4], 71), 0),
        "weights": jnp.clip(jnp.exp(math.log(1.0) - 3.912023 * jax.random.uniform(splits[2], (K,), jnp.float32) ** levels(splits[2], (K,), ((0, 32),), -0.2, 0.2)), 0.02, 1.0),
        "plan": draw_plan(jax.random.fold_in(splits[4], 71), 0),
    }


EPSILON = 1e-06

def rotation(gram):
    diagonal = jnp.diagonal(gram, axis1=1, axis2=2)
    spread = diagonal[:, None, :] - diagonal[:, :, None]
    middle = 0.5 * (diagonal[:, None, :] + diagonal[:, :, None])
    angles = gram * spread / (2.0 * (spread * spread + middle * middle + EPSILON))
    identity = jnp.eye(gram.shape[1], dtype=jnp.float32)
    raised = identity[None] + angles
    lowered = identity[None] - angles
    return jnp.linalg.solve(lowered, raised)

def reference(left_factor, right_factor, weights, plan):
    scaled = (left_factor.astype(jnp.float32) * weights[None, :]).astype(jnp.bfloat16)
    theta_block = jnp.dot(scaled.astype(jnp.float32), right_factor.astype(jnp.float32), preferred_element_type=jnp.float32)
    blocks = theta_block.reshape(M, NB, BS)
    for round_index in range(ROUNDS):
        first_slots = plan[round_index, 0::2]
        second_slots = plan[round_index, 1::2]
        paired = jnp.concatenate([blocks[:, first_slots], blocks[:, second_slots]], axis=2)
        gram = jnp.einsum('mpi,mpj->pij', paired, paired, precision=lax.Precision.HIGHEST)
        turned = jnp.einsum('mpi,pij->mpj', paired, rotation(gram), precision=lax.Precision.HIGHEST)
        blocks = blocks.at[:, first_slots].set(turned[:, :, :BS])
        blocks = blocks.at[:, second_slots].set(turned[:, :, BS:])
    return blocks[:, plan[ROUNDS - 1]].reshape(M, M)
```

```python
import functools

import jax
import jax.numpy as jnp
from jax import lax
from jax.experimental import pallas as pl
from jax.experimental.pallas import tpu as pltpu
from jax.sharding import PartitionSpec as P

BS = 32
LANES = 128
EPSILON = 1e-06
TOLERANCE = 1e-04
STRIP = 256
TILE_ORDER = (0, 2, 1, 3, 4)
BF16 = jnp.bfloat16
F32 = jnp.float32
MESH = pl.DeviceIdType.MESH
ROWS = 1024
HALF = 512
QUARTER = 256
DEPTH = 256
SHARE = 144
VMEM_LIMIT = 48 * 1024 * 1024


def gather_kernel(
    left_ref, weights_ref, right_ref, plan_ref,
    high_ref, low_ref, gram_ref,
    own_buf, sib_buf, s_buf, r_buf, sib_r, theta, part, landed,
    send_sem, sib_sem, z_sem, zo_sem, y_sem, yo_sem, ss_sem,
    out_sem, zr_sem, x_sem, xo_sem, sr_sem, part_sem, full_sem,
):
    row = lax.axis_index("row")
    col = lax.axis_index("col")
    x, zl = row // 2, lax.rem(row, 2)
    core = lax.rem(col, 2)
    chip = col // 2
    y, zh = chip // 4, lax.rem(chip, 4)
    sibling = {"row": row, "col": col + 1 - 2 * core}
    outer_col = col - 1 + 2 * core
    at_end = jnp.logical_or(outer_col < 0, outer_col > 31)
    outer = {"row": row, "col": outer_col}

    def chip_at(yy, zz):
        return lax.rem(yy, 4) * 4 + lax.rem(zz, 4)

    def along(yy, zz):
        return {"row": row, "col": chip_at(yy, zz) * 2 + core}

    def row_at(xx, zz):
        return lax.rem(xx, 4) * 2 + zz

    sent = []

    def send(src, dst, sem, device):
        copy = pltpu.make_async_remote_copy(
            src_ref=src, dst_ref=dst, send_sem=send_sem.at[len(sent)], recv_sem=sem,
            device_id=device, device_id_type=MESH,
        )
        copy.start()
        sent.append(copy)

    def arrive(ref, sem):
        pltpu.make_async_copy(ref, ref, sem).wait()

    barrier = pltpu.get_barrier_semaphore()
    peers = [sibling, along(y, zh + 1), along(y, zh + 3), along(y + 1, zh), along(y + 3, zh)]
    for step in range(1, 8):
        peers.append({"row": lax.rem(row + step, 8), "col": col})
    for peer in peers:
        pl.semaphore_signal(barrier, inc=1, device_id=peer, device_id_type=MESH)

    @pl.when(jnp.logical_not(at_end))
    def _():
        pl.semaphore_signal(barrier, inc=1, device_id=outer, device_id_type=MESH)

    scaled = (left_ref[...].astype(F32) * weights_ref[...]).astype(BF16)
    own_buf[...] = jnp.concatenate([scaled, scaled], axis=1)

    ids = []
    for slot in (0, 4, 1, 5, 2, 6, 3, 7):
        there = jnp.where(core == 0, slot, 7 - slot)
        ids.append(plan_ref[0, col * 8 + there] - col * 8)
    block = lax.broadcasted_iota(jnp.int32, (DEPTH, 256), 1) // BS
    source = jnp.zeros((DEPTH, 256), jnp.int32)
    for at, value in enumerate(ids):
        source = jnp.where(block == at, value, source)
    column = lax.broadcasted_iota(jnp.int32, (DEPTH, 256), 1)
    place = lax.broadcasted_iota(jnp.int32, (DEPTH, 256), 0) == source * BS + lax.rem(column, BS)
    ordered = jnp.dot(right_ref[...], place.astype(BF16), preferred_element_type=F32).astype(BF16)
    r_buf[row, 0] = ordered[:, :LANES]
    r_buf[row, 1] = ordered[:, LANES:]

    pl.semaphore_wait(barrier, jnp.where(at_end, 12, 13))

    send(own_buf, sib_buf, sib_sem.at[0], sibling)

    to_outer = pltpu.make_async_remote_copy(
        src_ref=r_buf.at[row, pl.ds(0, 2)], dst_ref=r_buf.at[row, pl.ds(2, 2)],
        send_sem=out_sem.at[0], recv_sem=out_sem.at[1], device_id=outer, device_id_type=MESH,
    )

    @pl.when(jnp.logical_not(at_end))
    def _():
        to_outer.start()

    @pl.when(at_end)
    def _():
        r_buf[row, 2] = ordered[:, :LANES]
        r_buf[row, 3] = ordered[:, LANES:]

    arrive(sib_buf, sib_sem.at[0])
    lane = lax.broadcasted_iota(jnp.int32, (ROWS, LANES), 1)
    mine = (lane // 64) == core
    s_buf[chip] = jnp.where(mine, own_buf[...], sib_buf[...])

    half = pl.multiple_of(core * HALF, HALF)
    other = pl.multiple_of(HALF - core * HALF, HALF)

    def whole(q):
        return s_buf.at[q, pl.ds(half, HALF), :]

    def sub(q, which):
        return s_buf.at[q, pl.ds(pl.multiple_of(half + which * QUARTER, QUARTER), QUARTER), :]

    def pass_on(q, at):
        send(whole(q), whole(q), ss_sem.at[at], sibling)

    def y_sends(zz, at):
        q = chip_at(y, zz)
        send(whole(q), whole(q), y_sem.at[2 * at], along(y + 1, zh))
        send(whole(q), whole(q), y_sem.at[2 * at + 1], along(y + 3, zh))

    def y_arrive(zz, at):
        q = chip_at(y + 3, zz)
        arrive(whole(q), y_sem.at[2 * at])
        send(sub(q, 0), sub(q, 0), yo_sem.at[2 * at], along(y + 1, zh))
        pass_on(q, 3 + 3 * at)
        q = chip_at(y + 1, zz)
        arrive(whole(q), y_sem.at[2 * at + 1])
        send(sub(q, 1), sub(q, 1), yo_sem.at[2 * at + 1], along(y + 3, zh))
        pass_on(q, 4 + 3 * at)

    def y_opposite(zz, at):
        q = chip_at(y + 2, zz)
        arrive(sub(q, 0), yo_sem.at[2 * at])
        arrive(sub(q, 1), yo_sem.at[2 * at + 1])
        pass_on(q, 5 + 3 * at)

    def x_sends(zz, at):
        r = row_at(x, zz)
        send(r_buf.at[r], r_buf.at[r], x_sem.at[2 * at], {"row": row_at(x + 1, zl), "col": col})
        send(r_buf.at[r], r_buf.at[r], x_sem.at[2 * at + 1], {"row": row_at(x + 3, zl), "col": col})

    def share_right(r, at):
        send(r_buf.at[r, pl.ds(0, 2)], sib_r.at[r], sr_sem.at[at], sibling)

    def x_arrive(zz, at):
        r = row_at(x + 3, zz)
        arrive(r_buf.at[r], x_sem.at[2 * at])
        piece = r_buf.at[r, pl.ds(0, 2)]
        send(piece, piece, xo_sem.at[2 * at], {"row": row_at(x + 1, zl), "col": col})
        share_right(r, 2 + 3 * at)
        r = row_at(x + 1, zz)
        arrive(r_buf.at[r], x_sem.at[2 * at + 1])
        piece = r_buf.at[r, pl.ds(2, 2)]
        send(piece, piece, xo_sem.at[2 * at + 1], {"row": row_at(x + 3, zl), "col": col})
        share_right(r, 3 + 3 * at)

    def x_opposite(zz, at):
        r = row_at(x + 2, zz)
        arrive(r_buf.at[r, pl.ds(0, 2)], xo_sem.at[2 * at])
        arrive(r_buf.at[r, pl.ds(2, 2)], xo_sem.at[2 * at + 1])
        share_right(r, 4 + 3 * at)

    send(whole(chip), whole(chip), z_sem.at[0], along(y, zh + 1))
    send(whole(chip), whole(chip), z_sem.at[1], along(y, zh + 3))
    y_sends(zh, 0)

    @pl.when(jnp.logical_not(at_end))
    def _():
        arrive(r_buf.at[row, pl.ds(2, 2)], out_sem.at[1])

    send(r_buf.at[row], r_buf.at[row], zr_sem.at[0], {"row": row_at(x, 1 - zl), "col": col})
    x_sends(zl, 0)
    share_right(row, 0)

    y_arrive(zh, 0)

    q = chip_at(y, zh + 3)
    arrive(whole(q), z_sem.at[0])
    send(sub(q, 0), sub(q, 0), zo_sem.at[0], along(y, zh + 1))
    y_sends(zh + 3, 1)
    pass_on(q, 0)
    q = chip_at(y, zh + 1)
    arrive(whole(q), z_sem.at[1])
    send(sub(q, 1), sub(q, 1), zo_sem.at[1], along(y, zh + 3))
    y_sends(zh + 1, 2)
    pass_on(q, 1)

    y_opposite(zh, 0)
    x_arrive(zl, 0)

    r = row_at(x, 1 - zl)
    arrive(r_buf.at[r], zr_sem.at[0])
    x_sends(1 - zl, 1)
    share_right(r, 1)

    q = chip_at(y, zh + 2)
    arrive(sub(q, 0), zo_sem.at[0])
    arrive(sub(q, 1), zo_sem.at[1])
    y_sends(zh + 2, 3)
    pass_on(q, 2)

    y_arrive(zh + 3, 1)
    y_arrive(zh + 1, 2)
    x_opposite(zl, 0)
    x_arrive(1 - zl, 1)
    y_opposite(zh + 3, 1)
    y_opposite(zh + 1, 2)
    y_arrive(zh + 2, 3)
    x_opposite(1 - zl, 1)

    for at in range(8):
        arrive(sib_r.at[0], sr_sem.at[at])

    odd = lax.rem(lax.broadcasted_iota(jnp.int32, (DEPTH, LANES), 1) // BS, 2) == 1

    def window(r):
        own_e, own_o, out_e, out_o = (r_buf[r, t] for t in range(4))
        sib_e, sib_o = sib_r[r, 0], sib_r[r, 1]
        mixed = jnp.where(odd, sib_e, out_o)
        return jnp.concatenate([own_e, own_o, sib_o, out_e, mixed], axis=1)

    def add_up(yy, first):
        yy = lax.rem(yy, 4)
        weights = jnp.concatenate([window(2 * yy), window(2 * yy + 1)], axis=0)

        def strip(step, _):
            here = pl.ds(pl.multiple_of(step * STRIP, STRIP), STRIP)
            rows = jnp.concatenate([s_buf[yy * 4 + t, here, :] for t in range(4)], axis=1)
            value = jnp.dot(rows, weights, preferred_element_type=F32)
            theta[here, :] = value if first else theta[here, :] + value
            return 0

        lax.fori_loop(0, ROWS // STRIP, strip, 0)

    for at in range(3):
        arrive(whole(0), ss_sem.at[at])
    add_up(y, True)
    for at in (3, 6, 9, 12):
        arrive(whole(0), ss_sem.at[at])
    add_up(y + 3, False)
    for at in (4, 7, 10, 13):
        arrive(whole(0), ss_sem.at[at])
    add_up(y + 1, False)
    y_opposite(zh + 2, 3)
    for at in (5, 8, 11, 14):
        arrive(whole(0), ss_sem.at[at])
    add_up(y + 2, False)

    for t in range(5):
        value = theta[:, t * LANES:(t + 1) * LANES]
        rounded = value.astype(BF16)
        high_ref[t] = rounded
        low_ref[t] = (value - rounded.astype(F32)).astype(BF16)

    def gram(a, others):
        high = jnp.concatenate([high_ref[t] for t in others], axis=1)
        low = jnp.concatenate([low_ref[t] for t in others], axis=1)

        def over_rows(p, q):
            return lax.dot_general(p, q, (((0,), (0,)), ((), ())), preferred_element_type=F32)

        return over_rows(high_ref[a], high) + (over_rows(high_ref[a], low) + over_rows(low_ref[a], high))

    def put(at, value):
        part[at * LANES:(at + 1) * LANES, :] = value

    even = lax.rem(lax.broadcasted_iota(jnp.int32, (LANES, LANES), 1) // BS, 2) == 0
    e_own = gram(0, (0, 2, 4))
    o_own = gram(1, (1, 3, 4))
    e_far = gram(2, (2, 4))
    o_far = gram(3, (3, 4))
    put(0, e_own[:, :LANES])
    put(1, e_own[:, LANES:2 * LANES])
    put(2, e_far[:, :LANES])
    put(3, o_own[:, :LANES])
    put(4, o_own[:, LANES:2 * LANES])
    put(5, o_far[:, :LANES])
    put(6, jnp.where(even, e_own[:, 2 * LANES:], o_own[:, 2 * LANES:]))
    put(7, jnp.where(even, e_far[:, LANES:], o_far[:, LANES:]))
    put(8, gram(4, (4,)))

    def share(owner):
        return pl.ds(pl.multiple_of(owner * SHARE, 16), SHARE)

    for step in range(1, 8):
        peer = lax.rem(row + step, 8)
        send(part.at[share(peer), :], landed.at[step - 1], part_sem.at[step - 1], {"row": peer, "col": col})
    total = part[share(row), :]
    for step in range(1, 8):
        arrive(landed.at[step - 1], part_sem.at[step - 1])
        total = total + landed[step - 1]
    gram_ref[share(row), :] = total
    for step in range(1, 8):
        peer = lax.rem(row + step, 8)
        send(gram_ref.at[share(row), :], gram_ref.at[share(row), :], full_sem.at[step - 1], {"row": peer, "col": col})
    for step in range(1, 8):
        arrive(gram_ref.at[share(0), :], full_sem.at[step - 1])

    for copy in sent:
        copy.wait_send()

    @pl.when(jnp.logical_not(at_end))
    def _():
        to_outer.wait_send()


def split(value):
    high = value.astype(BF16)
    return high, (value - high.astype(F32)).astype(BF16)


def dot1(a, b):
    return jnp.dot(a, b, preferred_element_type=F32)


def dot3(a, b):
    ah, al = a if isinstance(a, tuple) else split(a)
    bh, bl = b if isinstance(b, tuple) else split(b)
    return dot1(ah, bh) + (dot1(ah, bl) + dot1(al, bh))


def block_of(shape, axis):
    return lax.broadcasted_iota(jnp.int32, shape, axis) // BS


def identity(n):
    shape = (n, n)
    rows = lax.broadcasted_iota(jnp.int32, shape, 0)
    return (rows == lax.broadcasted_iota(jnp.int32, shape, 1)).astype(F32)


def pair_ids(blocks, ids):
    out = jnp.full(blocks.shape, ids[0], jnp.int32)
    for at, value in enumerate(ids[1:], 1):
        out = jnp.where(blocks == at, value, out)
    return out


def pair_mask(n, ids):
    return pair_ids(block_of((n, n), 0), ids) == pair_ids(block_of((n, n), 1), ids)


def angles_of(gram, eye, mask):
    kept = gram * eye
    across = jnp.sum(kept, axis=0, keepdims=True)
    down = jnp.sum(kept, axis=1, keepdims=True)
    spread = across - down
    middle = 0.5 * (across + down)
    angles = gram * spread / (2.0 * (spread * spread + middle * middle + EPSILON))
    return jnp.where(mask, angles, 0.0)


def cayley(grams, ids, x_ref, e_ref):
    n = grams[0].shape[0]
    eye = identity(n)
    mask = pair_mask(n, ids)
    angles = [split(angles_of(g, eye, mask)) for g in grams]
    squares = [dot3(a, a) for a in angles]
    bound = jnp.zeros((), F32)
    for s in squares:
        bound = jnp.maximum(bound, jnp.max(jnp.sum(jnp.abs(s), axis=1)))
    scale = 2.0 / (2.0 + bound)
    rho = bound * scale * 0.5
    lift = 2.0 / (2.0 - rho * rho)
    for at, s in enumerate(squares):
        e = eye - scale * (eye - s)
        e_ref[at, :n, :n] = e
        x_ref[at, :n, :n] = (scale * lift) * (eye + e)

    def unfinished(state):
        return state[0] > TOLERANCE

    def refine(state):
        left, grow = state
        next_grow = 2.0 / (2.0 - left * left)
        for at in range(len(grams)):
            e = split(e_ref[at, :n, :n])
            e = eye - grow * (eye - dot3(e, e))
            x = x_ref[at, :n, :n]
            e_ref[at, :n, :n] = e
            x_ref[at, :n, :n] = next_grow * (x + dot3(e, x))
        return left * left * 0.5 * next_grow, next_grow

    lax.while_loop(unfinished, refine, (rho * rho * 0.5 * lift, lift))
    turns = []
    for at, a in enumerate(angles):
        x = x_ref[at, :n, :n]
        odd = 2.0 * dot3(a, x)
        even = 2.0 * x - eye
        turns.append((even + odd, even - odd))
    return turns


def rounds_kernel(g_ref, high_ref, low_ref, out_ref, x_ref, e_ref, w_ref):
    def tile(at):
        return g_ref[at * LANES:(at + 1) * LANES, :]

    own_e, own_o, far_e, far_o, mixed = (tile(t) for t in (0, 3, 2, 5, 8))
    turns = cayley([own_e, far_e, own_o, far_o, mixed], (0, 1, 0, 1), x_ref, e_ref)
    columns = block_of((LANES, LANES), 1)
    rows = block_of((LANES, LANES), 0)
    chains = []
    for own, far, own_turn, far_turn, base, moved in (
        (own_e, far_e, turns[0], turns[1], 0, 2),
        (own_o, far_o, turns[2], turns[3], 3, 1),
    ):
        near, own_mixed, far_mixed = tile(base + 1), tile(6), tile(7)
        mixed_turn = turns[4]
        far_q = jnp.where(columns == moved, 0.0, far_turn[0])
        far_t = jnp.where(rows == moved, 0.0, far_turn[1])
        mixed_q = jnp.where(columns == moved, mixed_turn[0], 0.0)
        mixed_t = jnp.where(rows == moved, mixed_turn[1], 0.0)
        tail_q = split(jnp.concatenate([far_q, mixed_q], axis=0))
        tail_t = split(jnp.concatenate([far_t, mixed_t], axis=1))
        own_q = split(own_turn[0])
        own_t = split(own_turn[1])
        head = jnp.concatenate([near, own_mixed], axis=1)
        body = jnp.concatenate(
            [
                jnp.concatenate([far, far_mixed], axis=1),
                jnp.concatenate([far_mixed.T, mixed], axis=1),
            ],
            axis=0,
        )
        corner = dot3(own_t, dot3(own, own_q))
        side = dot3(own_t, dot3(head, tail_q))
        rest = dot3(tail_t, dot3(body, tail_q))
        gram = jnp.concatenate(
            [jnp.concatenate([corner, side], axis=1), jnp.concatenate([side.T, rest], axis=1)],
            axis=0,
        )
        chains.append((gram, own_q, tail_q))
    turns = cayley([c[0] for c in chains], (0, 1, 2, 0, 3, 1, 2, 3), x_ref, e_ref)
    grams = []
    weights = []
    for (gram, own_q, tail_q), (q, t) in zip(chains, turns):
        q = split(q)
        grams.append(dot3(t, dot3(gram, q)))
        top = (q[0][:LANES], q[1][:LANES])
        bottom = (q[0][LANES:], q[1][LANES:])
        weights.append(jnp.concatenate([dot3(own_q, top), dot3(tail_q, bottom)], axis=0))
    turns = cayley(grams, (0, 1, 2, 3, 1, 0, 3, 2), x_ref, e_ref)
    lasts = []
    for at, (q, t) in enumerate(turns):
        if at == 0:
            q = jnp.where(block_of((2 * LANES, LANES), 1) == 3, pltpu.roll(q[:, :LANES], 96, 1), q[:, LANES:])
            t = jnp.concatenate([t[LANES:LANES + 96], t[:BS]], axis=0)
        else:
            q = jnp.where(block_of((2 * LANES, LANES), 1) == 0, pltpu.roll(q[:, :LANES], BS, 1), q[:, LANES:])
            t = jnp.concatenate([t[96:LANES], t[LANES + BS:]], axis=0)
        q = split(q)
        lasts.append(dot3(t, dot3(grams[at], q)))
        weights[at] = dot3(weights[at], q)
    turns = cayley(lasts, (0, 1, 1, 0), x_ref, e_ref)
    core = lax.rem(lax.axis_index("col"), 2)
    block = block_of((2 * LANES, 2 * LANES), 1)
    block = jnp.where(core == 0, block, 7 - block)
    source = pair_ids(block, (7, 4, 2, 1, 6, 5, 3, 0))
    row = lax.broadcasted_iota(jnp.int32, (2 * LANES, 2 * LANES), 0)
    lane = lax.broadcasted_iota(jnp.int32, (2 * LANES, 2 * LANES), 1)
    place = (row == source * BS + lane % BS).astype(BF16)
    placed = []
    for at, (q, _) in enumerate(turns):
        spot = place[at * LANES:(at + 1) * LANES]
        qh, ql = split(q)
        placed.append((dot1(qh, spot).astype(BF16), dot1(ql, spot).astype(BF16)))
    e_rows = dot3(weights[0], placed[0])
    o_rows = dot3(weights[1], placed[1])
    total = jnp.concatenate(
        [
            e_rows[:2 * LANES],
            o_rows[:2 * LANES],
            e_rows[2 * LANES:] + o_rows[2 * LANES:],
        ],
        axis=0,
    )
    w_high, w_low = split(total)
    w_ref[0] = w_high
    w_ref[1] = w_low

    def strip(step, _):
        here = pl.ds(pl.multiple_of(step * STRIP, STRIP), STRIP)
        high = jnp.concatenate([high_ref[t, here, :] for t in TILE_ORDER], axis=1)
        low = jnp.concatenate([low_ref[t, here, :] for t in TILE_ORDER], axis=1)
        out_ref[here, :] = dot1(high, w_ref[0]) + (dot1(high, w_ref[1]) + dot1(low, w_ref[0]))
        return 0

    lax.fori_loop(0, high_ref.shape[1] // STRIP, strip, 0)


def shards(left_factor, right_factor, weights, plan):
    vmem = pl.BlockSpec(memory_space=pltpu.VMEM)
    dma = pltpu.SemaphoreType.DMA
    high, low, gram = pl.pallas_call(
        gather_kernel,
        name="gather_and_gram",
        out_shape=(
            jax.ShapeDtypeStruct((5, ROWS, LANES), BF16),
            jax.ShapeDtypeStruct((5, ROWS, LANES), BF16),
            jax.ShapeDtypeStruct((9 * LANES, LANES), F32),
        ),
        in_specs=[vmem, vmem, vmem, pl.BlockSpec(memory_space=pltpu.SMEM)],
        out_specs=(vmem, vmem, vmem),
        scratch_shapes=[
            pltpu.VMEM((ROWS, LANES), BF16),
            pltpu.VMEM((ROWS, LANES), BF16),
            pltpu.VMEM((16, ROWS, LANES), BF16),
            pltpu.VMEM((8, 4, DEPTH, LANES), BF16),
            pltpu.VMEM((8, 2, DEPTH, LANES), BF16),
            pltpu.VMEM((ROWS, 5 * LANES), F32),
            pltpu.VMEM((9 * LANES, LANES), F32),
            pltpu.VMEM((7, SHARE, LANES), F32),
            dma((80,)),
            dma((1,)),
            dma((2,)),
            dma((2,)),
            dma((8,)),
            dma((8,)),
            dma((15,)),
            dma((2,)),
            dma((1,)),
            dma((4,)),
            dma((4,)),
            dma((8,)),
            dma((7,)),
            dma((7,)),
        ],
        compiler_params=pltpu.CompilerParams(
            collective_id=0, has_side_effects=True, vmem_limit_bytes=VMEM_LIMIT
        ),
    )(left_factor, weights.reshape(1, -1), right_factor, plan)
    return pl.pallas_call(
        rounds_kernel,
        name="rounds",
        out_shape=jax.ShapeDtypeStruct((ROWS, 2 * LANES), F32),
        in_specs=[vmem, vmem, vmem],
        out_specs=vmem,
        scratch_shapes=[
            pltpu.VMEM((5, 2 * LANES, 2 * LANES), F32),
            pltpu.VMEM((5, 2 * LANES, 2 * LANES), F32),
            pltpu.VMEM((2, 5 * LANES, 2 * LANES), BF16),
        ],
        compiler_params=pltpu.CompilerParams(vmem_limit_bytes=VMEM_LIMIT),
    )(gram, high, low)


def solution(mesh):
    in_specs = (P("row", "col"), P("row", "col"), P("col"), P())
    out_specs = P("row", "col")
    return jax.shard_map(shards, mesh=mesh, in_specs=in_specs, out_specs=out_specs, check_vma=False)
```

```python
import functools

import jax
import jax.numpy as jnp
from jax import lax
from jax.experimental import pallas as pl
from jax.experimental.pallas import tpu as pltpu
from jax.sharding import PartitionSpec as P

BS = 32
LANES = 128
EPSILON = 1e-06
TOLERANCE = 1e-04
STRIP = 256
TILE_ORDER = (0, 2, 1, 3, 4)
BF16 = jnp.bfloat16
F32 = jnp.float32
MESH = pl.DeviceIdType.MESH
ROWS = 1024
HALF = 512
QUARTER = 256
DEPTH = 256
PACKED = 384
SHARE = 104
GRAM_ROWS = 8 * SHARE
VECTORS = 6 * LANES
VMEM_LIMIT = 48 * 1024 * 1024


def gather_kernel(
    left_hbm, weights_hbm, right_hbm, plan_hbm,
    high_ref, low_ref, gram_ref,
    left_ref, weights_ref, right_ref, plan_ref,
    own_buf, sib_buf, fold_buf, s_buf, r_own, r_out, sib_r, theta, part, landed,
    in_sem, send_sem, out_sem, sib_sem, z_sem, zo_sem, y_sem, yo_sem, ss_sem,
    zr_sem, x_sem, xo_sem, sr_sem, part_sem, full_sem,
):
    row = lax.axis_index("row")
    col = lax.axis_index("col")
    x, zl = row // 2, lax.rem(row, 2)
    core = lax.rem(col, 2)
    chip = col // 2
    y, zh = chip // 4, lax.rem(chip, 4)
    sibling = {"row": row, "col": col + 1 - 2 * core}
    outer_col = col - 1 + 2 * core
    at_end = jnp.logical_or(outer_col < 0, outer_col > 31)
    outer = {"row": row, "col": outer_col}

    def chip_at(yy, zz):
        return lax.rem(yy, 4) * 4 + lax.rem(zz, 4)

    def along(yy, zz):
        return {"row": row, "col": chip_at(yy, zz) * 2 + core}

    def row_at(xx, zz):
        return lax.rem(xx, 4) * 2 + zz

    def across(xx, zz):
        return {"row": row_at(xx, zz), "col": col}

    sent = []

    def send(src, dst, sem, device):
        copy = pltpu.make_async_remote_copy(
            src_ref=src, dst_ref=dst, send_sem=send_sem.at[len(sent)], recv_sem=sem,
            device_id=device, device_id_type=MESH,
        )
        copy.start()
        sent.append(copy)

    def arrive(ref, sem):
        pltpu.make_async_copy(ref, ref, sem).wait()

    inputs = [
        pltpu.make_async_copy(src, dst, in_sem.at[at])
        for at, (src, dst) in enumerate((
            (right_hbm, right_ref), (plan_hbm, plan_ref),
            (left_hbm, left_ref), (weights_hbm, weights_ref.at[0]),
        ))
    ]
    for copy in inputs:
        copy.start()

    barrier = pltpu.get_barrier_semaphore()
    peers = [sibling, along(y, zh + 1), along(y, zh + 3), along(y + 1, zh), along(y + 3, zh)]
    for step in range(1, 8):
        peers.append({"row": lax.rem(row + step, 8), "col": col})
    for peer in peers:
        pl.semaphore_signal(barrier, inc=1, device_id=peer, device_id_type=MESH)

    @pl.when(jnp.logical_not(at_end))
    def _():
        pl.semaphore_signal(barrier, inc=1, device_id=outer, device_id_type=MESH)

    for copy in inputs:
        copy.wait()
    scaled = (left_ref[...].astype(F32) * weights_ref[...]).astype(BF16)
    own_buf[...] = jnp.concatenate([scaled, scaled], axis=1)

    ids = []
    for slot in (0, 4, 1, 5, 2, 6, 3, 7):
        there = jnp.where(core == 0, slot, 7 - slot)
        ids.append(plan_ref[0, col * 8 + there] - col * 8)
    block = lax.broadcasted_iota(jnp.int32, (DEPTH, 256), 1) // BS
    source = jnp.zeros((DEPTH, 256), jnp.int32)
    for at, value in enumerate(ids):
        source = jnp.where(block == at, value, source)
    column = lax.broadcasted_iota(jnp.int32, (DEPTH, 256), 1)
    place = lax.broadcasted_iota(jnp.int32, (DEPTH, 256), 0) == source * BS + lax.rem(column, BS)
    ordered = jnp.dot(right_ref[...], place.astype(BF16), preferred_element_type=F32)
    lane = lax.broadcasted_iota(jnp.int32, (LANES, LANES), 1)
    odd = lax.rem(lane // BS, 2) == 1
    tail = ordered[:, LANES:]
    folded = jnp.where(odd, pltpu.roll(tail[LANES:], BS, 1), tail[:LANES]).astype(BF16)
    first = ordered[:, :LANES].astype(BF16)
    r_own[row] = jnp.concatenate([first, tail.astype(BF16)], axis=0)
    own_fold = jnp.concatenate([first, folded], axis=0)
    fold_buf[...] = own_fold

    pl.semaphore_wait(barrier, jnp.where(at_end, 12, 13))

    half = pl.multiple_of(core * HALF, HALF)
    other = pl.multiple_of(HALF - core * HALF, HALF)

    def rows_of(q, which):
        return s_buf.at[q, pl.ds(pl.multiple_of(half + which * QUARTER, QUARTER), QUARTER), :]

    def whole(q):
        return s_buf.at[q, pl.ds(half, HALF), :]

    send(own_buf.at[pl.ds(other, HALF)], sib_buf.at[pl.ds(other, HALF)], sib_sem.at[0], sibling)
    to_outer = pltpu.make_async_remote_copy(
        src_ref=fold_buf, dst_ref=r_out.at[row],
        send_sem=out_sem.at[0], recv_sem=out_sem.at[1], device_id=outer, device_id_type=MESH,
    )

    @pl.when(jnp.logical_not(at_end))
    def _():
        to_outer.start()

    @pl.when(at_end)
    def _():
        r_out[row] = own_fold

    def part_of(buf, r, which):
        size = buf.shape[1] // 2
        return buf.at[r, pl.ds(which * size, size), :]

    def x_sends(buf, zz, at):
        r = row_at(x, zz)
        send(buf.at[r], buf.at[r], x_sem.at[2 * at], across(x + 1, zl))
        send(buf.at[r], buf.at[r], x_sem.at[2 * at + 1], across(x + 3, zl))

    def share_right(r, at):
        send(r_own.at[r], sib_r.at[r], sr_sem.at[at], sibling)

    def x_arrive(buf, zz, at, share=None):
        for which, step in ((0, 3), (1, 1)):
            r = row_at(x + step, zz)
            arrive(buf.at[r], x_sem.at[2 * at + which])
            piece = part_of(buf, r, which)
            send(piece, piece, xo_sem.at[2 * at + which], across(x + 4 - step, zl))
            if share is not None:
                share_right(r, share + which)

    def x_opposite(buf, zz, at, share=None):
        r = row_at(x + 2, zz)
        for which in range(2):
            arrive(part_of(buf, r, which), xo_sem.at[2 * at + which])
        if share is not None:
            share_right(r, share)

    def pass_on(q, at):
        send(whole(q), whole(q), ss_sem.at[at], sibling)

    def y_sends(zz, at, which):
        ref = rows_of(chip_at(y, zz), which)
        send(ref, ref, y_sem.at[4 * at + which], along(y + 1, zh))
        send(ref, ref, y_sem.at[4 * at + 2 + which], along(y + 3, zh))

    def y_arrive(zz, at):
        for which in range(2):
            ref = rows_of(chip_at(y + 3, zz), which)
            arrive(ref, y_sem.at[4 * at + which])
            if which == 0:
                send(ref, ref, yo_sem.at[2 * at], along(y + 1, zh))
            ref = rows_of(chip_at(y + 1, zz), which)
            arrive(ref, y_sem.at[4 * at + 2 + which])
            if which == 1:
                send(ref, ref, yo_sem.at[2 * at + 1], along(y + 3, zh))
        pass_on(chip_at(y + 3, zz), 4 + 3 * at)
        pass_on(chip_at(y + 1, zz), 5 + 3 * at)

    def y_opposite(zz, at):
        q = chip_at(y + 2, zz)
        arrive(rows_of(q, 0), yo_sem.at[2 * at])
        arrive(rows_of(q, 1), yo_sem.at[2 * at + 1])
        pass_on(q, 6 + 3 * at)

    x_sends(r_own, zl, 0)

    arrive(sib_buf.at[pl.ds(half, HALF)], sib_sem.at[0])
    mine = (lax.broadcasted_iota(jnp.int32, (HALF, LANES), 1) // 64) == core
    here = pl.ds(half, HALF)
    s_buf[chip, here, :] = jnp.where(mine, own_buf[here, :], sib_buf[here, :])
    for which in range(2):
        ref = rows_of(chip, which)
        send(ref, ref, z_sem.at[which], along(y, zh + 1))
        send(ref, ref, z_sem.at[2 + which], along(y, zh + 3))
        y_sends(zh, 0, which)
    send(r_own.at[row], r_own.at[row], zr_sem.at[0], across(x, 1 - zl))
    pass_on(chip, 0)
    share_right(row, 0)

    @pl.when(jnp.logical_not(at_end))
    def _():
        arrive(r_out.at[row], out_sem.at[1])

    x_sends(r_out, zl, 1)
    send(r_out.at[row], r_out.at[row], zr_sem.at[1], across(x, 1 - zl))

    x_arrive(r_own, zl, 0, 2)
    y_arrive(zh, 0)

    r = row_at(x, 1 - zl)
    arrive(r_own.at[r], zr_sem.at[0])
    x_sends(r_own, 1 - zl, 2)
    share_right(r, 1)

    for which in range(2):
        ref = rows_of(chip_at(y, zh + 3), which)
        arrive(ref, z_sem.at[which])
        if which == 0:
            send(ref, ref, zo_sem.at[0], along(y, zh + 1))
        y_sends(zh + 3, 1, which)
        ref = rows_of(chip_at(y, zh + 1), which)
        arrive(ref, z_sem.at[2 + which])
        if which == 1:
            send(ref, ref, zo_sem.at[1], along(y, zh + 3))
        y_sends(zh + 1, 2, which)
    pass_on(chip_at(y, zh + 3), 1)
    pass_on(chip_at(y, zh + 1), 2)

    x_opposite(r_own, zl, 0, 4)
    x_arrive(r_out, zl, 1)
    y_opposite(zh, 0)
    arrive(r_out.at[r], zr_sem.at[1])
    x_sends(r_out, 1 - zl, 3)

    q = chip_at(y, zh + 2)
    for which in range(2):
        arrive(rows_of(q, which), zo_sem.at[which])
        y_sends(zh + 2, 3, which)
    pass_on(q, 3)

    x_arrive(r_own, 1 - zl, 2, 5)
    x_opposite(r_out, zl, 1)
    y_arrive(zh + 3, 1)
    y_arrive(zh + 1, 2)
    x_opposite(r_own, 1 - zl, 2, 7)
    x_arrive(r_out, 1 - zl, 3)
    y_opposite(zh + 3, 1)
    y_opposite(zh + 1, 2)
    y_arrive(zh + 2, 3)
    x_opposite(r_out, 1 - zl, 3)

    for at in range(8):
        arrive(sib_r.at[0], sr_sem.at[at])

    def window(r):
        sib_e = sib_r[r, :DEPTH]
        folds = r_out[r, DEPTH:]
        unfolded = pltpu.roll(folds.astype(F32), LANES - BS, 1).astype(BF16)
        mixed = jnp.concatenate(
            [jnp.where(odd, sib_e[:LANES], folds), jnp.where(odd, sib_e[LANES:], unfolded)], axis=0
        )
        return jnp.concatenate(
            [r_own[r, :DEPTH], r_own[r, DEPTH:], sib_r[r, DEPTH:], r_out[r, :DEPTH], mixed], axis=1
        )

    def add_up(yy, first):
        yy = lax.rem(yy, 4)
        weights = jnp.concatenate([window(2 * yy), window(2 * yy + 1)], axis=0)

        def strip(step, _):
            here = pl.ds(pl.multiple_of(step * STRIP, STRIP), STRIP)
            rows = jnp.concatenate([s_buf[yy * 4 + t, here, :] for t in range(4)], axis=1)
            value = jnp.dot(rows, weights, preferred_element_type=F32)
            theta[here, :] = value if first else theta[here, :] + value
            return 0

        lax.fori_loop(0, ROWS // STRIP, strip, 0)

    for at in range(4):
        arrive(whole(0), ss_sem.at[at])
    add_up(y, True)
    for at in (4, 7, 10, 13):
        arrive(whole(0), ss_sem.at[at])
    add_up(y + 3, False)
    for at in (5, 8, 11, 14):
        arrive(whole(0), ss_sem.at[at])
    add_up(y + 1, False)
    y_opposite(zh + 2, 3)
    for at in (6, 9, 12, 15):
        arrive(whole(0), ss_sem.at[at])
    add_up(y + 2, False)

    for t in range(5):
        value = theta[:, t * LANES:(t + 1) * LANES]
        rounded = value.astype(BF16)
        high_ref[t] = rounded
        low_ref[t] = (value - rounded.astype(F32)).astype(BF16)

    def gram(a, others):
        high = jnp.concatenate([high_ref[t] for t in others], axis=1)
        low = jnp.concatenate([low_ref[t] for t in others], axis=1)

        def over_rows(p, q):
            return lax.dot_general(p, q, (((0,), (0,)), ((), ())), preferred_element_type=F32)

        return over_rows(high_ref[a], high) + (over_rows(high_ref[a], low) + over_rows(low_ref[a], high))

    def put(at, value):
        part[at * LANES:(at + 1) * LANES, :] = value

    row_ids = lax.broadcasted_iota(jnp.int32, (LANES, LANES), 0)
    upper = row_ids < lane
    same = lax.rem(row_ids // BS + lane // BS, 2) == 0
    diagonal = row_ids == lane
    e_own = gram(0, (0, 2, 4))
    o_own = gram(1, (1, 3, 4))
    e_far = gram(2, (2, 4))
    o_far = gram(3, (3, 4))
    put(0, jnp.where(upper, e_own[:, :LANES], o_own[:, :LANES]))
    put(1, jnp.where(upper, e_far[:, :LANES], o_far[:, :LANES]))
    put(2, e_own[:, LANES:2 * LANES])
    put(3, o_own[:, LANES:2 * LANES])
    put(4, jnp.where(odd, o_own[:, 2 * LANES:], e_own[:, 2 * LANES:]))
    put(5, jnp.where(same, gram(4, (4,)), jnp.where(odd, o_far[:, LANES:], e_far[:, LANES:])))
    vectors = [
        jnp.sum(jnp.where(diagonal, tile[:, :LANES], 0.0), axis=0, keepdims=True)
        for tile in (e_own, e_far)
    ]
    part[VECTORS:VECTORS + 8, :] = jnp.concatenate(
        vectors + [jnp.zeros((6, LANES), F32)], axis=0
    )
    part[VECTORS + 8:, :] = jnp.zeros((GRAM_ROWS - VECTORS - 8, LANES), F32)

    def share(owner):
        return pl.ds(pl.multiple_of(owner * SHARE, 8), SHARE)

    for step in range(1, 8):
        peer = lax.rem(row + step, 8)
        send(part.at[share(peer), :], landed.at[step - 1], part_sem.at[step - 1], {"row": peer, "col": col})
    total = part[share(row), :]
    for step in range(1, 8):
        arrive(landed.at[step - 1], part_sem.at[step - 1])
        total = total + landed[step - 1]
    gram_ref[share(row), :] = total
    for step in range(1, 8):
        peer = lax.rem(row + step, 8)
        send(gram_ref.at[share(row), :], gram_ref.at[share(row), :], full_sem.at[step - 1], {"row": peer, "col": col})
    for step in range(1, 8):
        arrive(gram_ref.at[share(0), :], full_sem.at[step - 1])

    for copy in sent:
        copy.wait_send()

    @pl.when(jnp.logical_not(at_end))
    def _():
        to_outer.wait_send()


def split(value):
    high = value.astype(BF16)
    return high, (value - high.astype(F32)).astype(BF16)


def dot1(a, b):
    return jnp.dot(a, b, preferred_element_type=F32)


def dot3(a, b):
    ah, al = a if isinstance(a, tuple) else split(a)
    bh, bl = b if isinstance(b, tuple) else split(b)
    return dot1(ah, bh) + (dot1(ah, bl) + dot1(al, bh))


def block_of(shape, axis):
    return lax.broadcasted_iota(jnp.int32, shape, axis) // BS


def identity(n):
    shape = (n, n)
    rows = lax.broadcasted_iota(jnp.int32, shape, 0)
    return (rows == lax.broadcasted_iota(jnp.int32, shape, 1)).astype(F32)


def pair_ids(blocks, ids):
    out = jnp.full(blocks.shape, ids[0], jnp.int32)
    for at, value in enumerate(ids[1:], 1):
        out = jnp.where(blocks == at, value, out)
    return out


def pair_mask(n, ids):
    return pair_ids(block_of((n, n), 0), ids) == pair_ids(block_of((n, n), 1), ids)


def angles_of(gram, eye, mask):
    kept = gram * eye
    across = jnp.sum(kept, axis=0, keepdims=True)
    down = jnp.sum(kept, axis=1, keepdims=True)
    spread = across - down
    middle = 0.5 * (across + down)
    angles = gram * spread / (2.0 * (spread * spread + middle * middle + EPSILON))
    return jnp.where(mask, angles, 0.0)


def cayley(grams, ids, x_ref, e_ref):
    n = grams[0].shape[0]
    eye = identity(n)
    mask = pair_mask(n, ids)
    angles = [split(angles_of(g, eye, mask)) for g in grams]
    squares = [dot3(a, a) for a in angles]
    bound = jnp.zeros((), F32)
    for s in squares:
        bound = jnp.maximum(bound, jnp.max(jnp.sum(jnp.abs(s), axis=1)))
    scale = 2.0 / (2.0 + bound)
    rho = bound * scale * 0.5
    lift = 2.0 / (2.0 - rho * rho)
    for at, s in enumerate(squares):
        e = eye - scale * (eye - s)
        e_ref[at, :n, :n] = e
        x_ref[at, :n, :n] = (scale * lift) * (eye + e)

    def unfinished(state):
        return state[0] > TOLERANCE

    def refine(state):
        left, grow = state
        next_grow = 2.0 / (2.0 - left * left)
        for at in range(len(grams)):
            e = split(e_ref[at, :n, :n])
            e = eye - grow * (eye - dot3(e, e))
            x = x_ref[at, :n, :n]
            e_ref[at, :n, :n] = e
            x_ref[at, :n, :n] = next_grow * (x + dot3(e, x))
        return left * left * 0.5 * next_grow, next_grow

    lax.while_loop(unfinished, refine, (rho * rho * 0.5 * lift, lift))
    turns = []
    for at, a in enumerate(angles):
        x = x_ref[at, :n, :n]
        odd = 2.0 * dot3(a, x)
        even = 2.0 * x - eye
        turns.append((even + odd, even - odd))
    return turns


def rounds_kernel(g_ref, high_ref, low_ref, out_ref, x_ref, e_ref, w_ref):
    def tile(at):
        return g_ref[at * LANES:(at + 1) * LANES, :]

    shape = (LANES, LANES)
    row_ids = lax.broadcasted_iota(jnp.int32, shape, 0)
    lane_ids = lax.broadcasted_iota(jnp.int32, shape, 1)

    def both(packed, vector):
        turned = packed.T
        diagonal = row_ids == lane_ids
        upper = jnp.where(row_ids < lane_ids, packed, turned)
        upper = jnp.where(diagonal, g_ref[VECTORS + vector:VECTORS + vector + 1, :], upper)
        return upper, jnp.where(row_ids < lane_ids, turned, packed)

    own_e, own_o = both(tile(0), 0)
    far_e, far_o = both(tile(1), 1)
    mixed = tile(5)
    turns = cayley([own_e, far_e, own_o, far_o, mixed], (0, 1, 0, 1), x_ref, e_ref)
    columns = block_of((LANES, LANES), 1)
    rows = block_of((LANES, LANES), 0)
    chains = []
    for own, far, own_turn, far_turn, base, moved in (
        (own_e, far_e, turns[0], turns[1], 2, 2),
        (own_o, far_o, turns[2], turns[3], 3, 1),
    ):
        near, own_mixed, far_mixed = tile(base), tile(4), tile(5)
        mixed_turn = turns[4]
        far_q = jnp.where(columns == moved, 0.0, far_turn[0])
        far_t = jnp.where(rows == moved, 0.0, far_turn[1])
        mixed_q = jnp.where(columns == moved, mixed_turn[0], 0.0)
        mixed_t = jnp.where(rows == moved, mixed_turn[1], 0.0)
        tail_q = split(jnp.concatenate([far_q, mixed_q], axis=0))
        tail_t = split(jnp.concatenate([far_t, mixed_t], axis=1))
        own_q = split(own_turn[0])
        own_t = split(own_turn[1])
        head = jnp.concatenate([near, own_mixed], axis=1)
        body = jnp.concatenate(
            [
                jnp.concatenate([far, far_mixed], axis=1),
                jnp.concatenate([far_mixed.T, mixed], axis=1),
            ],
            axis=0,
        )
        corner = dot3(own_t, dot3(own, own_q))
        side = dot3(own_t, dot3(head, tail_q))
        rest = dot3(tail_t, dot3(body, tail_q))
        gram = jnp.concatenate(
            [jnp.concatenate([corner, side], axis=1), jnp.concatenate([side.T, rest], axis=1)],
            axis=0,
        )
        chains.append((gram, own_q, tail_q))
    turns = cayley([c[0] for c in chains], (0, 1, 2, 0, 3, 1, 2, 3), x_ref, e_ref)
    grams = []
    weights = []
    for (gram, own_q, tail_q), (q, t) in zip(chains, turns):
        q = split(q)
        grams.append(dot3(t, dot3(gram, q)))
        top = (q[0][:LANES], q[1][:LANES])
        bottom = (q[0][LANES:], q[1][LANES:])
        weights.append(jnp.concatenate([dot3(own_q, top), dot3(tail_q, bottom)], axis=0))
    turns = cayley(grams, (0, 1, 2, 3, 1, 0, 3, 2), x_ref, e_ref)
    lasts = []
    for at, (q, t) in enumerate(turns):
        if at == 0:
            q = jnp.where(block_of((2 * LANES, LANES), 1) == 3, pltpu.roll(q[:, :LANES], 96, 1), q[:, LANES:])
            t = jnp.concatenate([t[LANES:LANES + 96], t[:BS]], axis=0)
        else:
            q = jnp.where(block_of((2 * LANES, LANES), 1) == 0, pltpu.roll(q[:, :LANES], BS, 1), q[:, LANES:])
            t = jnp.concatenate([t[96:LANES], t[LANES + BS:]], axis=0)
        q = split(q)
        lasts.append(dot3(t, dot3(grams[at], q)))
        weights[at] = dot3(weights[at], q)
    turns = cayley(lasts, (0, 1, 1, 0), x_ref, e_ref)
    core = lax.rem(lax.axis_index("col"), 2)
    block = block_of((2 * LANES, 2 * LANES), 1)
    block = jnp.where(core == 0, block, 7 - block)
    source = pair_ids(block, (7, 4, 2, 1, 6, 5, 3, 0))
    row = lax.broadcasted_iota(jnp.int32, (2 * LANES, 2 * LANES), 0)
    lane = lax.broadcasted_iota(jnp.int32, (2 * LANES, 2 * LANES), 1)
    place = (row == source * BS + lane % BS).astype(BF16)
    placed = []
    for at, (q, _) in enumerate(turns):
        spot = place[at * LANES:(at + 1) * LANES]
        qh, ql = split(q)
        placed.append((dot1(qh, spot).astype(BF16), dot1(ql, spot).astype(BF16)))
    e_rows = dot3(weights[0], placed[0])
    o_rows = dot3(weights[1], placed[1])
    total = jnp.concatenate(
        [
            e_rows[:2 * LANES],
            o_rows[:2 * LANES],
            e_rows[2 * LANES:] + o_rows[2 * LANES:],
        ],
        axis=0,
    )
    w_high, w_low = split(total)
    w_ref[0] = w_high
    w_ref[1] = w_low

    def strip(step, _):
        here = pl.ds(pl.multiple_of(step * STRIP, STRIP), STRIP)
        high = jnp.concatenate([high_ref[t, here, :] for t in TILE_ORDER], axis=1)
        low = jnp.concatenate([low_ref[t, here, :] for t in TILE_ORDER], axis=1)
        out_ref[here, :] = dot1(high, w_ref[0]) + (dot1(high, w_ref[1]) + dot1(low, w_ref[0]))
        return 0

    lax.fori_loop(0, high_ref.shape[1] // STRIP, strip, 0)


def shards(left_factor, right_factor, weights, plan):
    vmem = pl.BlockSpec(memory_space=pltpu.VMEM)
    dma = pltpu.SemaphoreType.DMA
    high, low, gram = pl.pallas_call(
        gather_kernel,
        name="gather_and_gram",
        out_shape=(
            jax.ShapeDtypeStruct((5, ROWS, LANES), BF16),
            jax.ShapeDtypeStruct((5, ROWS, LANES), BF16),
            jax.ShapeDtypeStruct((GRAM_ROWS, LANES), F32),
        ),
        in_specs=[pl.BlockSpec(memory_space=pltpu.HBM)] * 4,
        out_specs=(vmem, vmem, vmem),
        scratch_shapes=[
            pltpu.VMEM((ROWS, 64), BF16),
            pltpu.VMEM((1, 64), F32),
            pltpu.VMEM((DEPTH, 2 * LANES), BF16),
            pltpu.SMEM((4, 256), jnp.int32),
            pltpu.VMEM((ROWS, LANES), BF16),
            pltpu.VMEM((ROWS, LANES), BF16),
            pltpu.VMEM((PACKED, LANES), BF16),
            pltpu.VMEM((16, ROWS, LANES), BF16),
            pltpu.VMEM((8, 2 * DEPTH, LANES), BF16),
            pltpu.VMEM((8, PACKED, LANES), BF16),
            pltpu.VMEM((8, 2 * DEPTH, LANES), BF16),
            pltpu.VMEM((ROWS, 5 * LANES), F32),
            pltpu.VMEM((GRAM_ROWS, LANES), F32),
            pltpu.VMEM((7, SHARE, LANES), F32),
        ] + [dma((count,)) for count in (4, 100, 2, 1, 4, 2, 16, 8, 16, 2, 8, 8, 8, 7, 7)],
        compiler_params=pltpu.CompilerParams(
            collective_id=0, has_side_effects=True, vmem_limit_bytes=VMEM_LIMIT
        ),
    )(left_factor, weights, right_factor, plan)
    return pl.pallas_call(
        rounds_kernel,
        name="rounds",
        out_shape=jax.ShapeDtypeStruct((ROWS, 2 * LANES), F32),
        in_specs=[vmem, vmem, vmem],
        out_specs=vmem,
        scratch_shapes=[
            pltpu.VMEM((5, 2 * LANES, 2 * LANES), F32),
            pltpu.VMEM((5, 2 * LANES, 2 * LANES), F32),
            pltpu.VMEM((2, 5 * LANES, 2 * LANES), BF16),
        ],
        compiler_params=pltpu.CompilerParams(vmem_limit_bytes=VMEM_LIMIT),
    )(gram, high, low)


def solution(mesh):
    in_specs = (P("row", "col"), P("row", "col"), P("col"), P())
    out_specs = P("row", "col")
    return jax.shard_map(shards, mesh=mesh, in_specs=in_specs, out_specs=out_specs, check_vma=False)
```

```python
import functools

import jax
import jax.numpy as jnp
from jax import lax
from jax.experimental import pallas as pl
from jax.experimental.pallas import tpu as pltpu
from jax.sharding import PartitionSpec as P

BS = 32
LANES = 128
EPSILON = 1e-06
TOLERANCE = 1e-04
STRIP = 256
TILE_ORDER = (0, 2, 1, 3, 4)
BF16 = jnp.bfloat16
F32 = jnp.float32
MESH = pl.DeviceIdType.MESH
ROWS = 1024
HALF = 512
QUARTER = 256
DEPTH = 256
PACKED = 384
SHARE = 104
GRAM_ROWS = 8 * SHARE
VECTORS = 6 * LANES
GROUPS = ((0, 64), (512, 40))
VMEM_LIMIT = 48 * 1024 * 1024


def gather_kernel(
    left_hbm, weights_hbm, right_hbm, plan_hbm,
    high_ref, low_ref, gram_ref,
    left_ref, weights_ref, right_ref, plan_ref,
    own_buf, sib_buf, fold_buf, s_buf, r_own, r_out, sib_own, sib_out,
    wide, theta, high_sib, low_sib, part, part_sib, part_in, landed,
    in_sem, send_sem, out_sem, sib_sem, z_sem, zo_sem, y_sem, yo_sem,
    zr_sem, x_sem, xo_sem, sr_sem, so_sem, part_sem, full_sem,
):
    row = lax.axis_index("row")
    col = lax.axis_index("col")
    x, zl = row // 2, lax.rem(row, 2)
    core = lax.rem(col, 2)
    chip = col // 2
    y, zh = chip // 4, lax.rem(chip, 4)
    sibling = {"row": row, "col": col + 1 - 2 * core}
    outer_col = col - 1 + 2 * core
    at_end = jnp.logical_or(outer_col < 0, outer_col > 31)
    outer = {"row": row, "col": outer_col}

    def chip_at(yy, zz):
        return lax.rem(yy, 4) * 4 + lax.rem(zz, 4)

    def along(yy, zz):
        return {"row": row, "col": chip_at(yy, zz) * 2 + core}

    def row_at(xx, zz):
        return lax.rem(xx, 4) * 2 + zz

    def across(xx, zz):
        return {"row": row_at(xx, zz), "col": col}

    sent = []

    def send(src, dst, sem, device):
        copy = pltpu.make_async_remote_copy(
            src_ref=src, dst_ref=dst, send_sem=send_sem.at[len(sent)], recv_sem=sem,
            device_id=device, device_id_type=MESH,
        )
        copy.start()
        sent.append(copy)

    def arrive(ref, sem):
        pltpu.make_async_copy(ref, ref, sem).wait()

    inputs = [
        pltpu.make_async_copy(src, dst, in_sem.at[at])
        for at, (src, dst) in enumerate((
            (left_hbm, left_ref), (weights_hbm, weights_ref.at[0]),
            (right_hbm, right_ref), (plan_hbm, plan_ref),
        ))
    ]
    for copy in inputs:
        copy.start()

    barrier = pltpu.get_barrier_semaphore()
    peers = [sibling, along(y, zh + 1), along(y, zh + 3), along(y + 1, zh), along(y + 3, zh)]
    for step in range(1, 8):
        peers.append({"row": lax.rem(row + step, 8), "col": col})
    for peer in peers:
        pl.semaphore_signal(barrier, inc=1, device_id=peer, device_id_type=MESH)

    @pl.when(jnp.logical_not(at_end))
    def _():
        pl.semaphore_signal(barrier, inc=1, device_id=outer, device_id_type=MESH)

    inputs[0].wait()
    inputs[1].wait()
    scaled = (left_ref[...].astype(F32) * weights_ref[...]).astype(BF16)
    own_buf[...] = jnp.concatenate([scaled, scaled], axis=1)

    pl.semaphore_wait(barrier, jnp.where(at_end, 12, 13))

    half = pl.multiple_of(core * HALF, HALF)
    other = pl.multiple_of(HALF - core * HALF, HALF)
    send(own_buf.at[pl.ds(other, HALF)], sib_buf.at[pl.ds(other, HALF)], sib_sem.at[0], sibling)

    inputs[2].wait()
    inputs[3].wait()
    ids = []
    for slot in (0, 4, 1, 5, 2, 6, 3, 7):
        there = jnp.where(core == 0, slot, 7 - slot)
        ids.append(plan_ref[0, col * 8 + there] - col * 8)
    block = lax.broadcasted_iota(jnp.int32, (DEPTH, 256), 1) // BS
    source = jnp.zeros((DEPTH, 256), jnp.int32)
    for at, value in enumerate(ids):
        source = jnp.where(block == at, value, source)
    column = lax.broadcasted_iota(jnp.int32, (DEPTH, 256), 1)
    place = lax.broadcasted_iota(jnp.int32, (DEPTH, 256), 0) == source * BS + lax.rem(column, BS)
    ordered = jnp.dot(right_ref[...], place.astype(BF16), preferred_element_type=F32)
    lane = lax.broadcasted_iota(jnp.int32, (LANES, LANES), 1)
    odd = lax.rem(lane // BS, 2) == 1
    tail = ordered[:, LANES:]
    folded = jnp.where(odd, pltpu.roll(tail[LANES:], BS, 1), tail[:LANES]).astype(BF16)
    first = ordered[:, :LANES].astype(BF16)
    r_own[row] = jnp.concatenate([first, tail.astype(BF16)], axis=0)
    own_fold = jnp.concatenate([first, folded], axis=0)
    fold_buf[...] = own_fold

    def rows_of(q, which):
        return s_buf.at[q, pl.ds(which * QUARTER, QUARTER), :]

    to_outer = pltpu.make_async_remote_copy(
        src_ref=fold_buf, dst_ref=r_out.at[row],
        send_sem=out_sem.at[0], recv_sem=out_sem.at[1], device_id=outer, device_id_type=MESH,
    )

    @pl.when(jnp.logical_not(at_end))
    def _():
        to_outer.start()

    @pl.when(at_end)
    def _():
        r_out[row] = own_fold

    def part_of(buf, r, which):
        size = buf.shape[1] // 2
        return buf.at[r, pl.ds(which * size, size), :]

    def x_sends(buf, zz, at):
        r = row_at(x, zz)
        send(buf.at[r], buf.at[r], x_sem.at[2 * at], across(x + 1, zl))
        send(buf.at[r], buf.at[r], x_sem.at[2 * at + 1], across(x + 3, zl))

    def share_own(r, at):
        send(r_own.at[r], sib_own.at[r], sr_sem.at[at], sibling)

    def share_out(r, at):
        send(r_out.at[r], sib_out.at[r], so_sem.at[at], sibling)

    def x_arrive(buf, zz, at, share, first):
        for which, step in ((0, 3), (1, 1)):
            r = row_at(x + step, zz)
            arrive(buf.at[r], x_sem.at[2 * at + which])
            piece = part_of(buf, r, which)
            send(piece, piece, xo_sem.at[2 * at + which], across(x + 4 - step, zl))
            share(r, first + which)

    def x_opposite(buf, zz, at, share, first):
        r = row_at(x + 2, zz)
        for which in range(2):
            arrive(part_of(buf, r, which), xo_sem.at[2 * at + which])
        share(r, first)

    def y_sends(zz, at, which):
        ref = rows_of(chip_at(y, zz), which)
        send(ref, ref, y_sem.at[4 * at + which], along(y + 1, zh))
        send(ref, ref, y_sem.at[4 * at + 2 + which], along(y + 3, zh))

    def y_arrive(zz, at):
        for which in range(2):
            ref = rows_of(chip_at(y + 3, zz), which)
            arrive(ref, y_sem.at[4 * at + which])
            if which == 0:
                send(ref, ref, yo_sem.at[2 * at], along(y + 1, zh))
            ref = rows_of(chip_at(y + 1, zz), which)
            arrive(ref, y_sem.at[4 * at + 2 + which])
            if which == 1:
                send(ref, ref, yo_sem.at[2 * at + 1], along(y + 3, zh))

    def y_opposite(zz, at):
        for which in range(2):
            arrive(rows_of(chip_at(y + 2, zz), which), yo_sem.at[2 * at + which])

    def z_sends(which):
        ref = rows_of(chip, which)
        send(ref, ref, z_sem.at[which], along(y, zh + 1))
        send(ref, ref, z_sem.at[2 + which], along(y, zh + 3))

    def z_arrive(which):
        ref = rows_of(chip_at(y, zh + 3), which)
        arrive(ref, z_sem.at[which])
        if which == 0:
            send(ref, ref, zo_sem.at[0], along(y, zh + 1))
        y_sends(zh + 3, 1, which)
        ref = rows_of(chip_at(y, zh + 1), which)
        arrive(ref, z_sem.at[2 + which])
        if which == 1:
            send(ref, ref, zo_sem.at[1], along(y, zh + 3))
        y_sends(zh + 1, 2, which)

    x_sends(r_own, zl, 0)

    arrive(sib_buf.at[pl.ds(half, HALF)], sib_sem.at[0])
    mine = (lax.broadcasted_iota(jnp.int32, (HALF, LANES), 1) // 64) == core
    here = pl.ds(half, HALF)
    s_buf[chip] = jnp.where(mine, own_buf[here, :], sib_buf[here, :])
    z_sends(0)
    z_sends(1)
    y_sends(zh, 0, 0)
    y_sends(zh, 0, 1)
    share_own(row, 0)

    @pl.when(jnp.logical_not(at_end))
    def _():
        arrive(r_out.at[row], out_sem.at[1])

    x_sends(r_out, zl, 1)
    share_out(row, 0)

    z_arrive(0)
    send(r_own.at[row], r_own.at[row], zr_sem.at[0], across(x, 1 - zl))
    x_arrive(r_own, zl, 0, share_own, 2)
    y_arrive(zh, 0)
    z_arrive(1)
    send(r_out.at[row], r_out.at[row], zr_sem.at[1], across(x, 1 - zl))
    x_opposite(r_own, zl, 0, share_own, 4)
    x_arrive(r_out, zl, 1, share_out, 2)

    r = row_at(x, 1 - zl)
    arrive(r_own.at[r], zr_sem.at[0])
    x_sends(r_own, 1 - zl, 2)
    share_own(r, 1)

    for which in range(2):
        arrive(rows_of(chip_at(y, zh + 2), which), zo_sem.at[which])
        y_sends(zh + 2, 3, which)

    arrive(r_out.at[r], zr_sem.at[1])
    x_sends(r_out, 1 - zl, 3)
    share_out(r, 1)

    y_opposite(zh, 0)
    x_opposite(r_out, zl, 1, share_out, 4)
    def mixed_tile(far, out):
        unfolded = pltpu.roll(out.astype(F32), LANES - BS, 1).astype(BF16)
        return jnp.concatenate(
            [jnp.where(odd, far[:LANES], out), jnp.where(odd, far[LANES:], unfolded)], axis=0
        )

    def window(r):
        return jnp.concatenate(
            [
                r_own[r, :DEPTH], r_own[r, DEPTH:], sib_own[r, DEPTH:], r_out[r, :DEPTH],
                mixed_tile(sib_own[r, :DEPTH], r_out[r, DEPTH:]),
                sib_own[r, :DEPTH], sib_out[r, :DEPTH],
                mixed_tile(r_own[r, :DEPTH], sib_out[r, DEPTH:]),
            ],
            axis=1,
        )

    def build(xx, at):
        arrive(sib_own.at[0], sr_sem.at[at[0]])
        arrive(sib_out.at[0], so_sem.at[at[0]])
        arrive(sib_own.at[0], sr_sem.at[at[1]])
        arrive(sib_out.at[0], so_sem.at[at[1]])
        for zz in range(2):
            r = row_at(xx, zz)
            wide[r] = window(r)

    def add_up(blocks, last=False):
        blocks = [lax.rem(yy, 4) for yy in blocks]

        def strip(step, _):
            here = pl.ds(pl.multiple_of(step * STRIP, STRIP), STRIP)
            rows = jnp.concatenate(
                [s_buf[yy * 4 + t, here, :] for yy in blocks for t in range(4)], axis=1
            )
            weights = jnp.concatenate([wide[yy * 2 + t] for yy in blocks for t in range(2)], axis=0)
            value = jnp.dot(rows, weights, preferred_element_type=F32)
            if not last:
                theta[here, :] = value
                return 0
            value = theta[here, :] + value
            high = value.astype(BF16)
            low = (value - high.astype(F32)).astype(BF16)
            there = pl.ds(pl.multiple_of(half + step * STRIP, STRIP), STRIP)
            for t, source in enumerate((0, 1, 2, 3, 4)):
                lanes = slice(source * LANES, (source + 1) * LANES)
                high_ref[t, there, :] = high[:, lanes]
                low_ref[t, there, :] = low[:, lanes]
            for t, source in enumerate((5, 2, 1, 6, 7)):
                lanes = slice(source * LANES, (source + 1) * LANES)
                high_sib[t, here, :] = high[:, lanes]
                low_sib[t, here, :] = low[:, lanes]
            return 0

        lax.fori_loop(0, HALF // STRIP, strip, 0)

    y_arrive(zh + 3, 1)
    y_arrive(zh + 1, 2)
    build(x, (0, 1))
    x_arrive(r_own, 1 - zl, 2, share_own, 5)
    x_arrive(r_out, 1 - zl, 3, share_out, 5)
    x_opposite(r_own, 1 - zl, 2, share_own, 7)
    y_arrive(zh + 2, 3)
    build(x + 3, (2, 5))
    build(x + 1, (3, 6))
    x_opposite(r_out, 1 - zl, 3, share_out, 7)
    build(x + 2, (4, 7))
    add_up((y, y + 3, y + 1))
    y_opposite(zh + 3, 1)
    y_opposite(zh + 1, 2)
    y_opposite(zh + 2, 3)
    add_up((y + 2,), last=True)

    row_ids = lax.broadcasted_iota(jnp.int32, (LANES, LANES), 0)
    upper = row_ids < lane
    same = lax.rem(row_ids // BS + lane // BS, 2) == 0
    diagonal = row_ids == lane

    def gram_of(high_at, low_at, out):
        def gram(a, others):
            high = jnp.concatenate([high_at(t) for t in others], axis=1)
            low = jnp.concatenate([low_at(t) for t in others], axis=1)

            def over_rows(p, q):
                return lax.dot_general(p, q, (((0,), (0,)), ((), ())), preferred_element_type=F32)

            return over_rows(high_at(a), high) + (over_rows(high_at(a), low) + over_rows(low_at(a), high))

        def put(at, value):
            out[at * LANES:(at + 1) * LANES, :] = value

        def vector(at, tile):
            kept = jnp.sum(jnp.where(diagonal, tile, 0.0), axis=0, keepdims=True)
            out[VECTORS + at:VECTORS + at + 1, :] = kept

        def near():
            e_own = gram(0, (0, 2, 4))
            o_own = gram(1, (1, 3, 4))
            put(0, jnp.where(upper, e_own[:, :LANES], o_own[:, :LANES]))
            put(1, e_own[:, LANES:2 * LANES])
            put(2, o_own[:, LANES:2 * LANES])
            put(3, jnp.where(odd, o_own[:, 2 * LANES:], e_own[:, 2 * LANES:]))
            out[VECTORS:, :] = jnp.zeros((GRAM_ROWS - VECTORS, LANES), F32)
            vector(0, e_own[:, :LANES])

        def far():
            e_far = gram(2, (2, 4))
            o_far = gram(3, (3, 4))
            put(4, jnp.where(upper, e_far[:, :LANES], o_far[:, :LANES]))
            put(5, jnp.where(same, gram(4, (4,)), jnp.where(odd, o_far[:, LANES:], e_far[:, LANES:])))
            vector(1, e_far[:, :LANES])

        return near, far

    for_sib = gram_of(lambda t: high_sib[t], lambda t: low_sib[t], part_sib)
    for_own = gram_of(lambda t: high_ref[t, here, :], lambda t: low_ref[t, here, :], part)

    def shares(group, owner):
        start, size = GROUPS[group]
        return pl.ds(pl.multiple_of(start + owner * size, 8), size)

    def group_rows(group):
        start, size = GROUPS[group]
        return pl.ds(start, 8 * size)

    def peer_at(step):
        return lax.rem(row + step, 8)

    for group in range(2):
        for_sib[group]()
        rows = group_rows(group)
        send(part_sib.at[rows, :], part_in.at[rows, :], sib_sem.at[1 + group], sibling)
    for group in range(2):
        for_own[group]()
        rows = group_rows(group)
        arrive(part_in.at[rows, :], sib_sem.at[1 + group])
        part[rows, :] = part[rows, :] + part_in[rows, :]
        size = GROUPS[group][1]
        for step in range(1, 8):
            send(
                part.at[shares(group, peer_at(step)), :], landed.at[group, step - 1, pl.ds(0, size), :],
                part_sem.at[7 * group + step - 1], {"row": peer_at(step), "col": col},
            )
    send(high_sib, high_ref.at[:, here, :], sib_sem.at[3], sibling)
    send(low_sib, low_ref.at[:, here, :], sib_sem.at[4], sibling)
    for group in range(2):
        size = GROUPS[group][1]
        mine = shares(group, row)
        total = part[mine, :]
        for step in range(1, 8):
            arrive(landed.at[group, step - 1, pl.ds(0, size), :], part_sem.at[7 * group + step - 1])
            total = total + landed[group, step - 1, :size]
        gram_ref[mine, :] = total
        for step in range(1, 8):
            send(
                gram_ref.at[mine, :], gram_ref.at[mine, :], full_sem.at[7 * group + step - 1],
                {"row": peer_at(step), "col": col},
            )
    for group in range(2):
        for step in range(1, 8):
            arrive(gram_ref.at[shares(group, 0), :], full_sem.at[7 * group + step - 1])
    arrive(high_sib, sib_sem.at[3])
    arrive(low_sib, sib_sem.at[4])

    for copy in sent:
        copy.wait_send()

    @pl.when(jnp.logical_not(at_end))
    def _():
        to_outer.wait_send()


def split(value):
    high = value.astype(BF16)
    return high, (value - high.astype(F32)).astype(BF16)


def dot1(a, b):
    return jnp.dot(a, b, preferred_element_type=F32)


def dot3(a, b):
    ah, al = a if isinstance(a, tuple) else split(a)
    bh, bl = b if isinstance(b, tuple) else split(b)
    return dot1(ah, bh) + (dot1(ah, bl) + dot1(al, bh))


def block_of(shape, axis):
    return lax.broadcasted_iota(jnp.int32, shape, axis) // BS


def identity(n):
    shape = (n, n)
    rows = lax.broadcasted_iota(jnp.int32, shape, 0)
    return (rows == lax.broadcasted_iota(jnp.int32, shape, 1)).astype(F32)


def pair_ids(blocks, ids):
    out = jnp.full(blocks.shape, ids[0], jnp.int32)
    for at, value in enumerate(ids[1:], 1):
        out = jnp.where(blocks == at, value, out)
    return out


def pair_mask(n, ids):
    return pair_ids(block_of((n, n), 0), ids) == pair_ids(block_of((n, n), 1), ids)


def angles_of(gram, eye, mask):
    kept = gram * eye
    across = jnp.sum(kept, axis=0, keepdims=True)
    down = jnp.sum(kept, axis=1, keepdims=True)
    spread = across - down
    middle = 0.5 * (across + down)
    angles = gram * spread / (2.0 * (spread * spread + middle * middle + EPSILON))
    return jnp.where(mask, jnp.clip(angles, -0.25, 0.25), 0.0)


def cayley(grams, ids, x_ref, e_ref):
    n = grams[0].shape[0]
    eye = identity(n)
    mask = pair_mask(n, ids)
    angles = [split(angles_of(g, eye, mask)) for g in grams]
    squares = [dot3(a, a) for a in angles]
    sums = []
    for s in squares:
        sums.append(jnp.sum(jnp.abs(s), axis=0, keepdims=True))
    bound = jnp.max(functools.reduce(jnp.maximum, sums))
    scale = 2.0 / (2.0 + bound)
    rho = bound * scale * 0.5
    lift = 2.0 / (2.0 - rho * rho)
    for at, s in enumerate(squares):
        e = eye - scale * (eye - s)
        e_ref[at, :n, :n] = e
        x_ref[at, :n, :n] = (scale * lift) * (eye + e)

    def unfinished(state):
        return state[0] > TOLERANCE

    def refine(state):
        left, grow = state
        next_grow = 2.0 / (2.0 - left * left)
        for at in range(len(grams)):
            e = split(e_ref[at, :n, :n])
            e = eye - grow * (eye - dot3(e, e))
            x = x_ref[at, :n, :n]
            e_ref[at, :n, :n] = e
            x_ref[at, :n, :n] = next_grow * (x + dot3(e, x))
        return left * left * 0.5 * next_grow, next_grow

    lax.while_loop(unfinished, refine, (rho * rho * 0.5 * lift, lift))
    turns = []
    for at, a in enumerate(angles):
        x = x_ref[at, :n, :n]
        odd = 2.0 * dot3(a, x)
        even = 2.0 * x - eye
        turns.append((even + odd, even - odd))
    return turns


def rounds_kernel(g_ref, high_ref, low_ref, out_ref, x_ref, e_ref, w_ref):
    def tile(at):
        return g_ref[at * LANES:(at + 1) * LANES, :]

    shape = (LANES, LANES)
    row_ids = lax.broadcasted_iota(jnp.int32, shape, 0)
    lane_ids = lax.broadcasted_iota(jnp.int32, shape, 1)

    def both(packed, vector):
        turned = packed.T
        diagonal = row_ids == lane_ids
        upper = jnp.where(row_ids < lane_ids, packed, turned)
        upper = jnp.where(diagonal, g_ref[VECTORS + vector:VECTORS + vector + 1, :], upper)
        return upper, jnp.where(row_ids < lane_ids, turned, packed)

    own_e, own_o = both(tile(0), 0)
    far_e, far_o = both(tile(4), 1)
    mixed = tile(5)
    turns = cayley([own_e, far_e, own_o, far_o, mixed], (0, 1, 0, 1), x_ref, e_ref)
    columns = block_of((LANES, LANES), 1)
    rows = block_of((LANES, LANES), 0)
    chains = []
    for own, far, own_turn, far_turn, base, moved in (
        (own_e, far_e, turns[0], turns[1], 1, 2),
        (own_o, far_o, turns[2], turns[3], 2, 1),
    ):
        near, own_mixed, far_mixed = tile(base), tile(3), tile(5)
        mixed_turn = turns[4]
        far_q = jnp.where(columns == moved, 0.0, far_turn[0])
        far_t = jnp.where(rows == moved, 0.0, far_turn[1])
        mixed_q = jnp.where(columns == moved, mixed_turn[0], 0.0)
        mixed_t = jnp.where(rows == moved, mixed_turn[1], 0.0)
        tail_q = split(jnp.concatenate([far_q, mixed_q], axis=0))
        tail_t = split(jnp.concatenate([far_t, mixed_t], axis=1))
        own_q = split(own_turn[0])
        own_t = split(own_turn[1])
        head = jnp.concatenate([near, own_mixed], axis=1)
        body = jnp.concatenate(
            [
                jnp.concatenate([far, far_mixed], axis=1),
                jnp.concatenate([far_mixed.T, mixed], axis=1),
            ],
            axis=0,
        )
        corner = dot3(own_t, dot3(own, own_q))
        side = dot3(own_t, dot3(head, tail_q))
        rest = dot3(tail_t, dot3(body, tail_q))
        gram = jnp.concatenate(
            [jnp.concatenate([corner, side], axis=1), jnp.concatenate([side.T, rest], axis=1)],
            axis=0,
        )
        chains.append((gram, own_q, tail_q))
    turns = cayley([c[0] for c in chains], (0, 1, 2, 0, 3, 1, 2, 3), x_ref, e_ref)
    grams = []
    weights = []
    for (gram, own_q, tail_q), (q, t) in zip(chains, turns):
        q = split(q)
        grams.append(dot3(t, dot3(gram, q)))
        top = (q[0][:LANES], q[1][:LANES])
        bottom = (q[0][LANES:], q[1][LANES:])
        weights.append(jnp.concatenate([dot3(own_q, top), dot3(tail_q, bottom)], axis=0))
    turns = cayley(grams, (0, 1, 2, 3, 1, 0, 3, 2), x_ref, e_ref)
    lasts = []
    for at, (q, t) in enumerate(turns):
        if at == 0:
            q = jnp.where(block_of((2 * LANES, LANES), 1) == 3, pltpu.roll(q[:, :LANES], 96, 1), q[:, LANES:])
            t = jnp.concatenate([t[LANES:LANES + 96], t[:BS]], axis=0)
        else:
            q = jnp.where(block_of((2 * LANES, LANES), 1) == 0, pltpu.roll(q[:, :LANES], BS, 1), q[:, LANES:])
            t = jnp.concatenate([t[96:LANES], t[LANES + BS:]], axis=0)
        q = split(q)
        lasts.append(dot3(t, dot3(grams[at], q)))
        weights[at] = dot3(weights[at], q)
    turns = cayley(lasts, (0, 1, 1, 0), x_ref, e_ref)
    core = lax.rem(lax.axis_index("col"), 2)
    block = block_of((2 * LANES, 2 * LANES), 1)
    block = jnp.where(core == 0, block, 7 - block)
    source = pair_ids(block, (7, 4, 2, 1, 6, 5, 3, 0))
    row = lax.broadcasted_iota(jnp.int32, (2 * LANES, 2 * LANES), 0)
    lane = lax.broadcasted_iota(jnp.int32, (2 * LANES, 2 * LANES), 1)
    place = (row == source * BS + lane % BS).astype(BF16)
    placed = []
    for at, (q, _) in enumerate(turns):
        spot = place[at * LANES:(at + 1) * LANES]
        qh, ql = split(q)
        placed.append((dot1(qh, spot).astype(BF16), dot1(ql, spot).astype(BF16)))
    e_rows = dot3(weights[0], placed[0])
    o_rows = dot3(weights[1], placed[1])
    total = jnp.concatenate(
        [
            e_rows[:2 * LANES],
            o_rows[:2 * LANES],
            e_rows[2 * LANES:] + o_rows[2 * LANES:],
        ],
        axis=0,
    )
    w_high, w_low = split(total)
    w_ref[0] = w_high
    w_ref[1] = w_low

    def strip(step, _):
        here = pl.ds(pl.multiple_of(step * STRIP, STRIP), STRIP)
        high = jnp.concatenate([high_ref[t, here, :] for t in TILE_ORDER], axis=1)
        low = jnp.concatenate([low_ref[t, here, :] for t in TILE_ORDER], axis=1)
        out_ref[here, :] = dot1(high, w_ref[0]) + (dot1(high, w_ref[1]) + dot1(low, w_ref[0]))
        return 0

    lax.fori_loop(0, high_ref.shape[1] // STRIP, strip, 0)


def shards(left_factor, right_factor, weights, plan):
    vmem = pl.BlockSpec(memory_space=pltpu.VMEM)
    dma = pltpu.SemaphoreType.DMA
    high, low, gram = pl.pallas_call(
        gather_kernel,
        name="gather_and_gram",
        out_shape=(
            jax.ShapeDtypeStruct((5, ROWS, LANES), BF16),
            jax.ShapeDtypeStruct((5, ROWS, LANES), BF16),
            jax.ShapeDtypeStruct((GRAM_ROWS, LANES), F32),
        ),
        in_specs=[pl.BlockSpec(memory_space=pltpu.HBM)] * 4,
        out_specs=(vmem, vmem, vmem),
        scratch_shapes=[
            pltpu.VMEM((ROWS, 64), BF16),
            pltpu.VMEM((1, 64), F32),
            pltpu.VMEM((DEPTH, 2 * LANES), BF16),
            pltpu.SMEM((4, 256), jnp.int32),
            pltpu.VMEM((ROWS, LANES), BF16),
            pltpu.VMEM((ROWS, LANES), BF16),
            pltpu.VMEM((PACKED, LANES), BF16),
            pltpu.VMEM((16, HALF, LANES), BF16),
            pltpu.VMEM((8, 2 * DEPTH, LANES), BF16),
            pltpu.VMEM((8, PACKED, LANES), BF16),
            pltpu.VMEM((8, 2 * DEPTH, LANES), BF16),
            pltpu.VMEM((8, PACKED, LANES), BF16),
            pltpu.VMEM((8, DEPTH, 8 * LANES), BF16),
            pltpu.VMEM((HALF, 8 * LANES), F32),
            pltpu.VMEM((5, HALF, LANES), BF16),
            pltpu.VMEM((5, HALF, LANES), BF16),
            pltpu.VMEM((GRAM_ROWS, LANES), F32),
            pltpu.VMEM((GRAM_ROWS, LANES), F32),
            pltpu.VMEM((GRAM_ROWS, LANES), F32),
            pltpu.VMEM((2, 7, 64, LANES), F32),
        ] + [dma((count,)) for count in (4, 110, 2, 5, 4, 2, 16, 8, 2, 8, 8, 8, 8, 14, 14)],
        compiler_params=pltpu.CompilerParams(
            collective_id=0, has_side_effects=True, vmem_limit_bytes=VMEM_LIMIT
        ),
    )(left_factor, weights, right_factor, plan)
    return pl.pallas_call(
        rounds_kernel,
        name="rounds",
        out_shape=jax.ShapeDtypeStruct((ROWS, 2 * LANES), F32),
        in_specs=[vmem, vmem, vmem],
        out_specs=vmem,
        scratch_shapes=[
            pltpu.VMEM((5, 2 * LANES, 2 * LANES), F32),
            pltpu.VMEM((5, 2 * LANES, 2 * LANES), F32),
            pltpu.VMEM((2, 5 * LANES, 2 * LANES), BF16),
        ],
        compiler_params=pltpu.CompilerParams(vmem_limit_bytes=VMEM_LIMIT),
    )(gram, high, low)


def solution(mesh):
    in_specs = (P("row", "col"), P("row", "col"), P("col"), P())
    out_specs = P("row", "col")
    return jax.shard_map(shards, mesh=mesh, in_specs=in_specs, out_specs=out_specs, check_vma=False)
```

```python
import functools

import jax
import jax.numpy as jnp
from jax import lax
from jax.experimental import pallas as pl
from jax.experimental.pallas import tpu as pltpu
from jax.sharding import PartitionSpec as P

BS = 32
LANES = 128
EPSILON = 1e-06
TOLERANCE = 1e-04
STRIP = 256
TILE_ORDER = (0, 2, 1, 3, 4)
ALTERNATE = (0, 1, 0, 1)
ADJACENT = (0, 0, 1, 1)
OUTSIDE = (0, 1, 1, 0)
BF16 = jnp.bfloat16
F32 = jnp.float32
MESH = pl.DeviceIdType.MESH
ROWS = 1024
HALF = 512
QUARTER = 256
DEPTH = 256
PACKED = 384
SHARE = 104
GRAM_ROWS = 8 * SHARE
VECTORS = 6 * LANES
GROUPS = ((0, 64), (512, 40))
VMEM_LIMIT = 48 * 1024 * 1024


def gather_kernel(
    left_hbm, weights_hbm, right_hbm, plan_hbm,
    high_ref, low_ref, gram_ref,
    left_ref, weights_ref, right_ref, plan_ref,
    own_buf, sib_buf, fold_buf, s_buf, r_own, r_out, sib_own, sib_out,
    wide, theta, high_sib, low_sib, part, part_sib, part_in, landed,
    in_sem, send_sem, out_sem, sib_sem, z_sem, zo_sem, y_sem, yo_sem,
    zr_sem, x_sem, xo_sem, sr_sem, so_sem, part_sem, full_sem,
):
    row = lax.axis_index("row")
    col = lax.axis_index("col")
    x, zl = row // 2, lax.rem(row, 2)
    core = lax.rem(col, 2)
    chip = col // 2
    y, zh = chip // 4, lax.rem(chip, 4)
    sibling = {"row": row, "col": col + 1 - 2 * core}
    outer_col = col - 1 + 2 * core
    at_end = jnp.logical_or(outer_col < 0, outer_col > 31)
    outer = {"row": row, "col": outer_col}

    def chip_at(yy, zz):
        return lax.rem(yy, 4) * 4 + lax.rem(zz, 4)

    def along(yy, zz):
        return {"row": row, "col": chip_at(yy, zz) * 2 + core}

    def row_at(xx, zz):
        return lax.rem(xx, 4) * 2 + zz

    def across(xx, zz):
        return {"row": row_at(xx, zz), "col": col}

    sent = []

    def send(src, dst, sem, device):
        copy = pltpu.make_async_remote_copy(
            src_ref=src, dst_ref=dst, send_sem=send_sem.at[len(sent)], recv_sem=sem,
            device_id=device, device_id_type=MESH,
        )
        copy.start()
        sent.append(copy)

    def arrive(ref, sem):
        pltpu.make_async_copy(ref, ref, sem).wait()

    inputs = [
        pltpu.make_async_copy(src, dst, in_sem.at[at])
        for at, (src, dst) in enumerate((
            (left_hbm, left_ref), (weights_hbm, weights_ref.at[0]),
            (right_hbm, right_ref), (plan_hbm, plan_ref),
        ))
    ]
    for copy in inputs:
        copy.start()

    barrier = pltpu.get_barrier_semaphore()
    peers = [sibling, along(y, zh + 1), along(y, zh + 3), along(y + 1, zh), along(y + 3, zh)]
    for step in range(1, 8):
        peers.append({"row": lax.rem(row + step, 8), "col": col})
    for peer in peers:
        pl.semaphore_signal(barrier, inc=1, device_id=peer, device_id_type=MESH)

    @pl.when(jnp.logical_not(at_end))
    def _():
        pl.semaphore_signal(barrier, inc=1, device_id=outer, device_id_type=MESH)

    inputs[0].wait()
    inputs[1].wait()
    scaled = (left_ref[...].astype(F32) * weights_ref[...]).astype(BF16)
    own_buf[...] = jnp.concatenate([scaled, scaled], axis=1)

    pl.semaphore_wait(barrier, jnp.where(at_end, 12, 13))

    half = pl.multiple_of(core * HALF, HALF)
    other = pl.multiple_of(HALF - core * HALF, HALF)
    send(own_buf.at[pl.ds(other, HALF)], sib_buf.at[pl.ds(other, HALF)], sib_sem.at[0], sibling)

    inputs[2].wait()
    inputs[3].wait()
    ids = []
    for slot in (0, 4, 1, 5, 2, 6, 3, 7):
        there = jnp.where(core == 0, slot, 7 - slot)
        ids.append(plan_ref[0, col * 8 + there] - col * 8)
    block = lax.broadcasted_iota(jnp.int32, (DEPTH, 256), 1) // BS
    source = jnp.zeros((DEPTH, 256), jnp.int32)
    for at, value in enumerate(ids):
        source = jnp.where(block == at, value, source)
    column = lax.broadcasted_iota(jnp.int32, (DEPTH, 256), 1)
    place = lax.broadcasted_iota(jnp.int32, (DEPTH, 256), 0) == source * BS + lax.rem(column, BS)
    ordered = jnp.dot(right_ref[...], place.astype(BF16), preferred_element_type=F32)
    lane = lax.broadcasted_iota(jnp.int32, (LANES, LANES), 1)
    odd = lax.rem(lane // BS, 2) == 1
    tail = ordered[:, LANES:]
    folded = jnp.where(odd, pltpu.roll(tail[LANES:], BS, 1), tail[:LANES]).astype(BF16)
    first = ordered[:, :LANES].astype(BF16)
    r_own[row] = jnp.concatenate([first, tail.astype(BF16)], axis=0)
    own_fold = jnp.concatenate([first, folded], axis=0)
    fold_buf[...] = own_fold

    def rows_of(q, which):
        return s_buf.at[q, pl.ds(which * QUARTER, QUARTER), :]

    to_outer = pltpu.make_async_remote_copy(
        src_ref=fold_buf, dst_ref=r_out.at[row],
        send_sem=out_sem.at[0], recv_sem=out_sem.at[1], device_id=outer, device_id_type=MESH,
    )

    @pl.when(jnp.logical_not(at_end))
    def _():
        to_outer.start()

    @pl.when(at_end)
    def _():
        r_out[row] = own_fold

    def part_of(buf, r, which):
        size = buf.shape[1] // 2
        return buf.at[r, pl.ds(which * size, size), :]

    def x_sends(buf, zz, at):
        r = row_at(x, zz)
        send(buf.at[r], buf.at[r], x_sem.at[2 * at], across(x + 1, zl))
        send(buf.at[r], buf.at[r], x_sem.at[2 * at + 1], across(x + 3, zl))

    def share_own(r, at):
        send(r_own.at[r], sib_own.at[r], sr_sem.at[at], sibling)

    def share_out(r, at):
        send(r_out.at[r], sib_out.at[r], so_sem.at[at], sibling)

    def x_arrive(buf, zz, at, share, first):
        for which, step in ((0, 3), (1, 1)):
            r = row_at(x + step, zz)
            arrive(buf.at[r], x_sem.at[2 * at + which])
            piece = part_of(buf, r, which)
            send(piece, piece, xo_sem.at[2 * at + which], across(x + 4 - step, zl))
            share(r, first + which)

    def x_opposite(buf, zz, at, share, first):
        r = row_at(x + 2, zz)
        for which in range(2):
            arrive(part_of(buf, r, which), xo_sem.at[2 * at + which])
        share(r, first)

    def y_sends(zz, at, which):
        ref = rows_of(chip_at(y, zz), which)
        send(ref, ref, y_sem.at[4 * at + which], along(y + 1, zh))
        send(ref, ref, y_sem.at[4 * at + 2 + which], along(y + 3, zh))

    def y_arrive(zz, at):
        for which in range(2):
            ref = rows_of(chip_at(y + 3, zz), which)
            arrive(ref, y_sem.at[4 * at + which])
            if which == 0:
                send(ref, ref, yo_sem.at[2 * at], along(y + 1, zh))
            ref = rows_of(chip_at(y + 1, zz), which)
            arrive(ref, y_sem.at[4 * at + 2 + which])
            if which == 1:
                send(ref, ref, yo_sem.at[2 * at + 1], along(y + 3, zh))

    def y_opposite(zz, at):
        for which in range(2):
            arrive(rows_of(chip_at(y + 2, zz), which), yo_sem.at[2 * at + which])

    def z_sends(which):
        ref = rows_of(chip, which)
        send(ref, ref, z_sem.at[which], along(y, zh + 1))
        send(ref, ref, z_sem.at[2 + which], along(y, zh + 3))

    def z_arrive(which):
        ref = rows_of(chip_at(y, zh + 3), which)
        arrive(ref, z_sem.at[which])
        if which == 0:
            send(ref, ref, zo_sem.at[0], along(y, zh + 1))
        y_sends(zh + 3, 1, which)
        ref = rows_of(chip_at(y, zh + 1), which)
        arrive(ref, z_sem.at[2 + which])
        if which == 1:
            send(ref, ref, zo_sem.at[1], along(y, zh + 3))
        y_sends(zh + 1, 2, which)

    x_sends(r_own, zl, 0)

    arrive(sib_buf.at[pl.ds(half, HALF)], sib_sem.at[0])
    mine = (lax.broadcasted_iota(jnp.int32, (HALF, LANES), 1) // 64) == core
    here = pl.ds(half, HALF)
    s_buf[chip] = jnp.where(mine, own_buf[here, :], sib_buf[here, :])
    z_sends(0)
    z_sends(1)
    y_sends(zh, 0, 0)
    y_sends(zh, 0, 1)
    share_own(row, 0)

    @pl.when(jnp.logical_not(at_end))
    def _():
        arrive(r_out.at[row], out_sem.at[1])

    x_sends(r_out, zl, 1)
    share_out(row, 0)

    z_arrive(0)
    send(r_own.at[row], r_own.at[row], zr_sem.at[0], across(x, 1 - zl))
    x_arrive(r_own, zl, 0, share_own, 2)
    y_arrive(zh, 0)
    z_arrive(1)
    send(r_out.at[row], r_out.at[row], zr_sem.at[1], across(x, 1 - zl))
    x_opposite(r_own, zl, 0, share_own, 4)
    x_arrive(r_out, zl, 1, share_out, 2)

    r = row_at(x, 1 - zl)
    arrive(r_own.at[r], zr_sem.at[0])
    x_sends(r_own, 1 - zl, 2)
    share_own(r, 1)

    for which in range(2):
        arrive(rows_of(chip_at(y, zh + 2), which), zo_sem.at[which])
        y_sends(zh + 2, 3, which)

    arrive(r_out.at[r], zr_sem.at[1])
    x_sends(r_out, 1 - zl, 3)
    share_out(r, 1)

    y_opposite(zh, 0)
    x_opposite(r_out, zl, 1, share_out, 4)
    def mixed_tile(far, out):
        unfolded = pltpu.roll(out.astype(F32), LANES - BS, 1).astype(BF16)
        return jnp.concatenate(
            [jnp.where(odd, far[:LANES], out), jnp.where(odd, far[LANES:], unfolded)], axis=0
        )

    def window(r):
        return jnp.concatenate(
            [
                r_own[r, :DEPTH], r_own[r, DEPTH:], sib_own[r, DEPTH:], r_out[r, :DEPTH],
                mixed_tile(sib_own[r, :DEPTH], r_out[r, DEPTH:]),
                sib_own[r, :DEPTH], sib_out[r, :DEPTH],
                mixed_tile(r_own[r, :DEPTH], sib_out[r, DEPTH:]),
            ],
            axis=1,
        )

    def build(xx, at):
        arrive(sib_own.at[0], sr_sem.at[at[0]])
        arrive(sib_out.at[0], so_sem.at[at[0]])
        arrive(sib_own.at[0], sr_sem.at[at[1]])
        arrive(sib_out.at[0], so_sem.at[at[1]])
        for zz in range(2):
            r = row_at(xx, zz)
            wide[r] = window(r)

    def add_up(blocks, last=False):
        blocks = [lax.rem(yy, 4) for yy in blocks]

        def strip(step, _):
            here = pl.ds(pl.multiple_of(step * STRIP, STRIP), STRIP)
            rows = jnp.concatenate(
                [s_buf[yy * 4 + t, here, :] for yy in blocks for t in range(4)], axis=1
            )
            weights = jnp.concatenate([wide[yy * 2 + t] for yy in blocks for t in range(2)], axis=0)
            value = jnp.dot(rows, weights, preferred_element_type=F32)
            if not last:
                theta[here, :] = value
                return 0
            value = theta[here, :] + value
            high = value.astype(BF16)
            low = (value - high.astype(F32)).astype(BF16)
            there = pl.ds(pl.multiple_of(half + step * STRIP, STRIP), STRIP)
            for t, source in enumerate((0, 1, 2, 3, 4)):
                lanes = slice(source * LANES, (source + 1) * LANES)
                high_ref[t, there, :] = high[:, lanes]
                low_ref[t, there, :] = low[:, lanes]
            for t, source in enumerate((5, 2, 1, 6, 7)):
                lanes = slice(source * LANES, (source + 1) * LANES)
                high_sib[t, here, :] = high[:, lanes]
                low_sib[t, here, :] = low[:, lanes]
            return 0

        lax.fori_loop(0, HALF // STRIP, strip, 0)

    y_arrive(zh + 3, 1)
    y_arrive(zh + 1, 2)
    build(x, (0, 1))
    x_arrive(r_own, 1 - zl, 2, share_own, 5)
    x_arrive(r_out, 1 - zl, 3, share_out, 5)
    x_opposite(r_own, 1 - zl, 2, share_own, 7)
    y_arrive(zh + 2, 3)
    build(x + 3, (2, 5))
    build(x + 1, (3, 6))
    far_x = lax.rem(x + 2, 4)
    late = jnp.where(far_x == y, y, jnp.where(far_x == lax.rem(y + 1, 4), y + 1, y + 3))
    early = jnp.where(late == y, y + 1, y), jnp.where(late == y + 3, y + 1, y + 3)
    add_up(early)
    x_opposite(r_out, 1 - zl, 3, share_out, 7)
    build(x + 2, (4, 7))
    y_opposite(zh + 3, 1)
    y_opposite(zh + 1, 2)
    y_opposite(zh + 2, 3)
    add_up((late, y + 2), last=True)

    row_ids = lax.broadcasted_iota(jnp.int32, (LANES, LANES), 0)
    upper = row_ids < lane
    same = lax.rem(row_ids // BS + lane // BS, 2) == 0
    diagonal = row_ids == lane

    def gram_of(high_at, low_at, out):
        def gram(a, others):
            high = jnp.concatenate([high_at(t) for t in others], axis=1)
            low = jnp.concatenate([low_at(t) for t in others], axis=1)

            def over_rows(p, q):
                return lax.dot_general(p, q, (((0,), (0,)), ((), ())), preferred_element_type=F32)

            return over_rows(high_at(a), high) + (over_rows(high_at(a), low) + over_rows(low_at(a), high))

        def put(at, value):
            out[at * LANES:(at + 1) * LANES, :] = value

        def vector(at, tile):
            kept = jnp.sum(jnp.where(diagonal, tile, 0.0), axis=0, keepdims=True)
            out[VECTORS + at:VECTORS + at + 1, :] = kept

        def near():
            e_own = gram(0, (0, 2, 4))
            o_own = gram(1, (1, 3, 4))
            put(0, jnp.where(upper, e_own[:, :LANES], o_own[:, :LANES]))
            put(1, e_own[:, LANES:2 * LANES])
            put(2, o_own[:, LANES:2 * LANES])
            put(3, jnp.where(odd, o_own[:, 2 * LANES:], e_own[:, 2 * LANES:]))
            out[VECTORS:, :] = jnp.zeros((GRAM_ROWS - VECTORS, LANES), F32)
            vector(0, e_own[:, :LANES])

        def far():
            e_far = gram(2, (2, 4))
            o_far = gram(3, (3, 4))
            put(4, jnp.where(upper, e_far[:, :LANES], o_far[:, :LANES]))
            put(5, jnp.where(same, gram(4, (4,)), jnp.where(odd, o_far[:, LANES:], e_far[:, LANES:])))
            vector(1, e_far[:, :LANES])

        return near, far

    gathered = len(sent)
    for_sib = gram_of(lambda t: high_sib[t], lambda t: low_sib[t], part_sib)
    for_own = gram_of(lambda t: high_ref[t, here, :], lambda t: low_ref[t, here, :], part)

    def shares(group, owner):
        start, size = GROUPS[group]
        return pl.ds(pl.multiple_of(start + owner * size, 8), size)

    def group_rows(group):
        start, size = GROUPS[group]
        return pl.ds(start, 8 * size)

    def peer_at(step):
        return lax.rem(row + step, 8)

    for group in range(2):
        for_sib[group]()
        rows = group_rows(group)
        send(part_sib.at[rows, :], part_in.at[rows, :], sib_sem.at[1 + group], sibling)
        for_own[group]()
        arrive(part_in.at[rows, :], sib_sem.at[1 + group])
        part[rows, :] = part[rows, :] + part_in[rows, :]
        size = GROUPS[group][1]
        for step in range(1, 8):
            send(
                part.at[shares(group, peer_at(step)), :], landed.at[group, step - 1, pl.ds(0, size), :],
                part_sem.at[7 * group + step - 1], {"row": peer_at(step), "col": col},
            )
    send(high_sib, high_ref.at[:, here, :], sib_sem.at[3], sibling)
    send(low_sib, low_ref.at[:, here, :], sib_sem.at[4], sibling)
    for copy in sent[:gathered]:
        copy.wait_send()
    summed = len(sent)
    for group in range(2):
        size = GROUPS[group][1]
        mine = shares(group, row)
        total = part[mine, :]
        for step in range(1, 8):
            arrive(landed.at[group, step - 1, pl.ds(0, size), :], part_sem.at[7 * group + step - 1])
            total = total + landed[group, step - 1, :size]
        gram_ref[mine, :] = total
        for step in range(1, 8):
            send(
                gram_ref.at[mine, :], gram_ref.at[mine, :], full_sem.at[7 * group + step - 1],
                {"row": peer_at(step), "col": col},
            )

    @pl.when(jnp.logical_not(at_end))
    def _():
        to_outer.wait_send()

    for copy in sent[gathered:summed]:
        copy.wait_send()
    arrive(high_sib, sib_sem.at[3])
    arrive(low_sib, sib_sem.at[4])
    for group in range(2):
        for step in range(1, 8):
            arrive(gram_ref.at[shares(group, 0), :], full_sem.at[7 * group + step - 1])
    for copy in sent[summed:]:
        copy.wait_send()


def split(value):
    high = value.astype(BF16)
    return high, (value - high.astype(F32)).astype(BF16)


def dot1(a, b):
    return jnp.dot(a, b, preferred_element_type=F32)


def dot3(a, b):
    ah, al = a if isinstance(a, tuple) else split(a)
    bh, bl = b if isinstance(b, tuple) else split(b)
    return dot1(ah, bh) + (dot1(ah, bl) + dot1(al, bh))


def block_of(shape, axis):
    return lax.broadcasted_iota(jnp.int32, shape, axis) // BS


def identity(n):
    shape = (n, n)
    rows = lax.broadcasted_iota(jnp.int32, shape, 0)
    return (rows == lax.broadcasted_iota(jnp.int32, shape, 1)).astype(F32)


def pair_ids(blocks, ids):
    out = jnp.full(blocks.shape, ids[0], jnp.int32)
    for at, value in enumerate(ids[1:], 1):
        out = jnp.where(blocks == at, value, out)
    return out


def pair_mask(n, ids):
    return pair_ids(block_of((n, n), 0), ids) == pair_ids(block_of((n, n), 1), ids)


def angles_of(gram, eye, mask):
    kept = gram * eye
    across = jnp.sum(kept, axis=0, keepdims=True)
    down = jnp.sum(kept, axis=1, keepdims=True)
    spread = across - down
    middle = 0.5 * (across + down)
    angles = gram * spread / (2.0 * (spread * spread + middle * middle + EPSILON))
    return jnp.where(mask, jnp.clip(angles, -0.25, 0.25), 0.0)


def cayley(grams, ids, x_ref, e_ref):
    n = grams[0].shape[0]
    eye = identity(n)
    masks = {each: pair_mask(n, each) for each in set(ids)}
    angles = [split(angles_of(g, eye, masks[each])) for g, each in zip(grams, ids)]
    squares = [dot3(a, a) for a in angles]
    sums = []
    for s in squares:
        sums.append(jnp.sum(jnp.abs(s), axis=0, keepdims=True))
    bound = jnp.max(functools.reduce(jnp.maximum, sums))
    scale = 2.0 / (2.0 + bound)
    rho = bound * scale * 0.5
    lift = 2.0 / (2.0 - rho * rho)
    for at, s in enumerate(squares):
        e = eye - scale * (eye - s)
        e_ref[at, :n, :n] = e
        x_ref[at, :n, :n] = (scale * lift) * (eye + e)

    def unfinished(state):
        return state[0] > TOLERANCE

    def refine(state):
        left, grow = state
        next_grow = 2.0 / (2.0 - left * left)
        for at in range(len(grams)):
            e = split(e_ref[at, :n, :n])
            e = eye - grow * (eye - dot3(e, e))
            x = x_ref[at, :n, :n]
            e_ref[at, :n, :n] = e
            x_ref[at, :n, :n] = next_grow * (x + dot3(e, x))
        return left * left * 0.5 * next_grow, next_grow

    lax.while_loop(unfinished, refine, (rho * rho * 0.5 * lift, lift))
    turns = []
    for at, a in enumerate(angles):
        x = x_ref[at, :n, :n]
        odd = 2.0 * dot3(a, x)
        even = 2.0 * x - eye
        turns.append((even + odd, even - odd))
    return turns


def swap_middle(a, b, axis):
    if axis == 0:
        return (
            jnp.concatenate([a[:64], b[BS:64], a[96:]], axis=0),
            jnp.concatenate([b[:BS], a[64:96], b[64:]], axis=0),
        )
    block = block_of(a.shape, 1)
    return (
        jnp.where(block == 2, pltpu.roll(b, BS, 1), a),
        jnp.where(block == 1, pltpu.roll(a, LANES - BS, 1), b),
    )


def swap_odd(a, b, axis):
    if axis == 0:
        return (
            jnp.concatenate([a[:BS], b[BS:64], a[64:96], b[96:]], axis=0),
            jnp.concatenate([b[:BS], a[BS:64], b[64:96], a[96:]], axis=0),
        )
    odd = lax.rem(block_of(a.shape, 1), 2) == 1
    return jnp.where(odd, b, a), jnp.where(odd, a, b)


def swap_ends(a, b, axis):
    if axis == 0:
        return (
            jnp.concatenate([a[:96], b[:BS]], axis=0),
            jnp.concatenate([a[96:], b[BS:]], axis=0),
        )
    block = block_of(a.shape, 1)
    return (
        jnp.where(block == 3, pltpu.roll(b, 96, 1), a),
        jnp.where(block == 0, pltpu.roll(a, BS, 1), b),
    )


def regroup(gram, swap):
    near, cross, far = gram
    near, cross_top = swap(near, cross, 1)
    cross_bottom, far = swap(cross.T, far, 1)
    near, _ = swap(near, cross_bottom, 0)
    cross, far = swap(cross_top, far, 0)
    return near, cross, far


def rounds_kernel(g_ref, high_ref, low_ref, out_ref, x_ref, e_ref, w_ref, stage, out_sem):
    def tile(at):
        return g_ref[at * LANES:(at + 1) * LANES, :]

    shape = (LANES, LANES)
    row_ids = lax.broadcasted_iota(jnp.int32, shape, 0)
    lane_ids = lax.broadcasted_iota(jnp.int32, shape, 1)

    def both(packed, vector):
        turned = packed.T
        diagonal = row_ids == lane_ids
        upper = jnp.where(row_ids < lane_ids, packed, turned)
        upper = jnp.where(diagonal, g_ref[VECTORS + vector:VECTORS + vector + 1, :], upper)
        return upper, jnp.where(row_ids < lane_ids, turned, packed)

    own_e, own_o = both(tile(0), 0)
    far_e, far_o = both(tile(4), 1)
    mixed = tile(5)
    turns = cayley([own_e, far_e, own_o, far_o, mixed], (ALTERNATE,) * 5, x_ref, e_ref)
    columns = block_of((LANES, LANES), 1)
    rows = block_of((LANES, LANES), 0)
    chains = []
    for own, far, own_turn, far_turn, base, moved in (
        (own_e, far_e, turns[0], turns[1], 1, 2),
        (own_o, far_o, turns[2], turns[3], 2, 1),
    ):
        near, own_mixed, far_mixed = tile(base), tile(3), tile(5)
        mixed_turn = turns[4]
        far_q = jnp.where(columns == moved, 0.0, far_turn[0])
        far_t = jnp.where(rows == moved, 0.0, far_turn[1])
        mixed_q = jnp.where(columns == moved, mixed_turn[0], 0.0)
        mixed_t = jnp.where(rows == moved, mixed_turn[1], 0.0)
        tail_q = split(jnp.concatenate([far_q, mixed_q], axis=0))
        tail_t = split(jnp.concatenate([far_t, mixed_t], axis=1))
        own_q = split(own_turn[0])
        own_t = split(own_turn[1])
        head = jnp.concatenate([near, own_mixed], axis=1)
        body = jnp.concatenate(
            [
                jnp.concatenate([far, far_mixed], axis=1),
                jnp.concatenate([far_mixed.T, mixed], axis=1),
            ],
            axis=0,
        )
        corner = dot3(own_t, dot3(own, own_q))
        side = dot3(own_t, dot3(head, tail_q))
        rest = dot3(tail_t, dot3(body, tail_q))
        chains.append((regroup((corner, side, rest), swap_middle), own_q, tail_q))
    turns = cayley([t for c in chains for t in (c[0][0], c[0][2])], (OUTSIDE,) * 4, x_ref, e_ref)
    grams = []
    weights = []
    for at, ((near, cross, far), own_q, tail_q) in enumerate(chains):
        (near_q, near_t), (far_q, far_t) = turns[2 * at:2 * at + 2]
        zero = jnp.zeros((BS, LANES), F32)
        top = jnp.concatenate(
            [
                jnp.concatenate([near_q[:64], zero, near_q[96:]], axis=0),
                jnp.concatenate([zero, zero, far_q[BS:64], zero], axis=0),
            ],
            axis=1,
        )
        bottom = jnp.concatenate(
            [
                jnp.concatenate([zero, near_q[64:96], zero, zero], axis=0),
                jnp.concatenate([far_q[:BS], zero, far_q[64:]], axis=0),
            ],
            axis=1,
        )
        spread = jnp.concatenate([dot3(own_q, top), dot3(tail_q, bottom)], axis=0)
        swap = swap_odd if at == 0 else swap_ends
        weights.append(jnp.concatenate(swap(spread[:, :LANES], spread[:, LANES:], 1), axis=1))
        near_q, near_t, far_q, far_t = split(near_q), split(near_t), split(far_q), split(far_t)
        turned = (
            dot3(near_t, dot3(near, near_q)),
            dot3(near_t, dot3(cross, far_q)),
            dot3(far_t, dot3(far, far_q)),
        )
        grams.append(regroup(turned, swap))
    turns = cayley(
        [t for g in grams for t in (g[0], g[2])],
        (ALTERNATE, ADJACENT, ALTERNATE, ALTERNATE), x_ref, e_ref,
    )
    lasts = []
    for at, (near, cross, far) in enumerate(grams):
        (near_q, near_t), (far_q, far_t) = turns[2 * at:2 * at + 2]
        zero = jnp.zeros((BS, LANES), F32)
        if at == 0:
            kept = lax.rem(columns, 2) == 0
            near_q = jnp.where(kept, near_q, 0.0)
            far_q = jnp.where(kept, 0.0, pltpu.roll(far_q, BS, 1))
            near_t = jnp.concatenate([near_t[:BS], zero, near_t[64:96], zero], axis=0)
            far_t = jnp.concatenate([zero, far_t[:BS], zero, far_t[64:96]], axis=0)
        else:
            kept = columns == 1
            near_q = jnp.where(kept, pltpu.roll(near_q, LANES - BS, 1), 0.0)
            far_q = jnp.where(kept, 0.0, far_q)
            near_t = jnp.concatenate([zero, near_t[64:96], zero, zero], axis=0)
            far_t = jnp.concatenate([far_t[:BS], zero, far_t[64:]], axis=0)
        q = split(jnp.concatenate([near_q, far_q], axis=0))
        t = jnp.concatenate([near_t, far_t], axis=1)
        gram = jnp.concatenate(
            [jnp.concatenate([near, cross], axis=1), jnp.concatenate([cross.T, far], axis=1)], axis=0
        )
        lasts.append(dot3(t, dot3(gram, q)))
        weights[at] = dot3(weights[at], q)
    turns = cayley(lasts, (ADJACENT, OUTSIDE), x_ref, e_ref)
    core = lax.rem(lax.axis_index("col"), 2)
    block = block_of((2 * LANES, 2 * LANES), 1)
    block = jnp.where(core == 0, block, 7 - block)
    source = pair_ids(block, (7, 4, 3, 2, 6, 5, 0, 1))
    row = lax.broadcasted_iota(jnp.int32, (2 * LANES, 2 * LANES), 0)
    lane = lax.broadcasted_iota(jnp.int32, (2 * LANES, 2 * LANES), 1)
    place = (row == source * BS + lane % BS).astype(BF16)
    placed = []
    for at, (q, _) in enumerate(turns):
        spot = place[at * LANES:(at + 1) * LANES]
        qh, ql = split(q)
        placed.append((dot1(qh, spot).astype(BF16), dot1(ql, spot).astype(BF16)))
    e_rows = dot3(weights[0], placed[0])
    o_rows = dot3(weights[1], placed[1])
    total = jnp.concatenate(
        [
            e_rows[:2 * LANES],
            o_rows[:2 * LANES],
            e_rows[2 * LANES:] + o_rows[2 * LANES:],
        ],
        axis=0,
    )
    w_high, w_low = split(total)
    w_ref[0] = w_high
    w_ref[1] = w_low

    def strip(step, _):
        here = pl.ds(pl.multiple_of(step * STRIP, STRIP), STRIP)
        high = jnp.concatenate([high_ref[t, here, :] for t in TILE_ORDER], axis=1)
        low = jnp.concatenate([low_ref[t, here, :] for t in TILE_ORDER], axis=1)
        stage[here, :] = dot1(high, w_ref[0]) + (dot1(high, w_ref[1]) + dot1(low, w_ref[0]))
        pltpu.make_async_copy(stage.at[here, :], out_ref.at[here, :], out_sem.at[step]).start()
        return 0

    count = high_ref.shape[1] // STRIP
    lax.fori_loop(0, count, strip, 0)
    for step in range(count):
        here = pl.ds(step * STRIP, STRIP)
        pltpu.make_async_copy(stage.at[here, :], out_ref.at[here, :], out_sem.at[step]).wait()


def shards(left_factor, right_factor, weights, plan):
    vmem = pl.BlockSpec(memory_space=pltpu.VMEM)
    dma = pltpu.SemaphoreType.DMA
    high, low, gram = pl.pallas_call(
        gather_kernel,
        name="gather_and_gram",
        out_shape=(
            jax.ShapeDtypeStruct((5, ROWS, LANES), BF16),
            jax.ShapeDtypeStruct((5, ROWS, LANES), BF16),
            jax.ShapeDtypeStruct((GRAM_ROWS, LANES), F32),
        ),
        in_specs=[pl.BlockSpec(memory_space=pltpu.HBM)] * 4,
        out_specs=(vmem, vmem, vmem),
        scratch_shapes=[
            pltpu.VMEM((ROWS, 64), BF16),
            pltpu.VMEM((1, 64), F32),
            pltpu.VMEM((DEPTH, 2 * LANES), BF16),
            pltpu.SMEM((4, 256), jnp.int32),
            pltpu.VMEM((ROWS, LANES), BF16),
            pltpu.VMEM((ROWS, LANES), BF16),
            pltpu.VMEM((PACKED, LANES), BF16),
            pltpu.VMEM((16, HALF, LANES), BF16),
            pltpu.VMEM((8, 2 * DEPTH, LANES), BF16),
            pltpu.VMEM((8, PACKED, LANES), BF16),
            pltpu.VMEM((8, 2 * DEPTH, LANES), BF16),
            pltpu.VMEM((8, PACKED, LANES), BF16),
            pltpu.VMEM((8, DEPTH, 8 * LANES), BF16),
            pltpu.VMEM((HALF, 8 * LANES), F32),
            pltpu.VMEM((5, HALF, LANES), BF16),
            pltpu.VMEM((5, HALF, LANES), BF16),
            pltpu.VMEM((GRAM_ROWS, LANES), F32),
            pltpu.VMEM((GRAM_ROWS, LANES), F32),
            pltpu.VMEM((GRAM_ROWS, LANES), F32),
            pltpu.VMEM((2, 7, 64, LANES), F32),
        ] + [dma((count,)) for count in (4, 110, 2, 5, 4, 2, 16, 8, 2, 8, 8, 8, 8, 14, 14)],
        compiler_params=pltpu.CompilerParams(
            collective_id=0, has_side_effects=True, vmem_limit_bytes=VMEM_LIMIT
        ),
    )(left_factor, weights, right_factor, plan)
    return pl.pallas_call(
        rounds_kernel,
        name="rounds",
        out_shape=jax.ShapeDtypeStruct((ROWS, 2 * LANES), F32),
        in_specs=[vmem, vmem, vmem],
        out_specs=pl.BlockSpec(memory_space=pltpu.HBM),
        scratch_shapes=[
            pltpu.VMEM((5, 2 * LANES, 2 * LANES), F32),
            pltpu.VMEM((5, 2 * LANES, 2 * LANES), F32),
            pltpu.VMEM((2, 5 * LANES, 2 * LANES), BF16),
            pltpu.VMEM((ROWS, 2 * LANES), F32),
            dma((ROWS // STRIP,)),
        ],
        compiler_params=pltpu.CompilerParams(vmem_limit_bytes=VMEM_LIMIT),
    )(gram, high, low)


def solution(mesh):
    in_specs = (P("row", "col"), P("row", "col"), P("col"), P())
    out_specs = P("row", "col")
    return jax.shard_map(shards, mesh=mesh, in_specs=in_specs, out_specs=out_specs, check_vma=False)
```

```python
import functools

import jax
import jax.numpy as jnp
from jax import lax
from jax.experimental import pallas as pl
from jax.experimental.pallas import tpu as pltpu
from jax.sharding import PartitionSpec as P

BS = 32
LANES = 128
EPSILON = 1e-06
TOLERANCE = 1e-04
STRIP = 256
TILE_ORDER = (0, 2, 1, 3, 4)
ALTERNATE = (0, 1, 0, 1)
ADJACENT = (0, 0, 1, 1)
OUTSIDE = (0, 1, 1, 0)
BF16 = jnp.bfloat16
F32 = jnp.float32
MESH = pl.DeviceIdType.MESH
ROWS = 1024
HALF = 512
QUARTER = 256
DEPTH = 256
PACKED = 384
SHARE = 96
GRAM_ROWS = 8 * SHARE
VECTORS = 5 * LANES + 64
GROUPS = ((0, 64), (512, 32))
VMEM_LIMIT = 48 * 1024 * 1024


def gather_kernel(
    left_hbm, weights_hbm, right_hbm, plan_hbm,
    high_ref, low_ref, gram_ref,
    left_ref, weights_ref, right_ref, plan_ref,
    own_buf, sib_buf, fold_buf, s_buf, r_own, r_out, sib_own, sib_out,
    wide, theta, high_sib, low_sib, part, part_sib, part_in, landed,
    in_sem, send_sem, out_sem, sib_sem, z_sem, zo_sem, y_sem, yo_sem,
    zr_sem, x_sem, xo_sem, sr_sem, so_sem, part_sem, full_sem,
):
    row = lax.axis_index("row")
    col = lax.axis_index("col")
    x, zl = row // 2, lax.rem(row, 2)
    core = lax.rem(col, 2)
    chip = col // 2
    y, zh = chip // 4, lax.rem(chip, 4)
    sibling = {"row": row, "col": col + 1 - 2 * core}
    outer_col = col - 1 + 2 * core
    at_end = jnp.logical_or(outer_col < 0, outer_col > 31)
    outer = {"row": row, "col": outer_col}

    def chip_at(yy, zz):
        return lax.rem(yy, 4) * 4 + lax.rem(zz, 4)

    def along(yy, zz):
        return {"row": row, "col": chip_at(yy, zz) * 2 + core}

    def row_at(xx, zz):
        return lax.rem(xx, 4) * 2 + zz

    def across(xx, zz):
        return {"row": row_at(xx, zz), "col": col}

    sent = []

    def send(src, dst, sem, device):
        copy = pltpu.make_async_remote_copy(
            src_ref=src, dst_ref=dst, send_sem=send_sem.at[len(sent)], recv_sem=sem,
            device_id=device, device_id_type=MESH,
        )
        copy.start()
        sent.append(copy)

    def arrive(ref, sem):
        pltpu.make_async_copy(ref, ref, sem).wait()

    inputs = [
        pltpu.make_async_copy(src, dst, in_sem.at[at])
        for at, (src, dst) in enumerate((
            (left_hbm, left_ref), (weights_hbm, weights_ref.at[0]),
            (right_hbm, right_ref), (plan_hbm, plan_ref),
        ))
    ]
    for copy in inputs:
        copy.start()

    barrier = pltpu.get_barrier_semaphore()
    peers = [sibling, along(y, zh + 1), along(y, zh + 3), along(y + 1, zh), along(y + 3, zh)]
    for step in range(1, 8):
        peers.append({"row": lax.rem(row + step, 8), "col": col})
    for peer in peers:
        pl.semaphore_signal(barrier, inc=1, device_id=peer, device_id_type=MESH)

    @pl.when(jnp.logical_not(at_end))
    def _():
        pl.semaphore_signal(barrier, inc=1, device_id=outer, device_id_type=MESH)

    inputs[0].wait()
    inputs[1].wait()
    scaled = (left_ref[...].astype(F32) * weights_ref[...]).astype(BF16)
    own_buf[...] = jnp.concatenate([scaled, scaled], axis=1)

    pl.semaphore_wait(barrier, jnp.where(at_end, 12, 13))

    half = pl.multiple_of(core * HALF, HALF)
    other = pl.multiple_of(HALF - core * HALF, HALF)
    send(own_buf.at[pl.ds(other, HALF)], sib_buf.at[pl.ds(other, HALF)], sib_sem.at[0], sibling)

    inputs[2].wait()
    inputs[3].wait()
    ids = []
    for slot in (0, 4, 1, 5, 2, 6, 3, 7):
        there = jnp.where(core == 0, slot, 7 - slot)
        ids.append(plan_ref[0, col * 8 + there] - col * 8)
    block = lax.broadcasted_iota(jnp.int32, (DEPTH, 256), 1) // BS
    source = jnp.zeros((DEPTH, 256), jnp.int32)
    for at, value in enumerate(ids):
        source = jnp.where(block == at, value, source)
    column = lax.broadcasted_iota(jnp.int32, (DEPTH, 256), 1)
    place = lax.broadcasted_iota(jnp.int32, (DEPTH, 256), 0) == source * BS + lax.rem(column, BS)
    ordered = jnp.dot(right_ref[...], place.astype(BF16), preferred_element_type=F32)
    lane = lax.broadcasted_iota(jnp.int32, (LANES, LANES), 1)
    odd = lax.rem(lane // BS, 2) == 1
    tail = ordered[:, LANES:]
    folded = jnp.where(odd, pltpu.roll(tail[LANES:], BS, 1), tail[:LANES]).astype(BF16)
    first = ordered[:, :LANES].astype(BF16)
    r_own[row] = jnp.concatenate([first, tail.astype(BF16)], axis=0)
    own_fold = jnp.concatenate([first, folded], axis=0)
    fold_buf[...] = own_fold

    def rows_of(q, which):
        return s_buf.at[q, pl.ds(which * QUARTER, QUARTER), :]

    to_outer = pltpu.make_async_remote_copy(
        src_ref=fold_buf, dst_ref=r_out.at[row],
        send_sem=out_sem.at[0], recv_sem=out_sem.at[1], device_id=outer, device_id_type=MESH,
    )

    @pl.when(jnp.logical_not(at_end))
    def _():
        to_outer.start()

    @pl.when(at_end)
    def _():
        r_out[row] = own_fold

    def part_of(buf, r, which):
        size = buf.shape[1] // 2
        return buf.at[r, pl.ds(which * size, size), :]

    def x_sends(buf, zz, at):
        r = row_at(x, zz)
        send(buf.at[r], buf.at[r], x_sem.at[2 * at], across(x + 1, zl))
        send(buf.at[r], buf.at[r], x_sem.at[2 * at + 1], across(x + 3, zl))

    def share_own(r, at):
        send(r_own.at[r], sib_own.at[r], sr_sem.at[at], sibling)

    def share_out(r, at):
        send(r_out.at[r], sib_out.at[r], so_sem.at[at], sibling)

    def x_arrive(buf, zz, at, share, first):
        for which, step in ((0, 3), (1, 1)):
            r = row_at(x + step, zz)
            arrive(buf.at[r], x_sem.at[2 * at + which])
            piece = part_of(buf, r, which)
            send(piece, piece, xo_sem.at[2 * at + which], across(x + 4 - step, zl))
            share(r, first + which)

    def x_opposite(buf, zz, at, share, first):
        r = row_at(x + 2, zz)
        for which in range(2):
            arrive(part_of(buf, r, which), xo_sem.at[2 * at + which])
        share(r, first)

    def y_sends(zz, at, which):
        ref = rows_of(chip_at(y, zz), which)
        send(ref, ref, y_sem.at[4 * at + which], along(y + 1, zh))
        send(ref, ref, y_sem.at[4 * at + 2 + which], along(y + 3, zh))

    def y_arrive(zz, at):
        for which in range(2):
            ref = rows_of(chip_at(y + 3, zz), which)
            arrive(ref, y_sem.at[4 * at + which])
            if which == 0:
                send(ref, ref, yo_sem.at[2 * at], along(y + 1, zh))
            ref = rows_of(chip_at(y + 1, zz), which)
            arrive(ref, y_sem.at[4 * at + 2 + which])
            if which == 1:
                send(ref, ref, yo_sem.at[2 * at + 1], along(y + 3, zh))

    def y_opposite(zz, at):
        for which in range(2):
            arrive(rows_of(chip_at(y + 2, zz), which), yo_sem.at[2 * at + which])

    def z_sends(which):
        ref = rows_of(chip, which)
        send(ref, ref, z_sem.at[which], along(y, zh + 1))
        send(ref, ref, z_sem.at[2 + which], along(y, zh + 3))

    def z_arrive(which):
        ref = rows_of(chip_at(y, zh + 3), which)
        arrive(ref, z_sem.at[which])
        if which == 0:
            send(ref, ref, zo_sem.at[0], along(y, zh + 1))
        y_sends(zh + 3, 1, which)
        ref = rows_of(chip_at(y, zh + 1), which)
        arrive(ref, z_sem.at[2 + which])
        if which == 1:
            send(ref, ref, zo_sem.at[1], along(y, zh + 3))
        y_sends(zh + 1, 2, which)

    x_sends(r_own, zl, 0)

    arrive(sib_buf.at[pl.ds(half, HALF)], sib_sem.at[0])
    mine = (lax.broadcasted_iota(jnp.int32, (HALF, LANES), 1) // 64) == core
    here = pl.ds(half, HALF)
    s_buf[chip] = jnp.where(mine, own_buf[here, :], sib_buf[here, :])
    z_sends(0)
    z_sends(1)
    y_sends(zh, 0, 0)
    y_sends(zh, 0, 1)
    share_own(row, 0)

    @pl.when(jnp.logical_not(at_end))
    def _():
        arrive(r_out.at[row], out_sem.at[1])

    x_sends(r_out, zl, 1)
    share_out(row, 0)

    z_arrive(0)
    send(r_own.at[row], r_own.at[row], zr_sem.at[0], across(x, 1 - zl))
    y_arrive(zh, 0)
    x_arrive(r_own, zl, 0, share_own, 2)
    z_arrive(1)
    send(r_out.at[row], r_out.at[row], zr_sem.at[1], across(x, 1 - zl))
    x_opposite(r_own, zl, 0, share_own, 4)
    x_arrive(r_out, zl, 1, share_out, 2)

    r = row_at(x, 1 - zl)
    arrive(r_own.at[r], zr_sem.at[0])
    x_sends(r_own, 1 - zl, 2)
    share_own(r, 1)

    for which in range(2):
        arrive(rows_of(chip_at(y, zh + 2), which), zo_sem.at[which])
        y_sends(zh + 2, 3, which)

    arrive(r_out.at[r], zr_sem.at[1])
    x_sends(r_out, 1 - zl, 3)
    share_out(r, 1)

    def mixed_tile(far, out):
        unfolded = pltpu.roll(out.astype(F32), LANES - BS, 1).astype(BF16)
        return jnp.concatenate(
            [jnp.where(odd, far[:LANES], out), jnp.where(odd, far[LANES:], unfolded)], axis=0
        )

    def window(r):
        return jnp.concatenate(
            [
                r_own[r, :DEPTH], r_own[r, DEPTH:], sib_own[r, DEPTH:], r_out[r, :DEPTH],
                mixed_tile(sib_own[r, :DEPTH], r_out[r, DEPTH:]),
                sib_own[r, :DEPTH], sib_out[r, :DEPTH],
                mixed_tile(r_own[r, :DEPTH], sib_out[r, DEPTH:]),
            ],
            axis=1,
        )

    def build(xx, at):
        arrive(sib_own.at[0], sr_sem.at[at[0]])
        arrive(sib_out.at[0], so_sem.at[at[0]])
        arrive(sib_own.at[0], sr_sem.at[at[1]])
        arrive(sib_out.at[0], so_sem.at[at[1]])
        for zz in range(2):
            r = row_at(xx, zz)
            wide[r] = window(r)

    def add_up(blocks, last=False):
        blocks = [lax.rem(yy, 4) for yy in blocks]

        def strip(step, _):
            here = pl.ds(pl.multiple_of(step * STRIP, STRIP), STRIP)
            rows = jnp.concatenate(
                [s_buf[yy * 4 + t, here, :] for yy in blocks for t in range(4)], axis=1
            )
            weights = jnp.concatenate([wide[yy * 2 + t] for yy in blocks for t in range(2)], axis=0)
            value = jnp.dot(rows, weights, preferred_element_type=F32)
            if not last:
                theta[here, :] = value
                return 0
            value = theta[here, :] + value
            high = value.astype(BF16)
            low = (value - high.astype(F32)).astype(BF16)
            there = pl.ds(pl.multiple_of(half + step * STRIP, STRIP), STRIP)
            for t, source in enumerate((0, 1, 2, 3, 4)):
                lanes = slice(source * LANES, (source + 1) * LANES)
                high_ref[t, there, :] = high[:, lanes]
                low_ref[t, there, :] = low[:, lanes]
            for t, source in enumerate((5, 2, 1, 6, 7)):
                lanes = slice(source * LANES, (source + 1) * LANES)
                high_sib[t, here, :] = high[:, lanes]
                low_sib[t, here, :] = low[:, lanes]
            return 0

        lax.fori_loop(0, HALF // STRIP, strip, 0)

    y_arrive(zh + 3, 1)
    y_arrive(zh + 1, 2)
    x_opposite(r_out, zl, 1, share_out, 4)
    x_arrive(r_own, 1 - zl, 2, share_own, 5)
    x_arrive(r_out, 1 - zl, 3, share_out, 5)
    y_arrive(zh + 2, 3)
    build(x, (0, 1))
    x_opposite(r_own, 1 - zl, 2, share_own, 7)
    build(x + 3, (2, 5))
    build(x + 1, (3, 6))
    y_opposite(zh, 0)
    far_x = lax.rem(x + 2, 4)
    late = jnp.where(far_x == y, y, jnp.where(far_x == lax.rem(y + 1, 4), y + 1, y + 3))
    early = jnp.where(late == y, y + 1, y), jnp.where(late == y + 3, y + 1, y + 3)
    add_up(early)
    x_opposite(r_out, 1 - zl, 3, share_out, 7)
    build(x + 2, (4, 7))
    y_opposite(zh + 3, 1)
    y_opposite(zh + 1, 2)
    y_opposite(zh + 2, 3)
    add_up((late, y + 2), last=True)

    row_ids = lax.broadcasted_iota(jnp.int32, (LANES, LANES), 0)
    upper = row_ids < lane
    same = lax.rem(row_ids // BS + lane // BS, 2) == 0
    diagonal = row_ids == lane

    def gram_of(high_at, low_at, out):
        def gram(a, others):
            high = jnp.concatenate([high_at(t) for t in others], axis=1)
            low = jnp.concatenate([low_at(t) for t in others], axis=1)

            def over_rows(p, q):
                return lax.dot_general(p, q, (((0,), (0,)), ((), ())), preferred_element_type=F32)

            width = len(others) * LANES
            first = over_rows(high_at(a), jnp.concatenate([high, low], axis=1))
            return first[:, :width] + (first[:, width:] + over_rows(low_at(a), high))

        saved = []

        def put(at, value):
            out[at * LANES:(at + 1) * LANES, :] = value

        def segments(tile):
            kept = jnp.sum(jnp.where(diagonal, tile, 0.0), axis=0, keepdims=True)
            return [kept] + [pltpu.roll(kept, LANES - BS * k, 1) for k in range(1, 4)]

        def near():
            e_own = gram(0, (0, 2, 4))
            o_own = gram(1, (1, 3, 4))
            put(0, jnp.where(upper, e_own[:, :LANES], o_own[:, :LANES]))
            put(1, e_own[:, LANES:2 * LANES])
            put(2, o_own[:, LANES:2 * LANES])
            put(3, jnp.where(odd, o_own[:, 2 * LANES:], e_own[:, 2 * LANES:]))
            saved.extend(segments(e_own[:, :LANES]))

        def far():
            e_far = gram(2, (2, 4))
            o_far = gram(3, (3, 4))
            put(4, jnp.where(upper, e_far[:, :LANES], o_far[:, :LANES]))
            put(5, jnp.where(same, gram(4, (4,)), jnp.where(odd, o_far[:, LANES:], e_far[:, LANES:])))
            packed = jnp.concatenate(saved + segments(e_far[:, :LANES]), axis=0)
            there = slice(VECTORS, VECTORS + 8)
            out[there, :] = jnp.where(lane[:8] < BS, packed, out[there, :])

        return near, far

    gathered = len(sent)
    for_sib = gram_of(lambda t: high_sib[t], lambda t: low_sib[t], part_sib)
    for_own = gram_of(lambda t: high_ref[t, here, :], lambda t: low_ref[t, here, :], part)

    def shares(group, owner):
        start, size = GROUPS[group]
        return pl.ds(pl.multiple_of(start + owner * size, 8), size)

    def group_rows(group):
        start, size = GROUPS[group]
        return pl.ds(start, 8 * size)

    def peer_at(step):
        return lax.rem(row + step, 8)

    for group in range(2):
        for_sib[group]()
        rows = group_rows(group)
        send(part_sib.at[rows, :], part_in.at[rows, :], sib_sem.at[1 + group], sibling)
        for_own[group]()
        arrive(part_in.at[rows, :], sib_sem.at[1 + group])
        part[rows, :] = part[rows, :] + part_in[rows, :]
        size = GROUPS[group][1]
        for step in range(1, 8):
            send(
                part.at[shares(group, peer_at(step)), :], landed.at[group, step - 1, pl.ds(0, size), :],
                part_sem.at[7 * group + step - 1], {"row": peer_at(step), "col": col},
            )
    send(high_sib, high_ref.at[:, here, :], sib_sem.at[3], sibling)
    send(low_sib, low_ref.at[:, here, :], sib_sem.at[4], sibling)
    for copy in sent[:gathered]:
        copy.wait_send()
    summed = len(sent)
    for group in range(2):
        size = GROUPS[group][1]
        mine = shares(group, row)
        total = part[mine, :]
        for step in range(1, 8):
            arrive(landed.at[group, step - 1, pl.ds(0, size), :], part_sem.at[7 * group + step - 1])
            total = total + landed[group, step - 1, :size]
        gram_ref[mine, :] = total
        for step in range(1, 8):
            send(
                gram_ref.at[mine, :], gram_ref.at[mine, :], full_sem.at[7 * group + step - 1],
                {"row": peer_at(step), "col": col},
            )

    @pl.when(jnp.logical_not(at_end))
    def _():
        to_outer.wait_send()

    for copy in sent[gathered:summed]:
        copy.wait_send()
    arrive(high_sib, sib_sem.at[3])
    arrive(low_sib, sib_sem.at[4])
    for group in range(2):
        for step in range(1, 8):
            arrive(gram_ref.at[shares(group, 0), :], full_sem.at[7 * group + step - 1])
    for copy in sent[summed:]:
        copy.wait_send()


def split(value):
    high = value.astype(BF16)
    return high, (value - high.astype(F32)).astype(BF16)


def dot1(a, b):
    return jnp.dot(a, b, preferred_element_type=F32)


def dot3(a, b):
    ah, al = a if isinstance(a, tuple) else split(a)
    bh, bl = b if isinstance(b, tuple) else split(b)
    return dot1(ah, bh) + (dot1(ah, bl) + dot1(al, bh))


def block_of(shape, axis):
    return lax.broadcasted_iota(jnp.int32, shape, axis) // BS


def identity(n):
    shape = (n, n)
    rows = lax.broadcasted_iota(jnp.int32, shape, 0)
    return (rows == lax.broadcasted_iota(jnp.int32, shape, 1)).astype(F32)


def pair_ids(blocks, ids):
    out = jnp.full(blocks.shape, ids[0], jnp.int32)
    for at, value in enumerate(ids[1:], 1):
        out = jnp.where(blocks == at, value, out)
    return out


def pair_mask(n, ids):
    return pair_ids(block_of((n, n), 0), ids) == pair_ids(block_of((n, n), 1), ids)


def angles_of(gram, eye, mask):
    kept = gram * eye
    across = jnp.sum(kept, axis=0, keepdims=True)
    down = jnp.sum(kept, axis=1, keepdims=True)
    spread = across - down
    middle = 0.5 * (across + down)
    angles = gram * spread / (2.0 * (spread * spread + middle * middle + EPSILON))
    return jnp.where(mask, jnp.clip(angles, -0.25, 0.25), 0.0)


def cayley(grams, ids, x_ref, e_ref):
    n = grams[0].shape[0]
    eye = identity(n)
    masks = {each: pair_mask(n, each) for each in set(ids)}
    angles = [split(angles_of(g, eye, masks[each])) for g, each in zip(grams, ids)]
    squares = [dot3(a, a) for a in angles]
    sums = []
    for s in squares:
        sums.append(jnp.sum(jnp.abs(s), axis=0, keepdims=True))
    bound = jnp.max(functools.reduce(jnp.maximum, sums))
    scale = 2.0 / (2.0 + bound)
    rho = bound * scale * 0.5
    lift = 2.0 / (2.0 - rho * rho)
    for at, s in enumerate(squares):
        e = eye - scale * (eye - s)
        e_ref[at, :n, :n] = e
        x_ref[at, :n, :n] = (scale * lift) * (eye + e)

    def unfinished(state):
        return state[0] > TOLERANCE

    def refine(state):
        left, grow = state
        next_grow = 2.0 / (2.0 - left * left)
        for at in range(len(grams)):
            e = split(e_ref[at, :n, :n])
            e = eye - grow * (eye - dot3(e, e))
            x = x_ref[at, :n, :n]
            e_ref[at, :n, :n] = e
            x_ref[at, :n, :n] = next_grow * (x + dot3(e, x))
        return left * left * 0.5 * next_grow, next_grow

    lax.while_loop(unfinished, refine, (rho * rho * 0.5 * lift, lift))
    turns = []
    for at, a in enumerate(angles):
        x = x_ref[at, :n, :n]
        odd = 2.0 * dot3(a, x)
        even = 2.0 * x - eye
        turns.append((even + odd, even - odd))
    return turns


def swap_middle(a, b, axis):
    if axis == 0:
        return (
            jnp.concatenate([a[:64], b[BS:64], a[96:]], axis=0),
            jnp.concatenate([b[:BS], a[64:96], b[64:]], axis=0),
        )
    block = block_of(a.shape, 1)
    return (
        jnp.where(block == 2, pltpu.roll(b, BS, 1), a),
        jnp.where(block == 1, pltpu.roll(a, LANES - BS, 1), b),
    )


def swap_odd(a, b, axis):
    if axis == 0:
        return (
            jnp.concatenate([a[:BS], b[BS:64], a[64:96], b[96:]], axis=0),
            jnp.concatenate([b[:BS], a[BS:64], b[64:96], a[96:]], axis=0),
        )
    odd = lax.rem(block_of(a.shape, 1), 2) == 1
    return jnp.where(odd, b, a), jnp.where(odd, a, b)


def swap_ends(a, b, axis):
    if axis == 0:
        return (
            jnp.concatenate([a[:96], b[:BS]], axis=0),
            jnp.concatenate([a[96:], b[BS:]], axis=0),
        )
    block = block_of(a.shape, 1)
    return (
        jnp.where(block == 3, pltpu.roll(b, 96, 1), a),
        jnp.where(block == 0, pltpu.roll(a, BS, 1), b),
    )


def regroup(gram, swap):
    near, cross, far = gram
    near, cross_top = swap(near, cross, 1)
    cross_bottom, far = swap(cross.T, far, 1)
    near, _ = swap(near, cross_bottom, 0)
    cross, far = swap(cross_top, far, 0)
    return near, cross, far


def rounds_kernel(g_ref, high_ref, low_ref, out_ref, x_ref, e_ref, w_ref, stage, out_sem):
    def tile(at):
        return g_ref[at * LANES:(at + 1) * LANES, :]

    shape = (LANES, LANES)
    row_ids = lax.broadcasted_iota(jnp.int32, shape, 0)
    lane_ids = lax.broadcasted_iota(jnp.int32, shape, 1)

    def segment(at):
        return g_ref[VECTORS + at:VECTORS + at + 1, :]

    def both(packed, vector):
        turned = packed.T
        diagonal = row_ids == lane_ids
        upper = jnp.where(row_ids < lane_ids, packed, turned)
        kept = segment(4 * vector)
        for k in range(1, 4):
            kept = jnp.where(lane_ids[:1] // BS == k, pltpu.roll(segment(4 * vector + k), BS * k, 1), kept)
        upper = jnp.where(diagonal, kept, upper)
        return upper, jnp.where(row_ids < lane_ids, turned, packed)

    own_e, own_o = both(tile(0), 0)
    far_e, far_o = both(tile(4), 1)
    mixed = jnp.where(row_ids < lane_ids, tile(5), tile(5).T)
    turns = cayley([own_e, far_e, own_o, far_o, mixed], (ALTERNATE,) * 5, x_ref, e_ref)
    columns = block_of((LANES, LANES), 1)
    rows = block_of((LANES, LANES), 0)
    chains = []
    for own, far, own_turn, far_turn, base, moved in (
        (own_e, far_e, turns[0], turns[1], 1, 2),
        (own_o, far_o, turns[2], turns[3], 2, 1),
    ):
        near, own_mixed, far_mixed = tile(base), tile(3), tile(5)
        mixed_turn = turns[4]
        far_q = jnp.where(columns == moved, 0.0, far_turn[0])
        far_t = jnp.where(rows == moved, 0.0, far_turn[1])
        mixed_q = jnp.where(columns == moved, mixed_turn[0], 0.0)
        mixed_t = jnp.where(rows == moved, mixed_turn[1], 0.0)
        tail_q = split(jnp.concatenate([far_q, mixed_q], axis=0))
        tail_t = split(jnp.concatenate([far_t, mixed_t], axis=1))
        own_q = split(own_turn[0])
        own_t = split(own_turn[1])
        head = jnp.concatenate([near, own_mixed], axis=1)
        body = jnp.concatenate(
            [
                jnp.concatenate([far, far_mixed], axis=1),
                jnp.concatenate([far_mixed.T, mixed], axis=1),
            ],
            axis=0,
        )
        corner = dot3(own_t, dot3(own, own_q))
        side = dot3(own_t, dot3(head, tail_q))
        rest = dot3(tail_t, dot3(body, tail_q))
        chains.append((regroup((corner, side, rest), swap_middle), own_q, tail_q))
    turns = cayley([t for c in chains for t in (c[0][0], c[0][2])], (OUTSIDE,) * 4, x_ref, e_ref)
    grams = []
    weights = []
    for at, ((near, cross, far), own_q, tail_q) in enumerate(chains):
        (near_q, near_t), (far_q, far_t) = turns[2 * at:2 * at + 2]
        zero = jnp.zeros((BS, LANES), F32)
        top = jnp.concatenate(
            [
                jnp.concatenate([near_q[:64], zero, near_q[96:]], axis=0),
                jnp.concatenate([zero, zero, far_q[BS:64], zero], axis=0),
            ],
            axis=1,
        )
        bottom = jnp.concatenate(
            [
                jnp.concatenate([zero, near_q[64:96], zero, zero], axis=0),
                jnp.concatenate([far_q[:BS], zero, far_q[64:]], axis=0),
            ],
            axis=1,
        )
        spread = jnp.concatenate([dot3(own_q, top), dot3(tail_q, bottom)], axis=0)
        swap = swap_odd if at == 0 else swap_ends
        weights.append(jnp.concatenate(swap(spread[:, :LANES], spread[:, LANES:], 1), axis=1))
        near_q, near_t, far_q, far_t = split(near_q), split(near_t), split(far_q), split(far_t)
        turned = (
            dot3(near_t, dot3(near, near_q)),
            dot3(near_t, dot3(cross, far_q)),
            dot3(far_t, dot3(far, far_q)),
        )
        grams.append(regroup(turned, swap))
    turns = cayley(
        [t for g in grams for t in (g[0], g[2])],
        (ALTERNATE, ADJACENT, ALTERNATE, ALTERNATE), x_ref, e_ref,
    )
    lasts = []
    for at, (near, cross, far) in enumerate(grams):
        (near_q, near_t), (far_q, far_t) = turns[2 * at:2 * at + 2]
        zero = jnp.zeros((BS, LANES), F32)
        if at == 0:
            kept = lax.rem(columns, 2) == 0
            near_q = jnp.where(kept, near_q, 0.0)
            far_q = jnp.where(kept, 0.0, pltpu.roll(far_q, BS, 1))
            near_t = jnp.concatenate([near_t[:BS], zero, near_t[64:96], zero], axis=0)
            far_t = jnp.concatenate([zero, far_t[:BS], zero, far_t[64:96]], axis=0)
        else:
            kept = columns == 1
            near_q = jnp.where(kept, pltpu.roll(near_q, LANES - BS, 1), 0.0)
            far_q = jnp.where(kept, 0.0, far_q)
            near_t = jnp.concatenate([zero, near_t[64:96], zero, zero], axis=0)
            far_t = jnp.concatenate([far_t[:BS], zero, far_t[64:]], axis=0)
        q = split(jnp.concatenate([near_q, far_q], axis=0))
        t = jnp.concatenate([near_t, far_t], axis=1)
        gram = jnp.concatenate(
            [jnp.concatenate([near, cross], axis=1), jnp.concatenate([cross.T, far], axis=1)], axis=0
        )
        lasts.append(dot3(t, dot3(gram, q)))
        weights[at] = dot3(weights[at], q)
    turns = cayley(lasts, (ADJACENT, OUTSIDE), x_ref, e_ref)
    core = lax.rem(lax.axis_index("col"), 2)
    block = block_of((2 * LANES, 2 * LANES), 1)
    block = jnp.where(core == 0, block, 7 - block)
    source = pair_ids(block, (7, 4, 3, 2, 6, 5, 0, 1))
    row = lax.broadcasted_iota(jnp.int32, (2 * LANES, 2 * LANES), 0)
    lane = lax.broadcasted_iota(jnp.int32, (2 * LANES, 2 * LANES), 1)
    place = (row == source * BS + lane % BS).astype(BF16)
    placed = []
    for at, (q, _) in enumerate(turns):
        spot = place[at * LANES:(at + 1) * LANES]
        qh, ql = split(q)
        placed.append((dot1(qh, spot).astype(BF16), dot1(ql, spot).astype(BF16)))
    e_rows = dot3(weights[0], placed[0])
    o_rows = dot3(weights[1], placed[1])
    total = jnp.concatenate(
        [
            e_rows[:2 * LANES],
            o_rows[:2 * LANES],
            e_rows[2 * LANES:] + o_rows[2 * LANES:],
        ],
        axis=0,
    )
    w_high, w_low = split(total)
    w_ref[0] = w_high
    w_ref[1] = w_low

    def strip(step, _):
        here = pl.ds(pl.multiple_of(step * STRIP, STRIP), STRIP)
        high = jnp.concatenate([high_ref[t, here, :] for t in TILE_ORDER], axis=1)
        low = jnp.concatenate([low_ref[t, here, :] for t in TILE_ORDER], axis=1)
        stage[here, :] = dot1(high, w_ref[0]) + (dot1(high, w_ref[1]) + dot1(low, w_ref[0]))
        pltpu.make_async_copy(stage.at[here, :], out_ref.at[here, :], out_sem.at[step]).start()
        return 0

    count = high_ref.shape[1] // STRIP
    lax.fori_loop(0, count, strip, 0)
    for step in range(count):
        here = pl.ds(step * STRIP, STRIP)
        pltpu.make_async_copy(stage.at[here, :], out_ref.at[here, :], out_sem.at[step]).wait()


def shards(left_factor, right_factor, weights, plan):
    vmem = pl.BlockSpec(memory_space=pltpu.VMEM)
    dma = pltpu.SemaphoreType.DMA
    high, low, gram = pl.pallas_call(
        gather_kernel,
        name="gather_and_gram",
        out_shape=(
            jax.ShapeDtypeStruct((5, ROWS, LANES), BF16),
            jax.ShapeDtypeStruct((5, ROWS, LANES), BF16),
            jax.ShapeDtypeStruct((GRAM_ROWS, LANES), F32),
        ),
        in_specs=[pl.BlockSpec(memory_space=pltpu.HBM)] * 4,
        out_specs=(vmem, vmem, vmem),
        scratch_shapes=[
            pltpu.VMEM((ROWS, 64), BF16),
            pltpu.VMEM((1, 64), F32),
            pltpu.VMEM((DEPTH, 2 * LANES), BF16),
            pltpu.SMEM((4, 256), jnp.int32),
            pltpu.VMEM((ROWS, LANES), BF16),
            pltpu.VMEM((ROWS, LANES), BF16),
            pltpu.VMEM((PACKED, LANES), BF16),
            pltpu.VMEM((16, HALF, LANES), BF16),
            pltpu.VMEM((8, 2 * DEPTH, LANES), BF16),
            pltpu.VMEM((8, PACKED, LANES), BF16),
            pltpu.VMEM((8, 2 * DEPTH, LANES), BF16),
            pltpu.VMEM((8, PACKED, LANES), BF16),
            pltpu.VMEM((8, DEPTH, 8 * LANES), BF16),
            pltpu.VMEM((HALF, 8 * LANES), F32),
            pltpu.VMEM((5, HALF, LANES), BF16),
            pltpu.VMEM((5, HALF, LANES), BF16),
            pltpu.VMEM((GRAM_ROWS, LANES), F32),
            pltpu.VMEM((GRAM_ROWS, LANES), F32),
            pltpu.VMEM((GRAM_ROWS, LANES), F32),
            pltpu.VMEM((2, 7, 64, LANES), F32),
        ] + [dma((count,)) for count in (4, 110, 2, 5, 4, 2, 16, 8, 2, 8, 8, 8, 8, 14, 14)],
        compiler_params=pltpu.CompilerParams(
            collective_id=0, has_side_effects=True, vmem_limit_bytes=VMEM_LIMIT
        ),
    )(left_factor, weights, right_factor, plan)
    return pl.pallas_call(
        rounds_kernel,
        name="rounds",
        out_shape=jax.ShapeDtypeStruct((ROWS, 2 * LANES), F32),
        in_specs=[vmem, vmem, vmem],
        out_specs=pl.BlockSpec(memory_space=pltpu.HBM),
        scratch_shapes=[
            pltpu.VMEM((5, 2 * LANES, 2 * LANES), F32),
            pltpu.VMEM((5, 2 * LANES, 2 * LANES), F32),
            pltpu.VMEM((2, 5 * LANES, 2 * LANES), BF16),
            pltpu.VMEM((ROWS, 2 * LANES), F32),
            dma((ROWS // STRIP,)),
        ],
        compiler_params=pltpu.CompilerParams(vmem_limit_bytes=VMEM_LIMIT),
    )(gram, high, low)


def solution(mesh):
    in_specs = (P("row", "col"), P("row", "col"), P("col"), P())
    out_specs = P("row", "col")
    return jax.shard_map(shards, mesh=mesh, in_specs=in_specs, out_specs=out_specs, check_vma=False)
```

```python
import functools

import jax
import jax.numpy as jnp
from jax import lax
from jax.experimental import pallas as pl
from jax.experimental.pallas import tpu as pltpu
from jax.sharding import PartitionSpec as P

BS = 32
LANES = 128
EPSILON = 1e-06
TOLERANCE = 1e-04
STRIP = 256
TILE_ORDER = (0, 2, 1, 3, 4)
ALTERNATE = (0, 1, 0, 1)
ADJACENT = (0, 0, 1, 1)
OUTSIDE = (0, 1, 1, 0)
BF16 = jnp.bfloat16
F32 = jnp.float32
MESH = pl.DeviceIdType.MESH
ROWS = 1024
HALF = 512
QUARTER = 256
DEPTH = 256
PACKED = 384
SHARE = 96
GRAM_ROWS = 8 * SHARE
VECTORS = 5 * LANES + 64
GROUPS = ((0, 64), (512, 32))
VMEM_LIMIT = 48 * 1024 * 1024


def gather_kernel(
    left_hbm, weights_hbm, right_hbm, plan_hbm,
    high_ref, low_ref, gram_ref,
    left_ref, weights_ref, right_ref, plan_ref,
    own_buf, sib_buf, fold_buf, s_buf, r_own, r_out, sib_own, sib_out,
    wide, theta, high_sib, low_sib, part, part_sib, part_in, landed,
    in_sem, send_sem, out_sem, sib_sem, z_sem, zo_sem, y_sem, yo_sem,
    zr_sem, x_sem, xo_sem, sr_sem, so_sem, part_sem, full_sem,
):
    row = lax.axis_index("row")
    col = lax.axis_index("col")
    x, zl = row // 2, lax.rem(row, 2)
    core = lax.rem(col, 2)
    chip = col // 2
    y, zh = chip // 4, lax.rem(chip, 4)
    sibling = {"row": row, "col": col + 1 - 2 * core}
    outer_col = col - 1 + 2 * core
    at_end = jnp.logical_or(outer_col < 0, outer_col > 31)
    outer = {"row": row, "col": outer_col}

    def chip_at(yy, zz):
        return lax.rem(yy, 4) * 4 + lax.rem(zz, 4)

    def along(yy, zz):
        return {"row": row, "col": chip_at(yy, zz) * 2 + core}

    def row_at(xx, zz):
        return lax.rem(xx, 4) * 2 + zz

    def across(xx, zz):
        return {"row": row_at(xx, zz), "col": col}

    sent = []

    def send(src, dst, sem, device):
        copy = pltpu.make_async_remote_copy(
            src_ref=src, dst_ref=dst, send_sem=send_sem.at[len(sent)], recv_sem=sem,
            device_id=device, device_id_type=MESH,
        )
        copy.start()
        sent.append(copy)

    def arrive(ref, sem):
        pltpu.make_async_copy(ref, ref, sem).wait()

    inputs = [
        pltpu.make_async_copy(src, dst, in_sem.at[at])
        for at, (src, dst) in enumerate((
            (left_hbm, left_ref), (weights_hbm, weights_ref.at[0]),
            (right_hbm, right_ref), (plan_hbm, plan_ref),
        ))
    ]
    for copy in inputs:
        copy.start()

    barrier = pltpu.get_barrier_semaphore()
    peers = [sibling, along(y, zh + 1), along(y, zh + 3), along(y + 1, zh), along(y + 3, zh)]
    for step in range(1, 8):
        peers.append({"row": lax.rem(row + step, 8), "col": col})
    for peer in peers:
        pl.semaphore_signal(barrier, inc=1, device_id=peer, device_id_type=MESH)

    @pl.when(jnp.logical_not(at_end))
    def _():
        pl.semaphore_signal(barrier, inc=1, device_id=outer, device_id_type=MESH)

    inputs[0].wait()
    inputs[1].wait()
    scaled = (left_ref[...].astype(F32) * weights_ref[...]).astype(BF16)
    own_buf[...] = jnp.concatenate([scaled, scaled], axis=1)

    pl.semaphore_wait(barrier, jnp.where(at_end, 12, 13))

    half = pl.multiple_of(core * HALF, HALF)
    other = pl.multiple_of(HALF - core * HALF, HALF)
    send(own_buf.at[pl.ds(other, HALF)], sib_buf.at[pl.ds(other, HALF)], sib_sem.at[0], sibling)

    inputs[2].wait()
    inputs[3].wait()
    ids = []
    for slot in (0, 4, 1, 5, 2, 6, 3, 7):
        there = jnp.where(core == 0, slot, 7 - slot)
        ids.append(plan_ref[0, col * 8 + there] - col * 8)
    block = lax.broadcasted_iota(jnp.int32, (DEPTH, 256), 1) // BS
    source = jnp.zeros((DEPTH, 256), jnp.int32)
    for at, value in enumerate(ids):
        source = jnp.where(block == at, value, source)
    column = lax.broadcasted_iota(jnp.int32, (DEPTH, 256), 1)
    place = lax.broadcasted_iota(jnp.int32, (DEPTH, 256), 0) == source * BS + lax.rem(column, BS)
    ordered = jnp.dot(right_ref[...], place.astype(BF16), preferred_element_type=F32)
    lane = lax.broadcasted_iota(jnp.int32, (LANES, LANES), 1)
    odd = lax.rem(lane // BS, 2) == 1
    tail = ordered[:, LANES:]
    folded = jnp.where(odd, pltpu.roll(tail[LANES:], BS, 1), tail[:LANES]).astype(BF16)
    first = ordered[:, :LANES].astype(BF16)
    r_own[row] = jnp.concatenate([first, tail.astype(BF16)], axis=0)
    own_fold = jnp.concatenate([first, folded], axis=0)
    fold_buf[...] = own_fold

    def rows_of(q, which):
        return s_buf.at[q, pl.ds(which * QUARTER, QUARTER), :]

    to_outer = pltpu.make_async_remote_copy(
        src_ref=fold_buf, dst_ref=r_out.at[row],
        send_sem=out_sem.at[0], recv_sem=out_sem.at[1], device_id=outer, device_id_type=MESH,
    )

    @pl.when(jnp.logical_not(at_end))
    def _():
        to_outer.start()

    @pl.when(at_end)
    def _():
        r_out[row] = own_fold

    def part_of(buf, r, which):
        size = buf.shape[1] // 2
        return buf.at[r, pl.ds(which * size, size), :]

    def x_sends(buf, zz, at):
        r = row_at(x, zz)
        send(buf.at[r], buf.at[r], x_sem.at[2 * at], across(x + 1, zl))
        send(buf.at[r], buf.at[r], x_sem.at[2 * at + 1], across(x + 3, zl))

    def share_own(r, at):
        send(r_own.at[r], sib_own.at[r], sr_sem.at[at], sibling)

    def share_out(r, at):
        send(r_out.at[r], sib_out.at[r], so_sem.at[at], sibling)

    def x_arrive(buf, zz, at, share, first):
        for which, step in ((0, 3), (1, 1)):
            r = row_at(x + step, zz)
            arrive(buf.at[r], x_sem.at[2 * at + which])
            piece = part_of(buf, r, which)
            send(piece, piece, xo_sem.at[2 * at + which], across(x + 4 - step, zl))
            share(r, first + which)

    def x_opposite(buf, zz, at, share, first):
        r = row_at(x + 2, zz)
        for which in range(2):
            arrive(part_of(buf, r, which), xo_sem.at[2 * at + which])
        share(r, first)

    def y_sends(zz, at, which):
        ref = rows_of(chip_at(y, zz), which)
        send(ref, ref, y_sem.at[4 * at + which], along(y + 1, zh))
        send(ref, ref, y_sem.at[4 * at + 2 + which], along(y + 3, zh))

    def y_arrive(zz, at):
        for which in range(2):
            ref = rows_of(chip_at(y + 3, zz), which)
            arrive(ref, y_sem.at[4 * at + which])
            if which == 0:
                send(ref, ref, yo_sem.at[2 * at], along(y + 1, zh))
            ref = rows_of(chip_at(y + 1, zz), which)
            arrive(ref, y_sem.at[4 * at + 2 + which])
            if which == 1:
                send(ref, ref, yo_sem.at[2 * at + 1], along(y + 3, zh))

    def y_opposite(zz, at):
        for which in range(2):
            arrive(rows_of(chip_at(y + 2, zz), which), yo_sem.at[2 * at + which])

    def z_sends(which):
        ref = rows_of(chip, which)
        send(ref, ref, z_sem.at[which], along(y, zh + 1))
        send(ref, ref, z_sem.at[2 + which], along(y, zh + 3))

    def z_arrive(which):
        ref = rows_of(chip_at(y, zh + 3), which)
        arrive(ref, z_sem.at[which])
        if which == 0:
            send(ref, ref, zo_sem.at[0], along(y, zh + 1))
        y_sends(zh + 3, 1, which)
        ref = rows_of(chip_at(y, zh + 1), which)
        arrive(ref, z_sem.at[2 + which])
        if which == 1:
            send(ref, ref, zo_sem.at[1], along(y, zh + 3))
        y_sends(zh + 1, 2, which)

    x_sends(r_own, zl, 0)

    arrive(sib_buf.at[pl.ds(half, HALF)], sib_sem.at[0])
    mine = (lax.broadcasted_iota(jnp.int32, (HALF, LANES), 1) // 64) == core
    here = pl.ds(half, HALF)
    s_buf[chip] = jnp.where(mine, own_buf[here, :], sib_buf[here, :])
    z_sends(0)
    z_sends(1)
    y_sends(zh, 0, 0)
    y_sends(zh, 0, 1)
    share_own(row, 0)

    @pl.when(jnp.logical_not(at_end))
    def _():
        arrive(r_out.at[row], out_sem.at[1])

    x_sends(r_out, zl, 1)
    share_out(row, 0)

    z_arrive(0)
    send(r_own.at[row], r_own.at[row], zr_sem.at[0], across(x, 1 - zl))
    y_arrive(zh, 0)
    x_arrive(r_own, zl, 0, share_own, 2)
    z_arrive(1)
    send(r_out.at[row], r_out.at[row], zr_sem.at[1], across(x, 1 - zl))
    x_opposite(r_own, zl, 0, share_own, 4)
    x_arrive(r_out, zl, 1, share_out, 2)

    r = row_at(x, 1 - zl)
    arrive(r_own.at[r], zr_sem.at[0])
    x_sends(r_own, 1 - zl, 2)
    share_own(r, 1)

    for which in range(2):
        arrive(rows_of(chip_at(y, zh + 2), which), zo_sem.at[which])
        y_sends(zh + 2, 3, which)

    arrive(r_out.at[r], zr_sem.at[1])
    x_sends(r_out, 1 - zl, 3)
    share_out(r, 1)

    def mixed_tile(far, out):
        unfolded = pltpu.roll(out.astype(F32), LANES - BS, 1).astype(BF16)
        return jnp.concatenate(
            [jnp.where(odd, far[:LANES], out), jnp.where(odd, far[LANES:], unfolded)], axis=0
        )

    def window(r):
        return jnp.concatenate(
            [
                r_own[r, :DEPTH], r_own[r, DEPTH:], sib_own[r, DEPTH:], r_out[r, :DEPTH],
                mixed_tile(sib_own[r, :DEPTH], r_out[r, DEPTH:]),
                sib_own[r, :DEPTH], sib_out[r, :DEPTH],
                mixed_tile(r_own[r, :DEPTH], sib_out[r, DEPTH:]),
            ],
            axis=1,
        )

    def build(xx, at):
        arrive(sib_own.at[0], sr_sem.at[at[0]])
        arrive(sib_out.at[0], so_sem.at[at[0]])
        arrive(sib_own.at[0], sr_sem.at[at[1]])
        arrive(sib_out.at[0], so_sem.at[at[1]])
        for zz in range(2):
            r = row_at(xx, zz)
            wide[r] = window(r)

    def add_up(blocks, last=False):
        blocks = [lax.rem(yy, 4) for yy in blocks]

        def strip(step, _):
            here = pl.ds(pl.multiple_of(step * STRIP, STRIP), STRIP)
            rows = jnp.concatenate(
                [s_buf[yy * 4 + t, here, :] for yy in blocks for t in range(4)], axis=1
            )
            weights = jnp.concatenate([wide[yy * 2 + t] for yy in blocks for t in range(2)], axis=0)
            value = jnp.dot(rows, weights, preferred_element_type=F32)
            if not last:
                theta[here, :] = value
                return 0
            value = theta[here, :] + value
            high = value.astype(BF16)
            low = (value - high.astype(F32)).astype(BF16)
            there = pl.ds(pl.multiple_of(half + step * STRIP, STRIP), STRIP)
            for t, source in enumerate((0, 1, 2, 3, 4)):
                lanes = slice(source * LANES, (source + 1) * LANES)
                high_ref[t, there, :] = high[:, lanes]
                low_ref[t, there, :] = low[:, lanes]
            for t, source in enumerate((5, 2, 1, 6, 7)):
                lanes = slice(source * LANES, (source + 1) * LANES)
                high_sib[t, here, :] = high[:, lanes]
                low_sib[t, here, :] = low[:, lanes]
            return 0

        lax.fori_loop(0, HALF // STRIP, strip, 0)

    y_arrive(zh + 3, 1)
    y_arrive(zh + 1, 2)
    x_opposite(r_out, zl, 1, share_out, 4)
    x_arrive(r_own, 1 - zl, 2, share_own, 5)
    x_arrive(r_out, 1 - zl, 3, share_out, 5)
    y_arrive(zh + 2, 3)
    build(x, (0, 1))
    x_opposite(r_own, 1 - zl, 2, share_own, 7)
    build(x + 3, (2, 5))
    build(x + 1, (3, 6))
    y_opposite(zh, 0)
    far_x = lax.rem(x + 2, 4)
    late = jnp.where(far_x == y, y, jnp.where(far_x == lax.rem(y + 1, 4), y + 1, y + 3))
    early = jnp.where(late == y, y + 1, y), jnp.where(late == y + 3, y + 1, y + 3)
    add_up(early)
    x_opposite(r_out, 1 - zl, 3, share_out, 7)
    build(x + 2, (4, 7))
    y_opposite(zh + 3, 1)
    y_opposite(zh + 1, 2)
    y_opposite(zh + 2, 3)
    add_up((late, y + 2), last=True)

    row_ids = lax.broadcasted_iota(jnp.int32, (LANES, LANES), 0)
    upper = row_ids < lane
    same = lax.rem(row_ids // BS + lane // BS, 2) == 0
    diagonal = row_ids == lane

    def gram_of(high_at, low_at, out):
        def gram(a, others):
            high = jnp.concatenate([high_at(t) for t in others], axis=1)
            low = jnp.concatenate([low_at(t) for t in others], axis=1)

            def over_rows(p, q):
                return lax.dot_general(p, q, (((0,), (0,)), ((), ())), preferred_element_type=F32)

            width = len(others) * LANES
            first = over_rows(high_at(a), jnp.concatenate([high, low], axis=1))
            return first[:, :width] + (first[:, width:] + over_rows(low_at(a), high))

        saved = []

        def put(at, value):
            out[at * LANES:(at + 1) * LANES, :] = value

        def segments(tile):
            kept = jnp.sum(jnp.where(diagonal, tile, 0.0), axis=0, keepdims=True)
            return [kept] + [pltpu.roll(kept, LANES - BS * k, 1) for k in range(1, 4)]

        def near():
            e_own = gram(0, (0, 2, 4))
            o_own = gram(1, (1, 3, 4))
            put(0, jnp.where(upper, e_own[:, :LANES], o_own[:, :LANES]))
            put(1, e_own[:, LANES:2 * LANES])
            put(2, o_own[:, LANES:2 * LANES])
            put(3, jnp.where(odd, o_own[:, 2 * LANES:], e_own[:, 2 * LANES:]))
            saved.extend(segments(e_own[:, :LANES]))

        def far():
            e_far = gram(2, (2, 4))
            o_far = gram(3, (3, 4))
            put(4, jnp.where(upper, e_far[:, :LANES], o_far[:, :LANES]))
            put(5, jnp.where(same, gram(4, (4,)), jnp.where(odd, o_far[:, LANES:], e_far[:, LANES:])))
            packed = jnp.concatenate(saved + segments(e_far[:, :LANES]), axis=0)
            there = slice(VECTORS, VECTORS + 8)
            out[there, :] = jnp.where(lane[:8] < BS, packed, out[there, :])

        return near, far

    gathered = len(sent)
    for_sib = gram_of(lambda t: high_sib[t], lambda t: low_sib[t], part_sib)
    for_own = gram_of(lambda t: high_ref[t, here, :], lambda t: low_ref[t, here, :], part)

    def shares(group, owner):
        start, size = GROUPS[group]
        return pl.ds(pl.multiple_of(start + owner * size, 8), size)

    def group_rows(group):
        start, size = GROUPS[group]
        return pl.ds(start, 8 * size)

    def peer_at(step):
        return lax.rem(row + step, 8)

    for group in range(2):
        for_sib[group]()
        rows = group_rows(group)
        send(part_sib.at[rows, :], part_in.at[rows, :], sib_sem.at[1 + group], sibling)
        for_own[group]()
        arrive(part_in.at[rows, :], sib_sem.at[1 + group])
        part[rows, :] = part[rows, :] + part_in[rows, :]
        size = GROUPS[group][1]
        for step in range(1, 8):
            send(
                part.at[shares(group, peer_at(step)), :], landed.at[group, step - 1, pl.ds(0, size), :],
                part_sem.at[7 * group + step - 1], {"row": peer_at(step), "col": col},
            )
    send(high_sib, high_ref.at[:, here, :], sib_sem.at[3], sibling)
    send(low_sib, low_ref.at[:, here, :], sib_sem.at[4], sibling)
    for copy in sent[:gathered]:
        copy.wait_send()
    summed = len(sent)
    for group in range(2):
        size = GROUPS[group][1]
        mine = shares(group, row)
        total = part[mine, :]
        for step in range(1, 8):
            arrive(landed.at[group, step - 1, pl.ds(0, size), :], part_sem.at[7 * group + step - 1])
            total = total + landed[group, step - 1, :size]
        gram_ref[mine, :] = total
        for step in range(1, 8):
            send(
                gram_ref.at[mine, :], gram_ref.at[mine, :], full_sem.at[7 * group + step - 1],
                {"row": peer_at(step), "col": col},
            )

    @pl.when(jnp.logical_not(at_end))
    def _():
        to_outer.wait_send()

    for copy in sent[gathered:summed]:
        copy.wait_send()
    arrive(high_sib, sib_sem.at[3])
    arrive(low_sib, sib_sem.at[4])
    for group in range(2):
        for step in range(1, 8):
            arrive(gram_ref.at[shares(group, 0), :], full_sem.at[7 * group + step - 1])
    for copy in sent[summed:]:
        copy.wait_send()


def split(value):
    high = value.astype(BF16)
    return high, (value - high.astype(F32)).astype(BF16)


def dot1(a, b):
    return jnp.dot(a, b, preferred_element_type=F32)


def dot3(a, b):
    ah, al = a if isinstance(a, tuple) else split(a)
    bh, bl = b if isinstance(b, tuple) else split(b)
    return dot1(ah, bh) + (dot1(ah, bl) + dot1(al, bh))


def block_of(shape, axis):
    return lax.broadcasted_iota(jnp.int32, shape, axis) // BS


def identity(n):
    shape = (n, n)
    rows = lax.broadcasted_iota(jnp.int32, shape, 0)
    return (rows == lax.broadcasted_iota(jnp.int32, shape, 1)).astype(F32)


def pair_ids(blocks, ids):
    out = jnp.full(blocks.shape, ids[0], jnp.int32)
    for at, value in enumerate(ids[1:], 1):
        out = jnp.where(blocks == at, value, out)
    return out


def pair_mask(n, ids):
    return pair_ids(block_of((n, n), 0), ids) == pair_ids(block_of((n, n), 1), ids)


def angles_of(gram, eye, mask):
    kept = gram * eye
    across = jnp.sum(kept, axis=0, keepdims=True)
    down = jnp.sum(kept, axis=1, keepdims=True)
    spread = across - down
    middle = 0.5 * (across + down)
    angles = gram * spread / (2.0 * (spread * spread + middle * middle + EPSILON))
    return jnp.where(mask, jnp.clip(angles, -0.25, 0.25), 0.0)


def cayley(grams, ids, x_ref, e_ref):
    n = grams[0].shape[0]
    eye = identity(n)
    masks = {each: pair_mask(n, each) for each in set(ids)}
    angles = [split(angles_of(g, eye, masks[each])) for g, each in zip(grams, ids)]
    squares = [dot3(a, a) for a in angles]
    sums = []
    for s in squares:
        sums.append(jnp.sum(jnp.abs(s), axis=0, keepdims=True))
    bound = jnp.max(functools.reduce(jnp.maximum, sums))
    scale = 2.0 / (2.0 + bound)
    rho = bound * scale * 0.5
    lift = 2.0 / (2.0 - rho * rho)
    for at, s in enumerate(squares):
        e = eye - scale * (eye - s)
        e_ref[at, :n, :n] = e
        x_ref[at, :n, :n] = (scale * lift) * (eye + e)

    def unfinished(state):
        return state[0] > TOLERANCE

    def refine(state):
        left, grow = state
        next_grow = 2.0 / (2.0 - left * left)
        for at in range(len(grams)):
            e = split(e_ref[at, :n, :n])
            e = eye - grow * (eye - dot3(e, e))
            x = x_ref[at, :n, :n]
            e_ref[at, :n, :n] = e
            x_ref[at, :n, :n] = next_grow * (x + dot3(e, x))
        return left * left * 0.5 * next_grow, next_grow

    lax.while_loop(unfinished, refine, (rho * rho * 0.5 * lift, lift))
    turns = []
    for at, a in enumerate(angles):
        x = x_ref[at, :n, :n]
        odd = 2.0 * dot3(a, x)
        even = 2.0 * x - eye
        turns.append((even + odd, even - odd))
    return turns


def swap_middle(a, b, axis):
    if axis == 0:
        return (
            jnp.concatenate([a[:64], b[BS:64], a[96:]], axis=0),
            jnp.concatenate([b[:BS], a[64:96], b[64:]], axis=0),
        )
    block = block_of(a.shape, 1)
    return (
        jnp.where(block == 2, pltpu.roll(b, BS, 1), a),
        jnp.where(block == 1, pltpu.roll(a, LANES - BS, 1), b),
    )


def swap_odd(a, b, axis):
    if axis == 0:
        return (
            jnp.concatenate([a[:BS], b[BS:64], a[64:96], b[96:]], axis=0),
            jnp.concatenate([b[:BS], a[BS:64], b[64:96], a[96:]], axis=0),
        )
    odd = lax.rem(block_of(a.shape, 1), 2) == 1
    return jnp.where(odd, b, a), jnp.where(odd, a, b)


def swap_ends(a, b, axis):
    if axis == 0:
        return (
            jnp.concatenate([a[:96], b[:BS]], axis=0),
            jnp.concatenate([a[96:], b[BS:]], axis=0),
        )
    block = block_of(a.shape, 1)
    return (
        jnp.where(block == 3, pltpu.roll(b, 96, 1), a),
        jnp.where(block == 0, pltpu.roll(a, BS, 1), b),
    )


def regroup(gram, swap):
    near, cross, far = gram
    near, cross_top = swap(near, cross, 1)
    cross_bottom, far = swap(cross.T, far, 1)
    near, _ = swap(near, cross_bottom, 0)
    cross, far = swap(cross_top, far, 0)
    return near, cross, far


def rounds_kernel(g_ref, high_ref, low_ref, out_ref, x_ref, e_ref, w_ref, stage, out_sem):
    def tile(at):
        return g_ref[at * LANES:(at + 1) * LANES, :]

    shape = (LANES, LANES)
    row_ids = lax.broadcasted_iota(jnp.int32, shape, 0)
    lane_ids = lax.broadcasted_iota(jnp.int32, shape, 1)

    def segment(at):
        return g_ref[VECTORS + at:VECTORS + at + 1, :]

    def both(packed, vector):
        turned = packed.T
        diagonal = row_ids == lane_ids
        upper = jnp.where(row_ids < lane_ids, packed, turned)
        kept = segment(4 * vector)
        for k in range(1, 4):
            kept = jnp.where(lane_ids[:1] // BS == k, pltpu.roll(segment(4 * vector + k), BS * k, 1), kept)
        upper = jnp.where(diagonal, kept, upper)
        return upper, jnp.where(row_ids < lane_ids, turned, packed)

    own_e, own_o = both(tile(0), 0)
    far_e, far_o = both(tile(4), 1)
    mixed = jnp.where(row_ids < lane_ids, tile(5), tile(5).T)
    turns = cayley([own_e, far_e, own_o, far_o, mixed], (ALTERNATE,) * 5, x_ref, e_ref)
    columns = block_of((LANES, LANES), 1)
    rows = block_of((LANES, LANES), 0)
    chains = []
    for own, far, own_turn, far_turn, base, moved in (
        (own_e, far_e, turns[0], turns[1], 1, 2),
        (own_o, far_o, turns[2], turns[3], 2, 1),
    ):
        near, own_mixed, far_mixed = tile(base), tile(3), tile(5)
        mixed_turn = turns[4]
        far_q = jnp.where(columns == moved, 0.0, far_turn[0])
        far_t = jnp.where(rows == moved, 0.0, far_turn[1])
        mixed_q = jnp.where(columns == moved, mixed_turn[0], 0.0)
        mixed_t = jnp.where(rows == moved, mixed_turn[1], 0.0)
        tail_q = split(jnp.concatenate([far_q, mixed_q], axis=0))
        tail_t = split(jnp.concatenate([far_t, mixed_t], axis=1))
        own_q = split(own_turn[0])
        own_t = split(own_turn[1])
        head = jnp.concatenate([near, own_mixed], axis=1)
        body = jnp.concatenate(
            [
                jnp.concatenate([far, far_mixed], axis=1),
                jnp.concatenate([far_mixed.T, mixed], axis=1),
            ],
            axis=0,
        )
        corner = dot3(own_t, dot3(own, own_q))
        side = dot3(own_t, dot3(head, tail_q))
        rest = dot3(tail_t, dot3(body, tail_q))
        chains.append((regroup((corner, side, rest), swap_middle), own_q, tail_q))
    turns = cayley([t for c in chains for t in (c[0][0], c[0][2])], (OUTSIDE,) * 4, x_ref, e_ref)
    grams = []
    weights = []
    for at, ((near, cross, far), own_q, tail_q) in enumerate(chains):
        (near_q, near_t), (far_q, far_t) = turns[2 * at:2 * at + 2]
        zero = jnp.zeros((BS, LANES), F32)
        top = jnp.concatenate(
            [
                jnp.concatenate([near_q[:64], zero, near_q[96:]], axis=0),
                jnp.concatenate([zero, zero, far_q[BS:64], zero], axis=0),
            ],
            axis=1,
        )
        bottom = jnp.concatenate(
            [
                jnp.concatenate([zero, near_q[64:96], zero, zero], axis=0),
                jnp.concatenate([far_q[:BS], zero, far_q[64:]], axis=0),
            ],
            axis=1,
        )
        spread = jnp.concatenate([dot3(own_q, top), dot3(tail_q, bottom)], axis=0)
        swap = swap_odd if at == 0 else swap_ends
        weights.append(jnp.concatenate(swap(spread[:, :LANES], spread[:, LANES:], 1), axis=1))
        near_q, near_t, far_q, far_t = split(near_q), split(near_t), split(far_q), split(far_t)
        turned = (
            dot3(near_t, dot3(near, near_q)),
            dot3(near_t, dot3(cross, far_q)),
            dot3(far_t, dot3(far, far_q)),
        )
        grams.append(regroup(turned, swap))
    turns = cayley(
        [t for g in grams for t in (g[0], g[2])],
        (ALTERNATE, ADJACENT, ALTERNATE, ALTERNATE), x_ref, e_ref,
    )
    lasts = []
    for at, (near, cross, far) in enumerate(grams):
        (near_q, near_t), (far_q, far_t) = turns[2 * at:2 * at + 2]
        zero = jnp.zeros((BS, LANES), F32)
        if at == 0:
            kept = lax.rem(columns, 2) == 0
            near_q = jnp.where(kept, near_q, 0.0)
            far_q = jnp.where(kept, 0.0, pltpu.roll(far_q, BS, 1))
            near_t = jnp.concatenate([near_t[:BS], zero, near_t[64:96], zero], axis=0)
            far_t = jnp.concatenate([zero, far_t[:BS], zero, far_t[64:96]], axis=0)
        else:
            kept = columns == 1
            near_q = jnp.where(kept, pltpu.roll(near_q, LANES - BS, 1), 0.0)
            far_q = jnp.where(kept, 0.0, far_q)
            near_t = jnp.concatenate([zero, near_t[64:96], zero, zero], axis=0)
            far_t = jnp.concatenate([far_t[:BS], zero, far_t[64:]], axis=0)
        q = split(jnp.concatenate([near_q, far_q], axis=0))
        t = jnp.concatenate([near_t, far_t], axis=1)
        gram = jnp.concatenate(
            [jnp.concatenate([near, cross], axis=1), jnp.concatenate([cross.T, far], axis=1)], axis=0
        )
        lasts.append(dot3(t, dot3(gram, q)))
        weights[at] = dot3(weights[at], q)
    turns = cayley(lasts, (ADJACENT, OUTSIDE), x_ref, e_ref)
    core = lax.rem(lax.axis_index("col"), 2)
    block = block_of((2 * LANES, 2 * LANES), 1)
    block = jnp.where(core == 0, block, 7 - block)
    source = pair_ids(block, (7, 4, 3, 2, 6, 5, 0, 1))
    row = lax.broadcasted_iota(jnp.int32, (2 * LANES, 2 * LANES), 0)
    lane = lax.broadcasted_iota(jnp.int32, (2 * LANES, 2 * LANES), 1)
    place = (row == source * BS + lane % BS).astype(BF16)
    placed = []
    for at, (q, _) in enumerate(turns):
        spot = place[at * LANES:(at + 1) * LANES]
        qh, ql = split(q)
        placed.append((dot1(qh, spot).astype(BF16), dot1(ql, spot).astype(BF16)))
    e_rows = dot3(weights[0], placed[0])
    o_rows = dot3(weights[1], placed[1])
    total = jnp.concatenate(
        [
            e_rows[:2 * LANES],
            o_rows[:2 * LANES],
            e_rows[2 * LANES:] + o_rows[2 * LANES:],
        ],
        axis=0,
    )
    w_high, w_low = split(total)
    w_ref[0] = w_high
    w_ref[1] = w_low

    def strip(step, _):
        here = pl.ds(pl.multiple_of(step * STRIP, STRIP), STRIP)
        high = jnp.concatenate([high_ref[t, here, :] for t in TILE_ORDER], axis=1)
        low = jnp.concatenate([low_ref[t, here, :] for t in TILE_ORDER], axis=1)
        stage[here, :] = dot1(high, w_ref[0]) + (dot1(high, w_ref[1]) + dot1(low, w_ref[0]))
        pltpu.make_async_copy(stage.at[here, :], out_ref.at[here, :], out_sem.at[step]).start()
        return 0

    count = high_ref.shape[1] // STRIP
    lax.fori_loop(0, count, strip, 0, unroll=True)
    for step in range(count):
        here = pl.ds(step * STRIP, STRIP)
        pltpu.make_async_copy(stage.at[here, :], out_ref.at[here, :], out_sem.at[step]).wait()


def shards(left_factor, right_factor, weights, plan):
    vmem = pl.BlockSpec(memory_space=pltpu.VMEM)
    dma = pltpu.SemaphoreType.DMA
    high, low, gram = pl.pallas_call(
        gather_kernel,
        name="gather_and_gram",
        out_shape=(
            jax.ShapeDtypeStruct((5, ROWS, LANES), BF16),
            jax.ShapeDtypeStruct((5, ROWS, LANES), BF16),
            jax.ShapeDtypeStruct((GRAM_ROWS, LANES), F32),
        ),
        in_specs=[pl.BlockSpec(memory_space=pltpu.HBM)] * 4,
        out_specs=(vmem, vmem, vmem),
        scratch_shapes=[
            pltpu.VMEM((ROWS, 64), BF16),
            pltpu.VMEM((1, 64), F32),
            pltpu.VMEM((DEPTH, 2 * LANES), BF16),
            pltpu.SMEM((4, 256), jnp.int32),
            pltpu.VMEM((ROWS, LANES), BF16),
            pltpu.VMEM((ROWS, LANES), BF16),
            pltpu.VMEM((PACKED, LANES), BF16),
            pltpu.VMEM((16, HALF, LANES), BF16),
            pltpu.VMEM((8, 2 * DEPTH, LANES), BF16),
            pltpu.VMEM((8, PACKED, LANES), BF16),
            pltpu.VMEM((8, 2 * DEPTH, LANES), BF16),
            pltpu.VMEM((8, PACKED, LANES), BF16),
            pltpu.VMEM((8, DEPTH, 8 * LANES), BF16),
            pltpu.VMEM((HALF, 8 * LANES), F32),
            pltpu.VMEM((5, HALF, LANES), BF16),
            pltpu.VMEM((5, HALF, LANES), BF16),
            pltpu.VMEM((GRAM_ROWS, LANES), F32),
            pltpu.VMEM((GRAM_ROWS, LANES), F32),
            pltpu.VMEM((GRAM_ROWS, LANES), F32),
            pltpu.VMEM((2, 7, 64, LANES), F32),
        ] + [dma((count,)) for count in (4, 110, 2, 5, 4, 2, 16, 8, 2, 8, 8, 8, 8, 14, 14)],
        compiler_params=pltpu.CompilerParams(
            collective_id=0, has_side_effects=True, vmem_limit_bytes=VMEM_LIMIT
        ),
    )(left_factor, weights, right_factor, plan)
    return pl.pallas_call(
        rounds_kernel,
        name="rounds",
        out_shape=jax.ShapeDtypeStruct((ROWS, 2 * LANES), F32),
        in_specs=[vmem, vmem, vmem],
        out_specs=pl.BlockSpec(memory_space=pltpu.HBM),
        scratch_shapes=[
            pltpu.VMEM((5, 2 * LANES, 2 * LANES), F32),
            pltpu.VMEM((5, 2 * LANES, 2 * LANES), F32),
            pltpu.VMEM((2, 5 * LANES, 2 * LANES), BF16),
            pltpu.VMEM((ROWS, 2 * LANES), F32),
            dma((ROWS // STRIP,)),
        ],
        compiler_params=pltpu.CompilerParams(vmem_limit_bytes=VMEM_LIMIT),
    )(gram, high, low)


def solution(mesh):
    in_specs = (P("row", "col"), P("row", "col"), P("col"), P())
    out_specs = P("row", "col")
    return jax.shard_map(shards, mesh=mesh, in_specs=in_specs, out_specs=out_specs, check_vma=False)
```

```python
import functools

import jax
import jax.numpy as jnp
from jax import lax
from jax.experimental import pallas as pl
from jax.experimental.pallas import tpu as pltpu
from jax.sharding import PartitionSpec as P

BS = 32
LANES = 128
EPSILON = 1e-06
TOLERANCE = 1e-04
STRIP = 256
TILE_ORDER = (0, 2, 1, 3, 4)
ALTERNATE = (0, 1, 0, 1)
ADJACENT = (0, 0, 1, 1)
OUTSIDE = (0, 1, 1, 0)
BF16 = jnp.bfloat16
F32 = jnp.float32
MESH = pl.DeviceIdType.MESH
ROWS = 1024
HALF = 512
QUARTER = 256
DEPTH = 256
PACKED = 384
SHARE = 96
GRAM_ROWS = 8 * SHARE
VECTORS = 5 * LANES + 64
GROUPS = ((0, 64), (512, 32))
VMEM_LIMIT = 48 * 1024 * 1024


def gather_kernel(
    left_hbm, weights_hbm, right_hbm, plan_hbm,
    high_ref, low_ref, gram_ref,
    left_ref, weights_ref, right_ref, plan_ref,
    own_buf, sib_buf, fold_buf, s_buf, r_own, r_out, sib_own, sib_out,
    wide, theta, high_sib, low_sib, part, part_sib, part_in, landed,
    in_sem, send_sem, out_sem, sib_sem, z_sem, zo_sem, y_sem, yo_sem,
    zr_sem, x_sem, xo_sem, sr_sem, so_sem, part_sem, full_sem,
):
    row = lax.axis_index("row")
    col = lax.axis_index("col")
    x, zl = row // 2, lax.rem(row, 2)
    core = lax.rem(col, 2)
    chip = col // 2
    y, zh = chip // 4, lax.rem(chip, 4)
    sibling = {"row": row, "col": col + 1 - 2 * core}
    outer_col = col - 1 + 2 * core
    at_end = jnp.logical_or(outer_col < 0, outer_col > 31)
    outer = {"row": row, "col": outer_col}

    def chip_at(yy, zz):
        return lax.rem(yy, 4) * 4 + lax.rem(zz, 4)

    def along(yy, zz):
        return {"row": row, "col": chip_at(yy, zz) * 2 + core}

    def row_at(xx, zz):
        return lax.rem(xx, 4) * 2 + zz

    def across(xx, zz):
        return {"row": row_at(xx, zz), "col": col}

    sent = []

    def send(src, dst, sem, device):
        copy = pltpu.make_async_remote_copy(
            src_ref=src, dst_ref=dst, send_sem=send_sem.at[len(sent)], recv_sem=sem,
            device_id=device, device_id_type=MESH,
        )
        copy.start()
        sent.append(copy)

    def arrive(ref, sem):
        pltpu.make_async_copy(ref, ref, sem).wait()

    inputs = [
        pltpu.make_async_copy(src, dst, in_sem.at[at])
        for at, (src, dst) in enumerate((
            (left_hbm, left_ref), (weights_hbm, weights_ref.at[0]),
            (right_hbm, right_ref), (plan_hbm, plan_ref),
        ))
    ]
    for copy in inputs:
        copy.start()

    barrier = pltpu.get_barrier_semaphore()
    peers = [sibling, along(y, zh + 1), along(y, zh + 3), along(y + 1, zh), along(y + 3, zh)]
    for step in range(1, 8):
        peers.append({"row": lax.rem(row + step, 8), "col": col})
    for peer in peers:
        pl.semaphore_signal(barrier, inc=1, device_id=peer, device_id_type=MESH)

    @pl.when(jnp.logical_not(at_end))
    def _():
        pl.semaphore_signal(barrier, inc=1, device_id=outer, device_id_type=MESH)

    inputs[0].wait()
    inputs[1].wait()
    scaled = (left_ref[...].astype(F32) * weights_ref[...]).astype(BF16)
    own_buf[...] = jnp.concatenate([scaled, scaled], axis=1)

    pl.semaphore_wait(barrier, jnp.where(at_end, 12, 13))

    half = pl.multiple_of(core * HALF, HALF)
    other = pl.multiple_of(HALF - core * HALF, HALF)
    send(own_buf.at[pl.ds(other, HALF)], sib_buf.at[pl.ds(other, HALF)], sib_sem.at[0], sibling)

    inputs[2].wait()
    inputs[3].wait()
    ids = []
    for slot in (0, 4, 1, 5, 2, 6, 3, 7):
        there = jnp.where(core == 0, slot, 7 - slot)
        ids.append(plan_ref[0, col * 8 + there] - col * 8)
    block = lax.broadcasted_iota(jnp.int32, (DEPTH, 256), 1) // BS
    source = jnp.zeros((DEPTH, 256), jnp.int32)
    for at, value in enumerate(ids):
        source = jnp.where(block == at, value, source)
    column = lax.broadcasted_iota(jnp.int32, (DEPTH, 256), 1)
    place = lax.broadcasted_iota(jnp.int32, (DEPTH, 256), 0) == source * BS + lax.rem(column, BS)
    ordered = jnp.dot(right_ref[...], place.astype(BF16), preferred_element_type=F32)
    lane = lax.broadcasted_iota(jnp.int32, (LANES, LANES), 1)
    odd = lax.rem(lane // BS, 2) == 1
    tail = ordered[:, LANES:]
    folded = jnp.where(odd, pltpu.roll(tail[LANES:], BS, 1), tail[:LANES]).astype(BF16)
    first = ordered[:, :LANES].astype(BF16)
    r_own[row] = jnp.concatenate([first, tail.astype(BF16)], axis=0)
    own_fold = jnp.concatenate([first, folded], axis=0)
    fold_buf[...] = own_fold

    def rows_of(q, which):
        return s_buf.at[q, pl.ds(which * QUARTER, QUARTER), :]

    to_outer = pltpu.make_async_remote_copy(
        src_ref=fold_buf, dst_ref=r_out.at[row],
        send_sem=out_sem.at[0], recv_sem=out_sem.at[1], device_id=outer, device_id_type=MESH,
    )

    @pl.when(jnp.logical_not(at_end))
    def _():
        to_outer.start()

    @pl.when(at_end)
    def _():
        r_out[row] = own_fold

    def part_of(buf, r, which):
        size = buf.shape[1] // 2
        return buf.at[r, pl.ds(which * size, size), :]

    def x_sends(buf, zz, at):
        r = row_at(x, zz)
        send(buf.at[r], buf.at[r], x_sem.at[2 * at], across(x + 1, zl))
        send(buf.at[r], buf.at[r], x_sem.at[2 * at + 1], across(x + 3, zl))

    def share_own(r, at):
        send(r_own.at[r], sib_own.at[r], sr_sem.at[at], sibling)

    def share_out(r, at):
        send(r_out.at[r], sib_out.at[r], so_sem.at[at], sibling)

    def x_arrive(buf, zz, at, share, first):
        for which, step in ((0, 3), (1, 1)):
            r = row_at(x + step, zz)
            arrive(buf.at[r], x_sem.at[2 * at + which])
            piece = part_of(buf, r, which)
            send(piece, piece, xo_sem.at[2 * at + which], across(x + 4 - step, zl))
            share(r, first + which)

    def x_opposite(buf, zz, at, share, first):
        r = row_at(x + 2, zz)
        for which in range(2):
            arrive(part_of(buf, r, which), xo_sem.at[2 * at + which])
        share(r, first)

    def y_sends(zz, at, which):
        ref = rows_of(chip_at(y, zz), which)
        send(ref, ref, y_sem.at[4 * at + which], along(y + 1, zh))
        send(ref, ref, y_sem.at[4 * at + 2 + which], along(y + 3, zh))

    def y_arrive(zz, at):
        for which in range(2):
            ref = rows_of(chip_at(y + 3, zz), which)
            arrive(ref, y_sem.at[4 * at + which])
            if which == 0:
                send(ref, ref, yo_sem.at[2 * at], along(y + 1, zh))
            ref = rows_of(chip_at(y + 1, zz), which)
            arrive(ref, y_sem.at[4 * at + 2 + which])
            if which == 1:
                send(ref, ref, yo_sem.at[2 * at + 1], along(y + 3, zh))

    def y_opposite(zz, at):
        for which in range(2):
            arrive(rows_of(chip_at(y + 2, zz), which), yo_sem.at[2 * at + which])

    def z_sends(which):
        ref = rows_of(chip, which)
        send(ref, ref, z_sem.at[which], along(y, zh + 1))
        send(ref, ref, z_sem.at[2 + which], along(y, zh + 3))

    def z_arrive(which):
        ref = rows_of(chip_at(y, zh + 3), which)
        arrive(ref, z_sem.at[which])
        if which == 0:
            send(ref, ref, zo_sem.at[0], along(y, zh + 1))
        y_sends(zh + 3, 1, which)
        ref = rows_of(chip_at(y, zh + 1), which)
        arrive(ref, z_sem.at[2 + which])
        if which == 1:
            send(ref, ref, zo_sem.at[1], along(y, zh + 3))
        y_sends(zh + 1, 2, which)

    x_sends(r_own, zl, 0)

    arrive(sib_buf.at[pl.ds(half, HALF)], sib_sem.at[0])
    mine = (lax.broadcasted_iota(jnp.int32, (HALF, LANES), 1) // 64) == core
    here = pl.ds(half, HALF)
    s_buf[chip] = jnp.where(mine, own_buf[here, :], sib_buf[here, :])
    z_sends(0)
    z_sends(1)
    y_sends(zh, 0, 0)
    y_sends(zh, 0, 1)
    share_own(row, 0)

    @pl.when(jnp.logical_not(at_end))
    def _():
        arrive(r_out.at[row], out_sem.at[1])

    x_sends(r_out, zl, 1)
    share_out(row, 0)

    z_arrive(0)
    send(r_own.at[row], r_own.at[row], zr_sem.at[0], across(x, 1 - zl))
    y_arrive(zh, 0)
    x_arrive(r_own, zl, 0, share_own, 2)
    z_arrive(1)
    send(r_out.at[row], r_out.at[row], zr_sem.at[1], across(x, 1 - zl))
    x_opposite(r_own, zl, 0, share_own, 4)
    x_arrive(r_out, zl, 1, share_out, 2)

    r = row_at(x, 1 - zl)
    arrive(r_own.at[r], zr_sem.at[0])
    x_sends(r_own, 1 - zl, 2)
    share_own(r, 1)

    for which in range(2):
        arrive(rows_of(chip_at(y, zh + 2), which), zo_sem.at[which])
        y_sends(zh + 2, 3, which)

    arrive(r_out.at[r], zr_sem.at[1])
    x_sends(r_out, 1 - zl, 3)
    share_out(r, 1)

    def mixed_tile(far, out):
        unfolded = pltpu.roll(out.astype(F32), LANES - BS, 1).astype(BF16)
        return jnp.concatenate(
            [jnp.where(odd, far[:LANES], out), jnp.where(odd, far[LANES:], unfolded)], axis=0
        )

    def window(r):
        return jnp.concatenate(
            [
                r_own[r, :DEPTH], r_own[r, DEPTH:], sib_own[r, DEPTH:], r_out[r, :DEPTH],
                mixed_tile(sib_own[r, :DEPTH], r_out[r, DEPTH:]),
                sib_own[r, :DEPTH], sib_out[r, :DEPTH],
                mixed_tile(r_own[r, :DEPTH], sib_out[r, DEPTH:]),
            ],
            axis=1,
        )

    def build(xx, at):
        arrive(sib_own.at[0], sr_sem.at[at[0]])
        arrive(sib_out.at[0], so_sem.at[at[0]])
        arrive(sib_own.at[0], sr_sem.at[at[1]])
        arrive(sib_out.at[0], so_sem.at[at[1]])
        for zz in range(2):
            r = row_at(xx, zz)
            wide[r] = window(r)

    def add_up(blocks, last=False):
        blocks = [lax.rem(yy, 4) for yy in blocks]

        def strip(step, _):
            here = pl.ds(pl.multiple_of(step * STRIP, STRIP), STRIP)
            rows = jnp.concatenate(
                [s_buf[yy * 4 + t, here, :] for yy in blocks for t in range(4)], axis=1
            )
            weights = jnp.concatenate([wide[yy * 2 + t] for yy in blocks for t in range(2)], axis=0)
            value = jnp.dot(rows, weights, preferred_element_type=F32)
            if not last:
                theta[here, :] = value
                return 0
            value = theta[here, :] + value
            high = value.astype(BF16)
            low = (value - high.astype(F32)).astype(BF16)
            there = pl.ds(pl.multiple_of(half + step * STRIP, STRIP), STRIP)
            for t, source in enumerate((0, 1, 2, 3, 4)):
                lanes = slice(source * LANES, (source + 1) * LANES)
                high_ref[t, there, :] = high[:, lanes]
                low_ref[t, there, :] = low[:, lanes]
            for t, source in enumerate((5, 2, 1, 6, 7)):
                lanes = slice(source * LANES, (source + 1) * LANES)
                high_sib[t, here, :] = high[:, lanes]
                low_sib[t, here, :] = low[:, lanes]
            return 0

        lax.fori_loop(0, HALF // STRIP, strip, 0, unroll=True)

    y_arrive(zh + 3, 1)
    y_arrive(zh + 1, 2)
    x_opposite(r_out, zl, 1, share_out, 4)
    x_arrive(r_own, 1 - zl, 2, share_own, 5)
    x_arrive(r_out, 1 - zl, 3, share_out, 5)
    y_arrive(zh + 2, 3)
    build(x, (0, 1))
    x_opposite(r_own, 1 - zl, 2, share_own, 7)
    build(x + 3, (2, 5))
    build(x + 1, (3, 6))
    y_opposite(zh, 0)
    far_x = lax.rem(x + 2, 4)
    late = jnp.where(far_x == y, y, jnp.where(far_x == lax.rem(y + 1, 4), y + 1, y + 3))
    early = jnp.where(late == y, y + 1, y), jnp.where(late == y + 3, y + 1, y + 3)
    add_up(early)
    x_opposite(r_out, 1 - zl, 3, share_out, 7)
    build(x + 2, (4, 7))
    y_opposite(zh + 3, 1)
    y_opposite(zh + 1, 2)
    y_opposite(zh + 2, 3)
    add_up((late, y + 2), last=True)

    row_ids = lax.broadcasted_iota(jnp.int32, (LANES, LANES), 0)
    upper = row_ids < lane
    same = lax.rem(row_ids // BS + lane // BS, 2) == 0
    diagonal = row_ids == lane

    def gram_of(high_at, low_at, out):
        def gram(a, others):
            high = jnp.concatenate([high_at(t) for t in others], axis=1)
            low = jnp.concatenate([low_at(t) for t in others], axis=1)

            def over_rows(p, q):
                return lax.dot_general(p, q, (((0,), (0,)), ((), ())), preferred_element_type=F32)

            width = len(others) * LANES
            first = over_rows(high_at(a), jnp.concatenate([high, low], axis=1))
            return first[:, :width] + (first[:, width:] + over_rows(low_at(a), high))

        saved = []

        def put(at, value):
            out[at * LANES:(at + 1) * LANES, :] = value

        def segments(tile):
            kept = jnp.sum(jnp.where(diagonal, tile, 0.0), axis=0, keepdims=True)
            return [kept] + [pltpu.roll(kept, LANES - BS * k, 1) for k in range(1, 4)]

        def near():
            e_own = gram(0, (0, 2, 4))
            o_own = gram(1, (1, 3, 4))
            put(0, jnp.where(upper, e_own[:, :LANES], o_own[:, :LANES]))
            put(1, e_own[:, LANES:2 * LANES])
            put(2, o_own[:, LANES:2 * LANES])
            put(3, jnp.where(odd, o_own[:, 2 * LANES:], e_own[:, 2 * LANES:]))
            saved.extend(segments(e_own[:, :LANES]))

        def far():
            e_far = gram(2, (2, 4))
            o_far = gram(3, (3, 4))
            put(4, jnp.where(upper, e_far[:, :LANES], o_far[:, :LANES]))
            put(5, jnp.where(same, gram(4, (4,)), jnp.where(odd, o_far[:, LANES:], e_far[:, LANES:])))
            packed = jnp.concatenate(saved + segments(e_far[:, :LANES]), axis=0)
            there = slice(VECTORS, VECTORS + 8)
            out[there, :] = jnp.where(lane[:8] < BS, packed, out[there, :])

        return near, far

    gathered = len(sent)
    for_sib = gram_of(lambda t: high_sib[t], lambda t: low_sib[t], part_sib)
    for_own = gram_of(lambda t: high_ref[t, here, :], lambda t: low_ref[t, here, :], part)

    def shares(group, owner):
        start, size = GROUPS[group]
        return pl.ds(pl.multiple_of(start + owner * size, 8), size)

    def group_rows(group):
        start, size = GROUPS[group]
        return pl.ds(start, 8 * size)

    def peer_at(step):
        return lax.rem(row + step, 8)

    for group in range(2):
        for_sib[group]()
        rows = group_rows(group)
        send(part_sib.at[rows, :], part_in.at[rows, :], sib_sem.at[1 + group], sibling)
        for_own[group]()
        arrive(part_in.at[rows, :], sib_sem.at[1 + group])
        part[rows, :] = part[rows, :] + part_in[rows, :]
        size = GROUPS[group][1]
        for step in range(1, 8):
            send(
                part.at[shares(group, peer_at(step)), :], landed.at[group, step - 1, pl.ds(0, size), :],
                part_sem.at[7 * group + step - 1], {"row": peer_at(step), "col": col},
            )
    send(high_sib, high_ref.at[:, here, :], sib_sem.at[3], sibling)
    send(low_sib, low_ref.at[:, here, :], sib_sem.at[4], sibling)
    for copy in sent[:gathered]:
        copy.wait_send()
    summed = len(sent)
    for group in range(2):
        size = GROUPS[group][1]
        mine = shares(group, row)
        total = part[mine, :]
        for step in range(1, 8):
            arrive(landed.at[group, step - 1, pl.ds(0, size), :], part_sem.at[7 * group + step - 1])
            total = total + landed[group, step - 1, :size]
        gram_ref[mine, :] = total
        for step in range(1, 8):
            send(
                gram_ref.at[mine, :], gram_ref.at[mine, :], full_sem.at[7 * group + step - 1],
                {"row": peer_at(step), "col": col},
            )

    @pl.when(jnp.logical_not(at_end))
    def _():
        to_outer.wait_send()

    for copy in sent[gathered:summed]:
        copy.wait_send()
    arrive(high_sib, sib_sem.at[3])
    arrive(low_sib, sib_sem.at[4])
    for group in range(2):
        for step in range(1, 8):
            arrive(gram_ref.at[shares(group, 0), :], full_sem.at[7 * group + step - 1])
    for copy in sent[summed:]:
        copy.wait_send()


def split(value):
    high = value.astype(BF16)
    return high, (value - high.astype(F32)).astype(BF16)


def dot1(a, b):
    return jnp.dot(a, b, preferred_element_type=F32)


def dot3(a, b):
    ah, al = a if isinstance(a, tuple) else split(a)
    bh, bl = b if isinstance(b, tuple) else split(b)
    return dot1(ah, bh) + (dot1(ah, bl) + dot1(al, bh))


def block_of(shape, axis):
    return lax.broadcasted_iota(jnp.int32, shape, axis) // BS


def identity(n):
    shape = (n, n)
    rows = lax.broadcasted_iota(jnp.int32, shape, 0)
    return (rows == lax.broadcasted_iota(jnp.int32, shape, 1)).astype(F32)


def pair_ids(blocks, ids):
    out = jnp.full(blocks.shape, ids[0], jnp.int32)
    for at, value in enumerate(ids[1:], 1):
        out = jnp.where(blocks == at, value, out)
    return out


def pair_mask(n, ids):
    return pair_ids(block_of((n, n), 0), ids) == pair_ids(block_of((n, n), 1), ids)


def angles_of(gram, eye, mask):
    kept = gram * eye
    across = jnp.sum(kept, axis=0, keepdims=True)
    down = jnp.sum(kept, axis=1, keepdims=True)
    spread = across - down
    middle = 0.5 * (across + down)
    angles = gram * spread / (2.0 * (spread * spread + middle * middle + EPSILON))
    return jnp.where(mask, jnp.clip(angles, -0.25, 0.25), 0.0)


def cayley(grams, ids, x_ref, e_ref):
    n = grams[0].shape[0]
    eye = identity(n)
    masks = {each: pair_mask(n, each) for each in set(ids)}
    angles = [split(angles_of(g, eye, masks[each])) for g, each in zip(grams, ids)]
    squares = [dot3(a, a) for a in angles]
    sums = []
    for s in squares:
        sums.append(jnp.sum(jnp.abs(s), axis=0, keepdims=True))
    bound = jnp.max(functools.reduce(jnp.maximum, sums))
    scale = 2.0 / (2.0 + bound)
    rho = bound * scale * 0.5
    lift = 2.0 / (2.0 - rho * rho)
    for at, s in enumerate(squares):
        e = eye - scale * (eye - s)
        e_ref[at, :n, :n] = e
        x_ref[at, :n, :n] = (scale * lift) * (eye + e)

    def unfinished(state):
        return state[0] > TOLERANCE

    def refine(state):
        left, grow = state
        next_grow = 2.0 / (2.0 - left * left)
        for at in range(len(grams)):
            e = split(e_ref[at, :n, :n])
            e = eye - grow * (eye - dot3(e, e))
            x = x_ref[at, :n, :n]
            e_ref[at, :n, :n] = e
            x_ref[at, :n, :n] = next_grow * (x + dot3(e, x))
        return left * left * 0.5 * next_grow, next_grow

    lax.while_loop(unfinished, refine, (rho * rho * 0.5 * lift, lift))
    turns = []
    for at, a in enumerate(angles):
        x = x_ref[at, :n, :n]
        odd = 2.0 * dot3(a, x)
        even = 2.0 * x - eye
        turns.append((even + odd, even - odd))
    return turns


def swap_middle(a, b, axis):
    if axis == 0:
        return (
            jnp.concatenate([a[:64], b[BS:64], a[96:]], axis=0),
            jnp.concatenate([b[:BS], a[64:96], b[64:]], axis=0),
        )
    block = block_of(a.shape, 1)
    return (
        jnp.where(block == 2, pltpu.roll(b, BS, 1), a),
        jnp.where(block == 1, pltpu.roll(a, LANES - BS, 1), b),
    )


def swap_odd(a, b, axis):
    if axis == 0:
        return (
            jnp.concatenate([a[:BS], b[BS:64], a[64:96], b[96:]], axis=0),
            jnp.concatenate([b[:BS], a[BS:64], b[64:96], a[96:]], axis=0),
        )
    odd = lax.rem(block_of(a.shape, 1), 2) == 1
    return jnp.where(odd, b, a), jnp.where(odd, a, b)


def swap_ends(a, b, axis):
    if axis == 0:
        return (
            jnp.concatenate([a[:96], b[:BS]], axis=0),
            jnp.concatenate([a[96:], b[BS:]], axis=0),
        )
    block = block_of(a.shape, 1)
    return (
        jnp.where(block == 3, pltpu.roll(b, 96, 1), a),
        jnp.where(block == 0, pltpu.roll(a, BS, 1), b),
    )


def regroup(gram, swap):
    near, cross, far = gram
    near, cross_top = swap(near, cross, 1)
    cross_bottom, far = swap(cross.T, far, 1)
    near, _ = swap(near, cross_bottom, 0)
    cross, far = swap(cross_top, far, 0)
    return near, cross, far


def rounds_kernel(g_ref, high_ref, low_ref, out_ref, x_ref, e_ref, w_ref, stage, out_sem):
    def tile(at):
        return g_ref[at * LANES:(at + 1) * LANES, :]

    shape = (LANES, LANES)
    row_ids = lax.broadcasted_iota(jnp.int32, shape, 0)
    lane_ids = lax.broadcasted_iota(jnp.int32, shape, 1)

    def segment(at):
        return g_ref[VECTORS + at:VECTORS + at + 1, :]

    def both(packed, vector):
        turned = packed.T
        diagonal = row_ids == lane_ids
        upper = jnp.where(row_ids < lane_ids, packed, turned)
        kept = segment(4 * vector)
        for k in range(1, 4):
            kept = jnp.where(lane_ids[:1] // BS == k, pltpu.roll(segment(4 * vector + k), BS * k, 1), kept)
        upper = jnp.where(diagonal, kept, upper)
        return upper, jnp.where(row_ids < lane_ids, turned, packed)

    own_e, own_o = both(tile(0), 0)
    far_e, far_o = both(tile(4), 1)
    mixed = jnp.where(row_ids < lane_ids, tile(5), tile(5).T)
    turns = cayley([own_e, far_e, own_o, far_o, mixed], (ALTERNATE,) * 5, x_ref, e_ref)
    columns = block_of((LANES, LANES), 1)
    rows = block_of((LANES, LANES), 0)
    chains = []
    for own, far, own_turn, far_turn, base, moved in (
        (own_e, far_e, turns[0], turns[1], 1, 2),
        (own_o, far_o, turns[2], turns[3], 2, 1),
    ):
        near, own_mixed, far_mixed = tile(base), tile(3), tile(5)
        mixed_turn = turns[4]
        far_q = jnp.where(columns == moved, 0.0, far_turn[0])
        far_t = jnp.where(rows == moved, 0.0, far_turn[1])
        mixed_q = jnp.where(columns == moved, mixed_turn[0], 0.0)
        mixed_t = jnp.where(rows == moved, mixed_turn[1], 0.0)
        tail_q = split(jnp.concatenate([far_q, mixed_q], axis=0))
        tail_t = split(jnp.concatenate([far_t, mixed_t], axis=1))
        own_q = split(own_turn[0])
        own_t = split(own_turn[1])
        head = jnp.concatenate([near, own_mixed], axis=1)
        body = jnp.concatenate(
            [
                jnp.concatenate([far, far_mixed], axis=1),
                jnp.concatenate([far_mixed.T, mixed], axis=1),
            ],
            axis=0,
        )
        corner = dot3(own_t, dot3(own, own_q))
        side = dot3(own_t, dot3(head, tail_q))
        rest = dot3(tail_t, dot3(body, tail_q))
        chains.append((regroup((corner, side, rest), swap_middle), own_q, tail_q))
    turns = cayley([t for c in chains for t in (c[0][0], c[0][2])], (OUTSIDE,) * 4, x_ref, e_ref)
    grams = []
    weights = []
    for at, ((near, cross, far), own_q, tail_q) in enumerate(chains):
        (near_q, near_t), (far_q, far_t) = turns[2 * at:2 * at + 2]
        zero = jnp.zeros((BS, LANES), F32)
        top = jnp.concatenate(
            [
                jnp.concatenate([near_q[:64], zero, near_q[96:]], axis=0),
                jnp.concatenate([zero, zero, far_q[BS:64], zero], axis=0),
            ],
            axis=1,
        )
        bottom = jnp.concatenate(
            [
                jnp.concatenate([zero, near_q[64:96], zero, zero], axis=0),
                jnp.concatenate([far_q[:BS], zero, far_q[64:]], axis=0),
            ],
            axis=1,
        )
        spread = jnp.concatenate([dot3(own_q, top), dot3(tail_q, bottom)], axis=0)
        swap = swap_odd if at == 0 else swap_ends
        weights.append(jnp.concatenate(swap(spread[:, :LANES], spread[:, LANES:], 1), axis=1))
        near_q, near_t, far_q, far_t = split(near_q), split(near_t), split(far_q), split(far_t)
        turned = (
            dot3(near_t, dot3(near, near_q)),
            dot3(near_t, dot3(cross, far_q)),
            dot3(far_t, dot3(far, far_q)),
        )
        grams.append(regroup(turned, swap))
    turns = cayley(
        [t for g in grams for t in (g[0], g[2])],
        (ALTERNATE, ADJACENT, ALTERNATE, ALTERNATE), x_ref, e_ref,
    )
    lasts = []
    for at, (near, cross, far) in enumerate(grams):
        (near_q, near_t), (far_q, far_t) = turns[2 * at:2 * at + 2]
        zero = jnp.zeros((BS, LANES), F32)
        if at == 0:
            kept = lax.rem(columns, 2) == 0
            near_q = jnp.where(kept, near_q, 0.0)
            far_q = jnp.where(kept, 0.0, pltpu.roll(far_q, BS, 1))
            near_t = jnp.concatenate([near_t[:BS], zero, near_t[64:96], zero], axis=0)
            far_t = jnp.concatenate([zero, far_t[:BS], zero, far_t[64:96]], axis=0)
        else:
            kept = columns == 1
            near_q = jnp.where(kept, pltpu.roll(near_q, LANES - BS, 1), 0.0)
            far_q = jnp.where(kept, 0.0, far_q)
            near_t = jnp.concatenate([zero, near_t[64:96], zero, zero], axis=0)
            far_t = jnp.concatenate([far_t[:BS], zero, far_t[64:]], axis=0)
        q = split(jnp.concatenate([near_q, far_q], axis=0))
        t = jnp.concatenate([near_t, far_t], axis=1)
        gram = jnp.concatenate(
            [jnp.concatenate([near, cross], axis=1), jnp.concatenate([cross.T, far], axis=1)], axis=0
        )
        lasts.append(dot3(t, dot3(gram, q)))
        weights[at] = dot3(weights[at], q)
    turns = cayley(lasts, (ADJACENT, OUTSIDE), x_ref, e_ref)
    core = lax.rem(lax.axis_index("col"), 2)
    block = block_of((2 * LANES, 2 * LANES), 1)
    block = jnp.where(core == 0, block, 7 - block)
    source = pair_ids(block, (7, 4, 3, 2, 6, 5, 0, 1))
    row = lax.broadcasted_iota(jnp.int32, (2 * LANES, 2 * LANES), 0)
    lane = lax.broadcasted_iota(jnp.int32, (2 * LANES, 2 * LANES), 1)
    place = (row == source * BS + lane % BS).astype(BF16)
    placed = []
    for at, (q, _) in enumerate(turns):
        spot = place[at * LANES:(at + 1) * LANES]
        qh, ql = split(q)
        placed.append((dot1(qh, spot).astype(BF16), dot1(ql, spot).astype(BF16)))
    e_rows = dot3(weights[0], placed[0])
    o_rows = dot3(weights[1], placed[1])
    total = jnp.concatenate(
        [
            e_rows[:2 * LANES],
            o_rows[:2 * LANES],
            e_rows[2 * LANES:] + o_rows[2 * LANES:],
        ],
        axis=0,
    )
    w_high, w_low = split(total)
    w_ref[0] = w_high
    w_ref[1] = w_low

    def strip(step, _):
        here = pl.ds(pl.multiple_of(step * STRIP, STRIP), STRIP)
        high = jnp.concatenate([high_ref[t, here, :] for t in TILE_ORDER], axis=1)
        low = jnp.concatenate([low_ref[t, here, :] for t in TILE_ORDER], axis=1)
        stage[here, :] = dot1(high, w_ref[0]) + (dot1(high, w_ref[1]) + dot1(low, w_ref[0]))
        pltpu.make_async_copy(stage.at[here, :], out_ref.at[here, :], out_sem.at[step]).start()
        return 0

    count = high_ref.shape[1] // STRIP
    lax.fori_loop(0, count, strip, 0, unroll=True)
    for step in range(count):
        here = pl.ds(step * STRIP, STRIP)
        pltpu.make_async_copy(stage.at[here, :], out_ref.at[here, :], out_sem.at[step]).wait()


def shards(left_factor, right_factor, weights, plan):
    vmem = pl.BlockSpec(memory_space=pltpu.VMEM)
    dma = pltpu.SemaphoreType.DMA
    high, low, gram = pl.pallas_call(
        gather_kernel,
        name="gather_and_gram",
        out_shape=(
            jax.ShapeDtypeStruct((5, ROWS, LANES), BF16),
            jax.ShapeDtypeStruct((5, ROWS, LANES), BF16),
            jax.ShapeDtypeStruct((GRAM_ROWS, LANES), F32),
        ),
        in_specs=[pl.BlockSpec(memory_space=pltpu.HBM)] * 4,
        out_specs=(vmem, vmem, vmem),
        scratch_shapes=[
            pltpu.VMEM((ROWS, 64), BF16),
            pltpu.VMEM((1, 64), F32),
            pltpu.VMEM((DEPTH, 2 * LANES), BF16),
            pltpu.SMEM((4, 256), jnp.int32),
            pltpu.VMEM((ROWS, LANES), BF16),
            pltpu.VMEM((ROWS, LANES), BF16),
            pltpu.VMEM((PACKED, LANES), BF16),
            pltpu.VMEM((16, HALF, LANES), BF16),
            pltpu.VMEM((8, 2 * DEPTH, LANES), BF16),
            pltpu.VMEM((8, PACKED, LANES), BF16),
            pltpu.VMEM((8, 2 * DEPTH, LANES), BF16),
            pltpu.VMEM((8, PACKED, LANES), BF16),
            pltpu.VMEM((8, DEPTH, 8 * LANES), BF16),
            pltpu.VMEM((HALF, 8 * LANES), F32),
            pltpu.VMEM((5, HALF, LANES), BF16),
            pltpu.VMEM((5, HALF, LANES), BF16),
            pltpu.VMEM((GRAM_ROWS, LANES), F32),
            pltpu.VMEM((GRAM_ROWS, LANES), F32),
            pltpu.VMEM((GRAM_ROWS, LANES), F32),
            pltpu.VMEM((2, 7, 64, LANES), F32),
        ] + [dma((count,)) for count in (4, 110, 2, 5, 4, 2, 16, 8, 2, 8, 8, 8, 8, 14, 14)],
        compiler_params=pltpu.CompilerParams(
            collective_id=0, has_side_effects=True, vmem_limit_bytes=VMEM_LIMIT
        ),
    )(left_factor, weights, right_factor, plan)
    return pl.pallas_call(
        rounds_kernel,
        name="rounds",
        out_shape=jax.ShapeDtypeStruct((ROWS, 2 * LANES), F32),
        in_specs=[vmem, vmem, vmem],
        out_specs=pl.BlockSpec(memory_space=pltpu.HBM),
        scratch_shapes=[
            pltpu.VMEM((5, 2 * LANES, 2 * LANES), F32),
            pltpu.VMEM((5, 2 * LANES, 2 * LANES), F32),
            pltpu.VMEM((2, 5 * LANES, 2 * LANES), BF16),
            pltpu.VMEM((ROWS, 2 * LANES), F32),
            dma((ROWS // STRIP,)),
        ],
        compiler_params=pltpu.CompilerParams(vmem_limit_bytes=VMEM_LIMIT),
    )(gram, high, low)


def solution(mesh):
    in_specs = (P("row", "col"), P("row", "col"), P("col"), P())
    out_specs = P("row", "col")
    return jax.shard_map(shards, mesh=mesh, in_specs=in_specs, out_specs=out_specs, check_vma=False)
```
